32 devices in a mesh: dp: 2 (over core), wa: 16 (over z, y, x).
Axes of the slice: x: 2, y: 2, z: 4, core: 2. Of those that a mesh axis runs over, the one named last changes fastest.
Arguments:
- slow_in: bfloat16 [32, 8, 16, 16, 1024], P('dp', None, None, None, 'wa'), may hold values from -9 to 9
- fast_in: bfloat16 [32, 32, 16, 16, 128], P('dp', 'wa'), may hold values from -13 to 13
- clip_side: int32 [32], P('dp'), may hold values from 10 to 16, as said below
- fast_reduce: bfloat16 [3, 128, 32], replicated, may hold values from -0.3125 to 0.3125
- fast_spatial: bfloat16 [3, 3, 32, 32], replicated, may hold values from -0.375 to 0.375
- fast_expand: bfloat16 [32, 128], replicated, may hold values from -1 to 1
- lateral_weight: bfloat16 [5, 128, 256], replicated, may hold values from -0.25 to 0.25
- slow_reduce: bfloat16 [3, 1280, 256], replicated, may hold values from -0.09375 to 0.09375
- slow_spatial: bfloat16 [3, 3, 256, 256], replicated, may hold values from -0.125 to 0.125
- slow_expand: bfloat16 [256, 1024], replicated, may hold values from -0.375 to 0.375
- slow_project: bfloat16 [1280, 1024], replicated, may hold values from -0.15625 to 0.15625
- fast_reduce_norm: float32 [2, 32], replicated, may hold values from 0.25 to 1.75
- fast_spatial_norm: float32 [2, 32], replicated, may hold values from 0.25 to 1.75
- fast_expand_norm: float32 [2, 128], replicated, may hold values from 0.25 to 1.75
- lateral_norm: float32 [2, 256], replicated, may hold values from 0.25 to 1.75
- slow_reduce_norm: float32 [2, 256], replicated, may hold values from 0.25 to 1.75
- slow_spatial_norm: float32 [2, 256], replicated, may hold values from 0.25 to 1.75
- slow_expand_norm: float32 [2, 1024], replicated, may hold values from 0.25 to 1.75
- slow_project_norm: float32 [2, 1024], replicated, may hold values from 0.25 to 1.75
- slow_cot: bfloat16 [32, 8, 16, 16, 1024], P('dp', None, None, None, 'wa'), may hold values from -6 to 6
- fast_cot: bfloat16 [32, 32, 16, 16, 128], P('dp', 'wa'), may hold values from -6 to 6
Outputs:
- slow_result: bfloat16 [32, 8, 16, 16, 1024], P('dp', None, None, None, 'wa')
- fast_result: bfloat16 [32, 32, 16, 16, 128], P('dp', 'wa')
- slow_grad: bfloat16 [32, 8, 16, 16, 1024], P('dp', None, None, None, 'wa')
- fast_grad: bfloat16 [32, 32, 16, 16, 128], P('dp', 'wa')
- fast_reduce_grad: float32 [3, 128, 32], replicated
- fast_spatial_grad: float32 [3, 3, 32, 32], replicated
- fast_expand_grad: float32 [32, 128], replicated
- lateral_weight_grad: float32 [5, 128, 256], replicated
- slow_reduce_grad: float32 [3, 1280, 256], replicated
- slow_spatial_grad: float32 [3, 3, 256, 256], replicated
- slow_expand_grad: float32 [256, 1024], replicated
- slow_project_grad: float32 [1280, 1024], replicated
- fast_reduce_norm_grad: float32 [2, 32], replicated
- fast_spatial_norm_grad: float32 [2, 32], replicated
- fast_expand_norm_grad: float32 [2, 128], replicated
- lateral_norm_grad: float32 [2, 256], replicated
- slow_reduce_norm_grad: float32 [2, 256], replicated
- slow_spatial_norm_grad: float32 [2, 256], replicated
- slow_expand_norm_grad: float32 [2, 1024], replicated
- slow_project_norm_grad: float32 [2, 1024], replicated
The draws below stay inside these ranges and needn't reach their ends.
Inputs may be any that keep to these rules, and one draw needn't show every extreme that they name: `clip_side`: each clip's side is one of 10, 14 and 16.
All inputs are finite; a program needn't handle non-finite values.
Results may differ from the reference program's by a relative error of at most 0.018.
Values may be sent and summed in bfloat16 or wider, within the bound.
No kernel may reach another device: no remote copies, remote signals or barrier semaphores. Data moves between devices by JAX's collectives and lax.ppermute only.
A program may use at most 320 MiB of HBM per device.

```python
import jax
import jax.numpy as jnp
from jax import lax

C_S = 1024
C_F = 128
B_S = 256
B_F = 32
C_L = 256
T_S = 8
T_F = 32
ALPHA = 4
TAPS = 5
SIDE = 16
CLIPS_DEV = 16
CLIPS = 32
C_CAT = 1280


def clip_ramp(key_jitter, low_end, high_end):
    ramp = low_end + (high_end - low_end) * jnp.arange(CLIPS, dtype=jnp.float32) / (CLIPS - 1)
    jitter = jax.random.uniform(key_jitter, (CLIPS,), minval=0.8, maxval=1.25)
    return ramp * jitter


def draw_slow_in(key, part):
    key = jax.random.fold_in(key, 5)
    key_values, key_jitter = jax.random.split(key)
    shape = (CLIPS, T_S, SIDE, SIDE, C_S)
    values = jnp.clip(jax.random.normal(key_values, shape), -4.0, 4.0)
    scales = clip_ramp(key_jitter, 0.6, 1.8)
    return (values * scales[:, None, None, None, None]).astype(jnp.bfloat16)


def draw_fast_in(key, part):
    key = jax.random.fold_in(key, 7)
    key_values, key_jitter = jax.random.split(key)
    shape = (CLIPS, T_F, SIDE, SIDE, C_F)
    values = jnp.clip(jax.random.normal(key_values, shape), -4.0, 4.0)
    scales = clip_ramp(key_jitter, 0.6, 1.8)
    frame_ramp = 0.7 + 0.7 * jnp.arange(T_F, dtype=jnp.float32) / (T_F - 1)
    return (values * scales[:, None, None, None, None] * frame_ramp[None, :, None, None, None]).astype(jnp.bfloat16)


def draw_clip_side(key, part):
    key = jax.random.fold_in(key, 3)
    key_lean, key_pick, key_follow, key_top, key_bottom = jax.random.split(key, 5)
    blocks = CLIPS // CLIPS_DEV
    leaning = jax.random.randint(key_lean, (blocks, 1), 0, 3)
    picked = jax.random.randint(key_pick, (blocks, CLIPS_DEV), 0, 3)
    follow = jax.random.randint(key_follow, (blocks, CLIPS_DEV), 0, 4) < 3
    level = jnp.where(follow, leaning, picked).reshape(CLIPS)
    positions = jnp.arange(CLIPS)
    top_clip = jax.random.randint(key_top, (), 0, CLIPS)
    bottom_clip = jax.random.randint(key_bottom, (), 0, CLIPS)
    level = jnp.where((positions == bottom_clip) & (positions != top_clip), 0, level)
    level = jnp.where(positions == top_clip, 2, level)
    sides = jnp.where(level == 2, SIDE, jnp.where(level == 1, 7 * SIDE // 8, 5 * SIDE // 8))
    return sides.astype(jnp.int32)


def levels(key, dims, shards, least, largest):
    loudness, own = 1.0, jax.random.fold_in(key, 6)
    for dim, parts in shards:
        draws = jnp.exp(jax.random.uniform(jax.random.fold_in(own, dim), (parts,), jnp.float32, least / len(shards), largest / len(shards)))
        loudness = loudness * jnp.repeat(draws, dims[dim] // parts).reshape([-1 if axis == dim else 1 for axis in range(len(dims))])
    return loudness


def bell_draw(stream_key, shape, width, most, cuts=(), kind=jnp.bfloat16):
    factor_of = levels(stream_key, shape, cuts, -0.22, 0.18) if cuts else 1.0
    entries = jax.random.normal(stream_key, shape, jnp.float32) * width * factor_of
    return jnp.minimum(jnp.maximum(entries, -most), most).astype(kind)


def setup_inputs(seed: int = 0) -> dict:
    key_of = jax.random.split(jax.random.key(seed), 22)
    return {
        "slow_in": draw_slow_in(jax.random.fold_in(key_of[21], 71), 0),
        "fast_in": draw_fast_in(jax.random.fold_in(key_of[21], 71), 0),
        "clip_side": draw_clip_side(jax.random.fold_in(key_of[21], 71), 0),
        "fast_reduce": bell_draw(key_of[3], (3, C_F, B_F), (3 * C_F) ** -0.5, 0.3125),
        "fast_spatial": bell_draw(key_of[4], (3, 3, B_F, B_F), (9 * B_F) ** -0.5, 0.375),
        "fast_expand": bell_draw(key_of[5], (B_F, C_F), B_F ** -0.5, 1.0),
        "lateral_weight": bell_draw(key_of[6], (TAPS, C_F, C_L), (TAPS * C_F) ** -0.5, 0.25),
        "slow_reduce": bell_draw(key_of[7], (3, C_CAT, B_S), (3 * C_CAT) ** -0.5, 0.09375),
        "slow_spatial": bell_draw(key_of[8], (3, 3, B_S, B_S), (9 * B_S) ** -0.5, 0.125),
        "slow_expand": bell_draw(key_of[9], (B_S, C_S), B_S ** -0.5, 0.375),
        "slow_project": bell_draw(key_of[10], (C_CAT, C_S), C_CAT ** -0.5, 0.15625),
        "fast_reduce_norm": jnp.clip(1.0 + 0.15 * jax.random.normal(key_of[11], (2, B_F), jnp.float32), 0.25, 1.75),
        "fast_spatial_norm": jnp.clip(1.0 + 0.15 * jax.random.normal(key_of[12], (2, B_F), jnp.float32), 0.25, 1.75),
        "fast_expand_norm": jnp.clip(1.0 + 0.15 * jax.random.normal(key_of[13], (2, C_F), jnp.float32), 0.25, 1.75),
        "lateral_norm": jnp.clip(1.0 + 0.15 * jax.random.normal(key_of[14], (2, C_L), jnp.float32), 0.25, 1.75),
        "slow_reduce_norm": jnp.clip(1.0 + 0.15 * jax.random.normal(key_of[15], (2, B_S), jnp.float32), 0.25, 1.75),
        "slow_spatial_norm": jnp.clip(1.0 + 0.15 * jax.random.normal(key_of[16], (2, B_S), jnp.float32), 0.25, 1.75),
        "slow_expand_norm": jnp.clip(1.0 + 0.15 * jax.random.normal(key_of[17], (2, C_S), jnp.float32), 0.25, 1.75),
        "slow_project_norm": jnp.clip(1.0 + 0.15 * jax.random.normal(key_of[18], (2, C_S), jnp.float32), 0.25, 1.75),
        "slow_cot": bell_draw(key_of[19], (CLIPS, T_S, SIDE, SIDE, C_S), 1.0, 6.0, ((0, 2), (4, 16))),
        "fast_cot": bell_draw(key_of[20], (CLIPS, T_F, SIDE, SIDE, C_F), 1.0, 6.0, ((0, 2), (1, 16))),
    }


HIGH = lax.Precision.HIGHEST
EPSILON = 1e-05

@jax.custom_vjp
def low(v):
    return lax.optimization_barrier(v.astype(jnp.bfloat16)).astype(jnp.float32)

@jax.custom_vjp
def low_back(v):
    return v

def low_keep(v):
    return (low(v), None)

def low_pass(kept, grad):
    return (grad,)

def back_keep(v):
    return (v, None)

def back_low(kept, grad):
    return (low(grad),)
low.defvjp(low_keep, low_pass)
low_back.defvjp(back_keep, back_low)

def time_apply(values, weight, padding, stride, length):
    padded = jnp.pad(values, ((0, 0), (padding, padding), (0, 0), (0, 0), (0, 0)))
    summed = None
    for offset in range(weight.shape[0]):
        window = lax.slice_in_dim(padded, offset, offset + stride * (length - 1) + 1, stride, 1)
        tap_term = jnp.einsum('nthwi,io->nthwo', window, weight[offset], precision=HIGH)
        summed = tap_term if summed is None else summed + tap_term
    return summed

def plane_apply(values, weight):
    grid_rows, grid_cols = (values.shape[2], values.shape[3])
    padded = jnp.pad(values, ((0, 0), (0, 0), (1, 1), (1, 1), (0, 0)))
    summed = None
    for row_tap in range(3):
        for col_tap in range(3):
            window = padded[:, :, row_tap:row_tap + grid_rows, col_tap:col_tap + grid_cols]
            tap_term = jnp.einsum('nthwi,io->nthwo', window, weight[row_tap, col_tap], precision=HIGH)
            summed = tap_term if summed is None else summed + tap_term
    return summed

def batch_norm(values, norm_params, valid, count_all):
    first_sum = lax.optimization_barrier(jnp.sum(values * valid, axis=(0, 1, 2, 3)))
    second_sum = lax.optimization_barrier(jnp.sum(values * values * valid, axis=(0, 1, 2, 3)))
    mean_value = first_sum / count_all
    variance = second_sum / count_all - mean_value * mean_value
    return norm_params[0] * ((values - mean_value) * lax.rsqrt(variance + EPSILON)) + norm_params[1]

def reference(slow_in, fast_in, clip_side, fast_reduce, fast_spatial, fast_expand, lateral_weight, slow_reduce, slow_spatial, slow_expand, slow_project, fast_reduce_norm, fast_spatial_norm, fast_expand_norm, lateral_norm, slow_reduce_norm, slow_spatial_norm, slow_expand_norm, slow_project_norm, slow_cot, fast_cot):
    row_ids = lax.broadcasted_iota(jnp.int32, (SIDE, SIDE), 0)
    col_ids = lax.broadcasted_iota(jnp.int32, (SIDE, SIDE), 1)
    bounds = clip_side.astype(jnp.int32)[:, None, None]
    valid = ((row_ids[None] < bounds) & (col_ids[None] < bounds)).astype(jnp.float32)[:, None, :, :, None]
    valid_area = jnp.sum(clip_side * clip_side).astype(jnp.float32)
    fast_count = valid_area * T_F
    slow_count = valid_area * T_S

    def forward(slow_data, fast_data, reduce_weight, spatial_weight, expand_weight, lateral_data, narrow_weight, middle_weight, widen_weight, project_weight, reduce_norm, spatial_norm, expand_norm, lateral_params, narrow_norm, middle_norm, widen_norm, project_norm):
        reduce_pre = low_back(time_apply(fast_data, reduce_weight, 1, 1, T_F))
        reduce_act = low(valid * jax.nn.silu(batch_norm(reduce_pre, reduce_norm, valid, fast_count)))
        spatial_pre = low_back(plane_apply(reduce_act, spatial_weight))
        spatial_act = low(valid * jax.nn.silu(batch_norm(spatial_pre, spatial_norm, valid, fast_count)))
        expand_pre = low_back(jnp.einsum('nthwi,io->nthwo', spatial_act, expand_weight, precision=HIGH))
        fast_result = low(valid * jax.nn.silu(fast_data + batch_norm(expand_pre, expand_norm, valid, fast_count)))
        lateral_pre = low_back(time_apply(low_back(fast_result), lateral_data, TAPS // 2, ALPHA, T_S))
        lateral_act = low(valid * jax.nn.silu(batch_norm(lateral_pre, lateral_params, valid, slow_count)))
        joined = jnp.concatenate([slow_data, lateral_act], axis=4)
        narrow_pre = low_back(time_apply(joined, narrow_weight, 1, 1, T_S))
        narrow_act = low(valid * jax.nn.silu(batch_norm(narrow_pre, narrow_norm, valid, slow_count)))
        middle_pre = low_back(plane_apply(narrow_act, middle_weight))
        middle_act = low(valid * jax.nn.silu(batch_norm(middle_pre, middle_norm, valid, slow_count)))
        widen_pre = low_back(jnp.einsum('nthwi,io->nthwo', middle_act, widen_weight, precision=HIGH))
        project_pre = low_back(jnp.einsum('nthwi,io->nthwo', joined, project_weight, precision=HIGH))
        slow_sum = batch_norm(widen_pre, widen_norm, valid, slow_count) + batch_norm(project_pre, project_norm, valid, slow_count)
        return (valid * jax.nn.silu(slow_sum), fast_result)
    floats = tuple((entry.astype(jnp.float32) for entry in (slow_in, fast_in, fast_reduce, fast_spatial, fast_expand, lateral_weight, slow_reduce, slow_spatial, slow_expand, slow_project, fast_reduce_norm, fast_spatial_norm, fast_expand_norm, lateral_norm, slow_reduce_norm, slow_spatial_norm, slow_expand_norm, slow_project_norm)))
    results, pullback = jax.vjp(forward, *floats)
    gradients = pullback((slow_cot.astype(jnp.float32), fast_cot.astype(jnp.float32)))
    return (results[0].astype(jnp.bfloat16), results[1].astype(jnp.bfloat16), gradients[0].astype(jnp.bfloat16), gradients[1].astype(jnp.bfloat16), gradients[2], gradients[3], gradients[4], gradients[5], gradients[6], gradients[7], gradients[8], gradients[9], gradients[10], gradients[11], gradients[12], gradients[13], gradients[14], gradients[15], gradients[16], gradients[17])
```

```python
import functools

import jax
import jax.numpy as jnp
from jax import lax
from jax.experimental import pallas as pl
from jax.experimental.pallas import tpu as pltpu
from jax.sharding import PartitionSpec as P

EPSILON = 1e-05
BF = jnp.bfloat16
F32 = jnp.float32
LANES = 128
GROUPS = 4
VMEM_BYTES = 52 * 1024 * 1024


def whole(array):
    rank = len(array.shape)
    return pl.BlockSpec(array.shape, lambda *_: (0,) * rank)


def scalars():
    return pl.BlockSpec(memory_space=pltpu.SMEM)


def launch(body, name, grid, inputs, outputs, scratch=(), flops=0, after=(), carry=()):
    used, given = len(inputs), len(outputs)
    held = pl.BlockSpec(memory_space=pl.ANY)
    inputs = inputs + [(array, held) for array in (*after, *carry)]
    outputs = outputs + [(array.shape, array.dtype, held) for array in carry]
    first = used + len(after)
    aliases = {first + k: given + k for k in range(len(carry))}

    def kernel(*refs):
        outs = refs[len(inputs) :]
        body(*refs[:used], *outs[:given], *outs[len(outputs) :])

    traffic = sum(a.size * a.dtype.itemsize for a, _ in inputs)
    for shape, dtype, _ in outputs:
        count = 1
        for entry in shape:
            count *= entry
        traffic += count * jnp.dtype(dtype).itemsize
    return pl.pallas_call(
        kernel,
        name=name,
        grid=grid,
        in_specs=[spec for _, spec in inputs],
        out_specs=[spec for _, _, spec in outputs],
        out_shape=[jax.ShapeDtypeStruct(shape, dtype) for shape, dtype, _ in outputs],
        scratch_shapes=list(scratch),
        input_output_aliases=aliases,
        compiler_params=pltpu.CompilerParams(vmem_limit_bytes=VMEM_BYTES),
        cost_estimate=pl.CostEstimate(flops=flops, bytes_accessed=traffic, transcendentals=0),
    )(*[array for array, _ in inputs])


def dot(a, b):
    return lax.dot_general(a, b, (((1,), (0,)), ((), ())), preferred_element_type=F32)


def dot_nt(a, b):
    return lax.dot_general(a, b, (((1,), (1,)), ((), ())), preferred_element_type=F32)


def dot_tn(a, b):
    return lax.dot_general(a, b, (((0,), (0,)), ((), ())), preferred_element_type=F32)


def logistic(u):
    return 0.5 * jnp.tanh(0.5 * u) + 0.5


def silu(u):
    return u * logistic(u)


def silu_slope(u):
    g = logistic(u)
    return g + u * g * (1.0 - g)


def cell_ids(rows):
    ids = lax.broadcasted_iota(jnp.int32, (rows, 1), 0)
    return (ids >> 4) & 15, ids & 15


def clip_mask(side, rows):
    h, w = cell_ids(rows)
    return jnp.where((h < side) & (w < side), 1.0, 0.0).astype(F32)


def packed_mask(side_row, rows):
    ids = lax.broadcasted_iota(jnp.int32, (rows, LANES), 0)
    h, w = (ids >> 4) & 15, ids & 15
    return jnp.where((h < side_row) & (w < side_row), 1.0, 0.0).astype(F32)


def fold(row):
    width = LANES // GROUPS
    out = row
    for step in range(1, GROUPS):
        out = out + pltpu.roll(row, step * width, 1)
    return out


def norm_terms(gathered, params, count, folded=False):
    total = jnp.sum(gathered, axis=0)
    if folded:
        total = fold(total)
    mean = total[0:1] / count
    variance = total[1:2] / count - mean * mean
    inv = lax.rsqrt(variance + EPSILON)
    scale = params[0:1] * inv
    return mean, inv, scale, params[1:2] - mean * scale


def back_terms(gathered, params, count, mean, inv, folded=False):
    total = jnp.sum(gathered, axis=0)
    if folded:
        total = fold(total)
    a = params[0:1] * inv
    b = -a * inv * inv * total[1:2] / count
    return a, b, -a * total[0:1] / count - b * mean


def col_sum(v):
    return jnp.sum(v, axis=0, keepdims=True)


def add_stats(acc, first, rows, values):
    @pl.when(first)
    def _():
        acc[...] = jnp.zeros_like(acc)

    for row, value in zip(rows, values):
        acc[row : row + 1, :] += value


def send_stats(last, acc, out):
    @pl.when(last)
    def _():
        out[...] = jnp.broadcast_to(acc[...][None], out.shape)


def put_columns(wide, out):
    rows, width = wide.shape[0], out.shape[1]
    for block in range(wide.shape[1] // width):
        out[block * rows : (block + 1) * rows, :] = wide[:, block * width : (block + 1) * width].astype(BF)


def plane_windows(values, cells):
    rows = values.shape[0]
    w = lax.broadcasted_iota(jnp.int32, (rows, 1), 0) & (cells - 1)
    left = jnp.where(w == 0, 0.0, pltpu.roll(values, 1, 0))
    right = jnp.where(w == cells - 1, 0.0, pltpu.roll(values, rows - 1, 0))
    return jnp.concatenate([left.astype(BF), values.astype(BF), right.astype(BF)], axis=1)


def fill_windows(scratch, windows, cells):
    rows = windows.shape[0]
    zeros = jnp.zeros((cells, windows.shape[1]), BF)
    scratch[0:cells, :] = zeros
    scratch[cells : cells + rows, :] = windows
    scratch[cells + rows : 2 * cells + rows, :] = zeros


def plane_dot(scratch, weight, rows, cells):
    out = dot(scratch[0:rows, :], weight[0])
    for tap in (1, 2):
        out = out + dot(scratch[tap * cells : tap * cells + rows, :], weight[tap])
    return out


def fast_first(x, w, y, to_next, to_prev):
    def over(frame, tap):
        out = dot(x[0, frame], w[tap, 0])
        for g in range(1, GROUPS):
            out = out + dot(x[g, frame], w[tap, g])
        return out

    y[0, 0] = over(0, 1) + over(1, 2)
    y[0, 1] = over(0, 0) + over(1, 1)
    to_next[0] = over(1, 0).astype(BF)
    to_prev[0] = over(0, 2).astype(BF)


def fast_join(y, from_prev, from_next, sides, pre, stats, acc):
    i = pl.program_id(0)
    mask = packed_mask(sides[0], 256)
    first = y[0, 0] + from_prev[0].astype(F32)
    second = y[0, 1] + from_next[0].astype(F32)
    pre[0, 0] = first
    pre[0, 1] = second
    m1, m2 = first * mask, second * mask
    add_stats(acc, i == 0, (0, 1), (col_sum(m1 + m2), col_sum(m1 * first + m2 * second)))
    send_stats(i == pl.num_programs(0) - 1, acc, stats)


def fast_plane(count, pre, g1, params, sides, w, act, out, stats, acc, win):
    i = pl.program_id(0)
    _, _, scale, shift = norm_terms(g1[...], params[...], count[0, 0], True)
    mask = packed_mask(sides[0], 256)
    sums, squares = [], []
    for frame in range(2):
        a = mask * silu(pre[0, frame] * scale + shift)
        act[0, frame] = a.astype(BF)
        fill_windows(win, plane_windows(a, 16), 16)
        v = plane_dot(win, w, 256, 16)
        out[0, frame] = v
        mv = mask * v
        sums.append(mv)
        squares.append(mv * v)
    add_stats(acc, i == 0, (0, 1), (col_sum(sums[0] + sums[1]), col_sum(squares[0] + squares[1])))
    send_stats(i == pl.num_programs(0) - 1, acc, stats)


def fast_widen(count, pre, g2, params, sides, w, act, stats, acc):
    i = pl.program_id(0)
    _, _, scale, shift = norm_terms(g2[...], params[...], count[0, 0], True)
    mask = packed_mask(sides[0], 256)
    total, square = None, None
    for frame in range(2):
        a = (mask * silu(pre[0, frame] * scale + shift)).astype(BF)
        act[0, frame] = a
        for g in range(GROUPS):
            v = dot(a, w[g])
            total = v if total is None else total + v
            square = v * v if square is None else square + v * v
    add_stats(acc, i == 0, (0, 1), (col_sum(total), col_sum(square)))
    send_stats(i == pl.num_programs(0) - 1, acc, stats)


def fast_out(count, sides, x, act, g3, params, w, result):
    i = pl.program_id(0)
    _, _, scale, shift = norm_terms(g3[...], params[...], count[0, 0])
    for g in range(GROUPS):
        mask = clip_mask(sides[i * GROUPS + g], 256)
        for frame in range(2):
            u = x[g, frame].astype(F32) + dot(act[0, frame], w[g]) * scale + shift
            result[g, frame] = (mask * silu(u)).astype(BF)


def fast_back_sum(count, sides, cot, back, x, act, g3, params, w, grad, stats, acc):
    i = pl.program_id(0)
    mean, _, scale, shift = norm_terms(g3[...], params[...], count[0, 0])
    total, cross = None, None
    for g in range(GROUPS):
        mask = clip_mask(sides[i * GROUPS + g], 256)
        for frame in range(2):
            v = dot(act[0, frame], w[g])
            u = x[g, frame].astype(F32) + v * scale + shift
            e = (cot[g, frame].astype(F32) + back[g, frame].astype(F32)) * mask * silu_slope(u)
            grad[g, frame] = e
            total = e if total is None else total + e
            c = e * (v - mean)
            cross = c if cross is None else cross + c
    add_stats(acc, i == 0, (0, 1), (col_sum(total), col_sum(cross)))
    send_stats(i == pl.num_programs(0) - 1, acc, stats)


def fast_back_widen(
    count, sides, grad, act, g3, h3, params3, w, pre, g2, params2, lane_sides, out, w_grad, stats, acc
):
    i = pl.program_id(0)
    c = count[0, 0]
    mean3, inv3, _, _ = norm_terms(g3[...], params3[...], c)
    a, b, d = back_terms(h3[...], params3[...], c, mean3, inv3)
    mean2, _, scale2, shift2 = norm_terms(g2[...], params2[...], c, True)
    lane_mask = packed_mask(lane_sides[0], 256)

    @pl.when(i == 0)
    def _():
        w_grad[...] = jnp.zeros_like(w_grad)

    total, cross = None, None
    for frame in range(2):
        s = act[0, frame]
        back = None
        for g in range(GROUPS):
            mask = clip_mask(sides[i * GROUPS + g], 256)
            v = dot(s, w[g])
            low = (mask * (grad[g, frame] * a + v * b + d)).astype(BF)
            part = dot_nt(low, w[g])
            back = part if back is None else back + part
            w_grad[g] += dot_tn(s, low)
        p = pre[0, frame]
        e = back * lane_mask * silu_slope(p * scale2 + shift2)
        out[0, frame] = e
        total = e if total is None else total + e
        x = e * (p - mean2)
        cross = x if cross is None else cross + x
    add_stats(acc, i == 0, (0, 1), (col_sum(total), col_sum(cross)))
    send_stats(i == pl.num_programs(0) - 1, acc, stats)


def fast_back_plane(
    count, e2, pre2, g2, h2, params2, act1, pre1, g1, params1, lane_sides, w, out, w_grad, stats, acc, win
):
    i = pl.program_id(0)
    c = count[0, 0]
    mean2, inv2, _, _ = norm_terms(g2[...], params2[...], c, True)
    a, b, d = back_terms(h2[...], params2[...], c, mean2, inv2, True)
    mean1, _, scale1, shift1 = norm_terms(g1[...], params1[...], c, True)
    mask = packed_mask(lane_sides[0], 256)

    @pl.when(i == 0)
    def _():
        w_grad[...] = jnp.zeros_like(w_grad)

    total, cross = None, None
    for frame in range(2):
        low = mask * (e2[0, frame] * a + pre2[0, frame] * b + d)
        fill_windows(win, plane_windows(low, 16), 16)
        p = pre1[0, frame]
        e = plane_dot(win, w, 256, 16) * mask * silu_slope(p * scale1 + shift1)
        out[0, frame] = e
        total = e if total is None else total + e
        x = e * (p - mean1)
        cross = x if cross is None else cross + x
        low = low.astype(BF)
        fill_windows(win, plane_windows(act1[0, frame].astype(F32), 16), 16)
        for tap in range(3):
            w_grad[tap] += dot_tn(win[16 * tap : 16 * tap + 256, :], low)
    add_stats(acc, i == 0, (0, 1), (col_sum(total), col_sum(cross)))
    send_stats(i == pl.num_programs(0) - 1, acc, stats)


def fast_back_first(count, e1, pre1, g1, h1, params1, lane_sides, low):
    c = count[0, 0]
    mean1, inv1, _, _ = norm_terms(g1[...], params1[...], c, True)
    a, b, d = back_terms(h1[...], params1[...], c, mean1, inv1, True)
    mask = packed_mask(lane_sides[0], 256)
    for frame in range(2):
        low[frame, 0] = (mask * (e1[0, frame] * a + pre1[0, frame] * b + d)).astype(BF)


def fast_back_out(grad, low, from_prev, from_next, x, w, out, w_grad):
    i = pl.program_id(0)

    @pl.when(i == 0)
    def _():
        w_grad[...] = jnp.zeros_like(w_grad)

    around = (from_prev[0], low[0, 0], low[1, 0], from_next[0])
    for frame in range(2):
        before, here, after = around[frame], around[frame + 1], around[frame + 2]
        joined = jnp.concatenate([after, here, before], axis=1)
        for g in range(GROUPS):
            out[g, frame] = (grad[g, frame] + dot_nt(joined, w[g])).astype(BF)
            w_grad[g] += dot_tn(x[g, frame], joined)


def pack_kernel(x, out):
    half = x.shape[1] // 2
    for clip in range(x.shape[0]):
        out[clip] = jnp.concatenate([x[clip, :half], x[clip, half:]], axis=1)


def unpack_kernel(x, out):
    half = x.shape[1]
    width = x.shape[2] // 2
    for clip in range(x.shape[0]):
        out[clip, :half] = x[clip, :, :width]
        out[clip, half:] = x[clip, :, width:]


def gather_halves(x):
    devices, _, lanes = x.shape
    width = lanes // 2
    low, high = [], []
    for j in range(devices):
        part = x[j]
        low.append(part[:, :width])
        high.append(part[:, width:])
    return jnp.concatenate(low, axis=1), jnp.concatenate(high, axis=1)


def scatter_halves(low, high, out):
    devices, _, lanes = out.shape
    width = lanes // 2
    for j in range(devices):
        out[j] = jnp.concatenate(
            [low[:, j * width : (j + 1) * width], high[:, j * width : (j + 1) * width]], axis=1
        )


def slow_enter(x, w_time, w_project, own, narrow, project):
    i = pl.program_id(0)
    frames = narrow.shape[0] - 2

    @pl.when(i == 0)
    def _():
        narrow[...] = jnp.zeros_like(narrow)

    for half, frame in enumerate(gather_halves(x)):
        own[half, 0] = frame
        depth = frame.shape[1]
        project[half, 0] = dot(frame, w_project[:depth]).astype(BF)
        t = i + half * (frames // 2)
        for tap in range(3):
            narrow[t + 2 - tap] += dot(frame, w_time[tap, :depth])


def lateral_enter(side, fast, w, pre, stats, acc):
    frames = pre.shape[0]
    width = w.shape[1]
    mask = clip_mask(side[0], 256)
    for t in range(frames):
        taps = [k for k in range(5) if 0 <= 4 * t - 2 + k < 4 * frames]
        joined = jnp.concatenate([fast[4 * t - 2 + k] for k in taps], axis=1)
        v = dot(joined, w[taps[0] : taps[-1] + 1].reshape(len(taps) * width, w.shape[2]))
        pre[t] = v
        mv = mask * v
        add_stats(acc, t == 0, (0, 1), (col_sum(mv), col_sum(mv * v)))
    send_stats(True, acc, stats)


def narrow_enter(count, side, lateral, gl, params, base, w, act, pre, stats, acc):
    frames = pre.shape[0]
    _, _, scale, shift = norm_terms(gl[...], params[...], count[0, 0])
    mask = clip_mask(side[0], 256)
    for t in range(frames):
        act[t] = (mask * silu(lateral[t] * scale + shift)).astype(BF)
    width = act.shape[2]
    for t in range(frames):
        taps = [k for k in range(3) if 0 <= t - 1 + k < frames]
        joined = jnp.concatenate([act[t - 1 + k] for k in taps], axis=1)
        v = base[t + 1] + dot(joined, w[taps[0] * width : (taps[-1] + 1) * width, :])
        pre[t] = v
        mv = mask * v
        add_stats(acc, t == 0, (0, 1), (col_sum(mv), col_sum(mv * v)))
    send_stats(True, acc, stats)


def middle_enter(count, side, pre, gn, params, w, act, out, stats, acc, win):
    i = pl.program_id(0)
    _, _, scale, shift = norm_terms(gn[...], params[...], count[0, 0])
    mask = clip_mask(side[0], 256)
    a = mask * silu(pre[0] * scale + shift)
    act[0] = a.astype(BF)
    fill_windows(win, plane_windows(a, 16), 16)
    v = plane_dot(win, w, 256, 16)
    out[0] = v
    mv = mask * v
    add_stats(acc, i == 0, (0, 1), (col_sum(mv), col_sum(mv * v)))
    send_stats(i == pl.num_programs(0) - 1, acc, stats)


def wide_enter(count, side, pre, gm, params, base, lateral, w, w_project, act, project, acc):
    i = pl.program_id(0)
    _, _, scale, shift = norm_terms(gm[...], params[...], count[0, 0])
    mask = clip_mask(side[0], 256)
    a = (mask * silu(pre[0] * scale + shift)).astype(BF)
    act[0] = a
    v = dot(a, w[...])
    p = base[0].astype(F32) + dot(lateral[0], w_project[...])
    project[0] = p.astype(BF)
    mp = mask * p
    add_stats(
        acc, i == 0, (0, 1, 2, 3), (col_sum(v), col_sum(v * v), col_sum(mp), col_sum(mp * p))
    )


def wide_out(count, side, act, project, cot, g, params_w, params_p, w, result, grad, acc):
    i = pl.program_id(0)
    c = count[0, 0]
    gathered = g[...]
    mean_w, _, scale_w, shift_w = norm_terms(gathered[:, 0:2], params_w[...], c)
    mean_p, _, scale_p, shift_p = norm_terms(gathered[:, 2:4], params_p[...], c)
    mask = clip_mask(side[0], 256)
    shift = shift_w + shift_p
    halves = []
    sums = [None, None, None]
    for half, cot_half in enumerate(gather_halves(cot)):
        v = dot(act[half, 0], w[...])
        p = project[half, 0].astype(F32)
        u = v * scale_w + p * scale_p + shift
        gate = logistic(u)
        s = u * gate
        halves.append((mask * s).astype(BF))
        e = mask * cot_half.astype(F32) * (gate + s * (1.0 - gate))
        grad[half, 0] = e
        for k, value in enumerate((e, e * (v - mean_w), e * (p - mean_p))):
            value = col_sum(value)
            sums[k] = value if sums[k] is None else sums[k] + value
    scatter_halves(halves[0], halves[1], result)
    add_stats(acc, i == 0, (0, 1, 2), sums)


def middle_back(
    count, side, grad, act, g, h, params_w, w, pre, gm, params_m, out, w_grad, stats, acc, w_acc
):
    i = pl.program_id(0)
    c = count[0, 0]
    mean_w, inv_w, _, _ = norm_terms(g[...][:, 0:2], params_w[...], c)
    a, b, d = back_terms(h[...][:, 0:2], params_w[...], c, mean_w, inv_w)
    mean_m, _, scale_m, shift_m = norm_terms(gm[...], params_m[...], c)
    mask = clip_mask(side[0], 256)
    s = act[0]
    v = dot(s, w[...])
    low = (mask * (grad[0] * a + v * b + d)).astype(BF)
    p = pre[0]
    e = dot_nt(low, w[...]) * mask * silu_slope(p * scale_m + shift_m)
    out[0] = e
    add_stats(acc, i == 0, (0, 1), (col_sum(e), col_sum(e * (p - mean_m))))
    send_stats(i == pl.num_programs(0) - 1, acc, stats)

    @pl.when(i == 0)
    def _():
        w_acc[...] = jnp.zeros_like(w_acc)

    w_acc[...] += dot_tn(s, low)

    @pl.when(i == pl.num_programs(0) - 1)
    def _():
        put_columns(w_acc, w_grad)


def project_back(
    count, side, grad, project, g, h, params_p, own, lateral, w, joined, w_grad, w_acc
):
    i = pl.program_id(0)
    c = count[0, 0]
    mean_p, inv_p, _, _ = norm_terms(g[...][:, 2:4], params_p[...], c)
    rows = h[...]
    total = jnp.concatenate([rows[:, 0:1], rows[:, 2:3]], axis=1)
    a, b, d = back_terms(total, params_p[...], c, mean_p, inv_p)
    mask = clip_mask(side[0], 256)
    low = (mask * (grad[0] * a + project[0].astype(F32) * b + d)).astype(BF)
    joined[0] = dot_nt(low, w[...]).astype(BF)

    @pl.when(i == 0)
    def _():
        w_acc[...] = jnp.zeros_like(w_acc)

    width = own.shape[2]
    w_acc[0:width, :] += dot_tn(own[0], low)
    w_acc[width:, :] += dot_tn(lateral[0], low)

    @pl.when(i == pl.num_programs(0) - 1)
    def _():
        put_columns(w_acc, w_grad)


def narrow_back(
    count, side, grad, pre_m, gm, hm, params_m, w, pre_n, gn, params_n, low_out, out, stats, acc, win
):
    i = pl.program_id(0)
    c = count[0, 0]
    mean_m, inv_m, _, _ = norm_terms(gm[...], params_m[...], c)
    a, b, d = back_terms(hm[...], params_m[...], c, mean_m, inv_m)
    mean_n, _, scale_n, shift_n = norm_terms(gn[...], params_n[...], c)
    mask = clip_mask(side[0], 256)
    low = mask * (grad[0] * a + pre_m[0] * b + d)
    low_out[0] = low.astype(BF)
    fill_windows(win, plane_windows(low, 16), 16)
    p = pre_n[0]
    e = plane_dot(win, w, 256, 16) * mask * silu_slope(p * scale_n + shift_n)
    out[0] = e
    add_stats(acc, i == 0, (0, 1), (col_sum(e), col_sum(e * (p - mean_n))))
    send_stats(i == pl.num_programs(0) - 1, acc, stats)


def plane_weight(act, low, w_grad, w_acc, win):
    i = pl.program_id(0)

    @pl.when(i == 0)
    def _():
        w_acc[...] = jnp.zeros_like(w_acc)

    fill_windows(win, plane_windows(act[0].astype(F32), 16), 16)
    for tap in range(3):
        w_acc[tap] += dot_tn(win[16 * tap : 16 * tap + 256, :], low[0])

    @pl.when(i == pl.num_programs(0) - 1)
    def _():
        w_grad[...] = w_acc[...].astype(BF)


def join_back(
    count, side, grad, pre_n, gn, hn, params_n, w, joined, pre_l, gl, params_l, low, slow, out, stats, acc
):
    i = pl.program_id(0)
    steps = pl.num_programs(0)
    c = count[0, 0]
    frames = low.shape[0] - 2
    width = low.shape[2]
    mask = clip_mask(side[0], 256)

    @pl.when(i == 0)
    def _():
        mean_n, inv_n, _, _ = norm_terms(gn[...], params_n[...], c)
        a, b, d = back_terms(hn[...], params_n[...], c, mean_n, inv_n)
        low[0] = jnp.zeros((256, width), BF)
        low[frames + 1] = jnp.zeros((256, width), BF)
        for t in range(frames):
            low[t + 1] = (mask * (grad[t] * a + pre_n[t] * b + d)).astype(BF)

    mean_l, _, scale_l, shift_l = norm_terms(gl[...], params_l[...], c)
    halves = []
    sums = [None, None]
    for half in range(2):
        t = i + half * (frames // 2)
        j = joined[half, 0].astype(F32)
        for tap in range(3):
            j = j + dot_nt(low[t + 2 - tap], w[tap])
        slow_width = j.shape[1] - out.shape[3]
        halves.append(j[:, :slow_width].astype(BF))
        p = pre_l[half, 0]
        e = j[:, slow_width:] * mask * silu_slope(p * scale_l + shift_l)
        out[half, 0] = e
        for k, value in enumerate((e, e * (p - mean_l))):
            value = col_sum(value)
            sums[k] = value if sums[k] is None else sums[k] + value
    scatter_halves(halves[0], halves[1], slow)
    add_stats(acc, i == 0, (0, 1), sums)
    send_stats(i == steps - 1, acc, stats)


def lateral_back(count, side, grad, pre_l, gl, hl, params_l, w, low, out):
    c = count[0, 0]
    frames = grad.shape[0]
    mean_l, inv_l, _, _ = norm_terms(gl[...], params_l[...], c)
    a, b, d = back_terms(hl[...], params_l[...], c, mean_l, inv_l)
    mask = clip_mask(side[0], 256)
    for t in range(frames):
        low[t] = (mask * (grad[t] * a + pre_l[t] * b + d)).astype(BF)
    for t in range(frames):
        here = low[t]
        out[4 * t] = dot_nt(here, w[2]).astype(BF)
        out[4 * t + 1] = dot_nt(here, w[3]).astype(BF)
        third = dot_nt(here, w[4])
        if t + 1 < frames:
            after = low[t + 1]
            third = third + dot_nt(after, w[0])
            out[4 * t + 3] = dot_nt(after, w[1]).astype(BF)
        else:
            out[4 * t + 3] = jnp.zeros(out.shape[1:], BF)
        out[4 * t + 2] = third.astype(BF)


def lateral_weight_back(fast, low, w_grad, w_acc):
    frames = low.shape[0]
    width = fast.shape[2]
    w_acc[...] = jnp.zeros_like(w_acc)
    for t in range(frames):
        taps = [k for k in range(5) if 0 <= 4 * t - 2 + k < 4 * frames]
        joined = jnp.concatenate([fast[4 * t - 2 + k] for k in taps], axis=1)
        w_acc[taps[0] * width : (taps[-1] + 1) * width, :] += dot_tn(joined, low[t])
    w_grad[...] = w_acc[...].astype(BF)


def weight_merge(core, *refs):
    out = refs[-1]
    count = (len(refs) - 1) // 2
    rows = out.shape[0]
    for half in range(2):

        @pl.when(core[0] == half)
        def _(half=half):
            begin = 0
            for mine, other in zip(refs[:count], refs[count : 2 * count]):
                end = begin + mine.shape[0]
                low, high = max(begin, half * rows), min(end, (half + 1) * rows)
                if low < high:
                    part = slice(low - begin, high - begin)
                    total = mine[part, :].astype(F32) + other[part, :].astype(F32)
                    out[low - half * rows : high - half * rows, :] = total.astype(BF)
                begin = end


def weight_split(place, *refs):
    project, expand, spatial, time, lateral, full = refs[-6:]
    pieces = refs[:-6]
    near = 4
    rows = pieces[0].shape[0]
    for k, piece in enumerate(pieces):
        half = place[0] if k < near else 1 - place[0]
        if len(pieces) == near:
            half = 0
        spot = place[1] ^ (k % near)
        begin = pl.multiple_of((half * near + spot) * rows, 16)
        full[pl.ds(begin, rows), :] = piece[...]
    begin = 0
    for out in (project, expand):
        height, width = out.shape[0], full.shape[1]
        for block in range(out.shape[1] // width):
            out[:, block * width : (block + 1) * width] = full[begin : begin + height, :].astype(F32)
            begin += height
    spatial[...] = full[begin : begin + spatial.shape[0], :].astype(F32)
    begin += spatial.shape[0]
    height = project.shape[1]
    for tap in range(3):
        time[tap, :height] = full[begin : begin + height, :].astype(F32)
        begin += height
    rest = time.shape[1] - height
    for tap in range(3):
        time[tap, height:] = full[begin : begin + rest, :].astype(F32)
        begin += rest
    lateral[...] = full[begin : begin + lateral.shape[0], :].astype(F32)


def per_device(
    slow_in,
    fast_in,
    clip_side,
    fast_reduce,
    fast_spatial,
    fast_expand,
    lateral_weight,
    slow_reduce,
    slow_spatial,
    slow_expand,
    slow_project,
    fast_reduce_norm,
    fast_spatial_norm,
    fast_expand_norm,
    lateral_norm,
    slow_reduce_norm,
    slow_spatial_norm,
    slow_expand_norm,
    slow_project_norm,
    slow_cot,
    fast_cot,
):
    axes = ("dp", "wa")
    wa_count = lax.axis_size("wa")
    place = lax.axis_index("wa")
    devices = lax.axis_size("dp") * wa_count
    clips = fast_in.shape[0]
    cells = fast_in.shape[2] * fast_in.shape[3]
    frames = slow_in.shape[1]
    packs = clips // GROUPS
    c_f, b_f = fast_reduce.shape[1], fast_reduce.shape[2]
    c_l = lateral_weight.shape[2]
    b_s = slow_reduce.shape[2]
    c_s = slow_expand.shape[1]
    c_cat = slow_project.shape[0]
    half = frames // 2

    def exchange(array):
        return lax.all_to_all(array, "wa", 0, 0, tiled=True)

    def gather_stats(copies):
        return lax.all_to_all(copies, axes, 0, 0, tiled=True)

    def gather_wide(sums):
        dp_count = lax.axis_size("dp")
        if dp_count == 2:
            sums = sums + lax.ppermute(sums, "dp", [(0, 1), (1, 0)])
            copies = jnp.broadcast_to(sums[None], (wa_count,) + sums.shape)
            return lax.all_to_all(copies, "wa", 0, 0, tiled=True)
        return gather_stats(jnp.broadcast_to(sums[None], (devices,) + sums.shape))

    smem = scalars()

    area = jnp.sum(clip_side * clip_side)
    area_all = lax.psum(area, "dp").astype(F32)
    fast_count = (area_all * (fast_in.shape[1] * wa_count)).reshape(1, 1)
    slow_count = (area_all * frames).reshape(1, 1)
    own_side = lax.dynamic_slice_in_dim(clip_side, place, 1)
    lane_sides = jnp.repeat(clip_side.reshape(packs, GROUPS), LANES // GROUPS, axis=1)
    lane_sides = lane_sides.reshape(packs, 1, LANES)

    eye = jnp.eye(GROUPS, dtype=BF)
    w_first = jnp.einsum("kio,gh->kgiho", fast_reduce, eye).reshape(3, GROUPS, c_f, LANES)
    w_first_back = w_first.transpose(1, 2, 0, 3).reshape(GROUPS, c_f, 3 * LANES)
    w_plane = jnp.einsum("ijab,gh->ijgahb", fast_spatial, eye).reshape(3, 3 * LANES, LANES)
    flipped = fast_spatial[::-1, ::-1].transpose(0, 1, 3, 2)
    w_plane_back = jnp.einsum("ijab,gh->ijgahb", flipped, eye).reshape(3, 3 * LANES, LANES)
    w_widen = jnp.einsum("io,gh->ghio", fast_expand, eye).reshape(GROUPS, LANES, c_f)
    params1 = jnp.tile(fast_reduce_norm, (1, GROUPS))
    params2 = jnp.tile(fast_spatial_norm, (1, GROUPS))
    w_time_lateral = slow_reduce[:, c_s:].reshape(3 * c_l, b_s)
    w_middle = slow_spatial.reshape(3, 3 * b_s, b_s)
    w_middle_back = slow_spatial[::-1, ::-1].transpose(0, 1, 3, 2).reshape(3, 3 * b_s, b_s)

    def pack(array):
        rows = frames * cells
        width = array.shape[4]
        flat = array.reshape(clips, rows, width)
        return launch(
            pack_kernel,
            "pack",
            (packs,),
            [(flat, pl.BlockSpec((GROUPS, rows, width), lambda i: (i, 0, 0)))],
            [((clips, rows // 2, 2 * width), BF, pl.BlockSpec((GROUPS, rows // 2, 2 * width), lambda i: (i, 0, 0)))],
        )[0]

    def unpack(array, shape):
        rows = frames * cells
        width = shape[4]
        return launch(
            unpack_kernel,
            "unpack",
            (packs,),
            [(array, pl.BlockSpec((GROUPS, rows // 2, 2 * width), lambda i: (i, 0, 0)))],
            [((clips, rows, width), BF, pl.BlockSpec((GROUPS, rows, width), lambda i: (i, 0, 0)))],
        )[0].reshape(shape)

    slow_got = exchange(pack(slow_in))
    cot_got = exchange(pack(slow_cot))

    x = fast_in.reshape(clips, 2, cells, c_f)
    x_spec = pl.BlockSpec((GROUPS, 2, cells, c_f), lambda i: (i, 0, 0, 0))
    packed_shape = (packs, 2, cells, LANES)
    packed_spec = pl.BlockSpec((1, 2, cells, LANES), lambda i: (i, 0, 0, 0))
    rim_shape = (packs, cells, LANES)
    rim_spec = pl.BlockSpec((1, cells, LANES), lambda i: (i, 0, 0))
    sides_spec = pl.BlockSpec((1, 1, LANES), lambda i: (i, 0, 0))
    stat8 = ((devices, 8, LANES), F32, pl.BlockSpec((devices, 8, LANES), lambda *_: (0, 0, 0)))
    acc8 = pltpu.VMEM((8, LANES), F32)
    fast_win = pltpu.VMEM((cells + 32, 3 * LANES), BF)

    y, to_next, to_prev = launch(
        fast_first,
        "fast_first",
        (packs,),
        [(x, x_spec), (w_first, whole(w_first))],
        [(packed_shape, F32, packed_spec), (rim_shape, BF, rim_spec), (rim_shape, BF, rim_spec)],
    )
    forward = [(i, i + 1) for i in range(wa_count - 1)]
    backward = [(i + 1, i) for i in range(wa_count - 1)]
    from_prev = lax.ppermute(to_next, "wa", forward)
    from_next = lax.ppermute(to_prev, "wa", backward)
    pre1, s1 = launch(
        fast_join,
        "fast_join",
        (packs,),
        [(y, packed_spec), (from_prev, rim_spec), (from_next, rim_spec), (lane_sides, sides_spec)],
        [(packed_shape, F32, packed_spec), stat8],
        [acc8],
        after=(slow_got,),
    )
    g1 = gather_stats(s1)
    act1, pre2, s2 = launch(
        fast_plane,
        "fast_plane",
        (packs,),
        [
            (fast_count, smem),
            (pre1, packed_spec),
            (g1, whole(g1)),
            (params1, whole(params1)),
            (lane_sides, sides_spec),
            (w_plane, whole(w_plane)),
        ],
        [(packed_shape, BF, packed_spec), (packed_shape, F32, packed_spec), stat8],
        [acc8, fast_win],
    )
    g2 = gather_stats(s2)
    act2, s3 = launch(
        fast_widen,
        "fast_widen",
        (packs,),
        [
            (fast_count, smem),
            (pre2, packed_spec),
            (g2, whole(g2)),
            (params2, whole(params2)),
            (lane_sides, sides_spec),
            (w_widen, whole(w_widen)),
        ],
        [(packed_shape, BF, packed_spec), stat8],
        [acc8],
    )
    g3 = gather_stats(s3)
    (fast_result,) = launch(
        fast_out,
        "fast_out",
        (packs,),
        [
            (fast_count, smem),
            (clip_side, smem),
            (x, x_spec),
            (act2, packed_spec),
            (g3, whole(g3)),
            (fast_expand_norm, whole(fast_expand_norm)),
            (w_widen, whole(w_widen)),
        ],
        [(x.shape, BF, x_spec)],
    )

    fast_got = exchange(fast_result.reshape(clips, 2 * cells, c_f)).reshape(4 * frames, cells, c_f)

    def stat(rows, width):
        return ((devices, rows, width), F32, pl.BlockSpec((devices, rows, width), lambda *_: (0, 0, 0)))

    pre_l, s_l = launch(
        lateral_enter,
        "lateral_enter",
        (),
        [(own_side, smem), (fast_got, whole(fast_got)), (lateral_weight, whole(lateral_weight))],
        [
            ((frames, cells, c_l), F32, pl.BlockSpec((frames, cells, c_l), lambda *_: (0, 0, 0))),
            stat(2, c_l),
        ],
        [pltpu.VMEM((2, c_l), F32)],
    )
    g_l = gather_stats(s_l)

    got_spec = pl.BlockSpec((wa_count, cells, LANES), lambda i: (0, i, 0))

    def pair_spec(width):
        return pl.BlockSpec((2, 1, cells, width), lambda i: (0, i, 0, 0))

    def frame_spec(width):
        return pl.BlockSpec((1, cells, width), lambda i: (i, 0, 0))

    def pairs(array):
        return array.reshape((2, half) + array.shape[1:])

    own, base_n, base_p = launch(
        slow_enter,
        "slow_enter",
        (half,),
        [(slow_got, got_spec), (slow_reduce, whole(slow_reduce)), (slow_project, whole(slow_project))],
        [
            ((2, half, cells, c_s), BF, pair_spec(c_s)),
            (
                (frames + 2, cells, b_s),
                F32,
                pl.BlockSpec((frames + 2, cells, b_s), lambda *_: (0, 0, 0)),
            ),
            ((2, half, cells, c_s), BF, pair_spec(c_s)),
        ],
        flops=2 * frames * cells * c_s * (3 * b_s + c_s),
    )
    own = own.reshape(frames, cells, c_s)
    base_p = base_p.reshape(frames, cells, c_s)
    lateral_act, pre_n, s_n = launch(
        narrow_enter,
        "narrow_enter",
        (),
        [
            (slow_count, smem),
            (own_side, smem),
            (pre_l, whole(pre_l)),
            (g_l, whole(g_l)),
            (lateral_norm, whole(lateral_norm)),
            (base_n, whole(base_n)),
            (w_time_lateral, whole(w_time_lateral)),
        ],
        [
            ((frames, cells, c_l), BF, pl.BlockSpec((frames, cells, c_l), lambda *_: (0, 0, 0))),
            ((frames, cells, b_s), F32, pl.BlockSpec((frames, cells, b_s), lambda *_: (0, 0, 0))),
            stat(2, b_s),
        ],
        [pltpu.VMEM((2, b_s), F32)],
    )
    g_n = gather_stats(s_n)
    slow_win = pltpu.VMEM((cells + 32, 3 * b_s), BF)
    act_n, pre_m, s_m = launch(
        middle_enter,
        "middle_enter",
        (frames,),
        [
            (slow_count, smem),
            (own_side, smem),
            (pre_n, frame_spec(b_s)),
            (g_n, whole(g_n)),
            (slow_reduce_norm, whole(slow_reduce_norm)),
            (w_middle, whole(w_middle)),
        ],
        [
            ((frames, cells, b_s), BF, frame_spec(b_s)),
            ((frames, cells, b_s), F32, frame_spec(b_s)),
            stat(2, b_s),
        ],
        [pltpu.VMEM((2, b_s), F32), slow_win],
    )
    g_m = gather_stats(s_m)
    act_m, project, s_w = launch(
        wide_enter,
        "wide_enter",
        (frames,),
        [
            (slow_count, smem),
            (own_side, smem),
            (pre_m, frame_spec(b_s)),
            (g_m, whole(g_m)),
            (slow_spatial_norm, whole(slow_spatial_norm)),
            (base_p, frame_spec(c_s)),
            (lateral_act, frame_spec(c_l)),
            (slow_expand, whole(slow_expand)),
            (slow_project, pl.BlockSpec((c_l, c_s), lambda i: (c_s // c_l, 0))),
        ],
        [
            ((frames, cells, b_s), BF, frame_spec(b_s)),
            ((frames, cells, c_s), BF, frame_spec(c_s)),
            ((4, c_s), F32, pl.BlockSpec((4, c_s), lambda *_: (0, 0))),
        ],
    )
    g_w = gather_wide(s_w)
    out_packed, wide_grad, t_w = launch(
        wide_out,
        "wide_out",
        (half,),
        [
            (slow_count, smem),
            (own_side, smem),
            (pairs(act_m), pair_spec(b_s)),
            (pairs(project), pair_spec(c_s)),
            (cot_got, got_spec),
            (g_w, whole(g_w)),
            (slow_expand_norm, whole(slow_expand_norm)),
            (slow_project_norm, whole(slow_project_norm)),
            (slow_expand, whole(slow_expand)),
        ],
        [
            ((wa_count, half * cells, LANES), BF, got_spec),
            ((2, half, cells, c_s), F32, pair_spec(c_s)),
            ((4, c_s), F32, pl.BlockSpec((4, c_s), lambda *_: (0, 0))),
        ],
    )
    wide_grad = wide_grad.reshape(frames, cells, c_s)
    h_w = gather_wide(t_w)
    result_got = exchange(out_packed)
    slow_result = unpack(result_got, slow_in.shape)

    middle_grad, expand_w_grad, t_m = launch(
        middle_back,
        "middle_back",
        (frames,),
        [
            (slow_count, smem),
            (own_side, smem),
            (wide_grad, frame_spec(c_s)),
            (act_m, frame_spec(b_s)),
            (g_w, whole(g_w)),
            (h_w, whole(h_w)),
            (slow_expand_norm, whole(slow_expand_norm)),
            (slow_expand, whole(slow_expand)),
            (pre_m, frame_spec(b_s)),
            (g_m, whole(g_m)),
            (slow_spatial_norm, whole(slow_spatial_norm)),
        ],
        [
            ((frames, cells, b_s), F32, frame_spec(b_s)),
            ((c_s, b_s), BF, pl.BlockSpec((c_s, b_s), lambda *_: (0, 0))),
            stat(2, b_s),
        ],
        [pltpu.VMEM((2, b_s), F32), pltpu.VMEM((b_s, c_s), F32)],
    )
    h_m = gather_stats(t_m)
    joined_part, project_w_grad = launch(
        project_back,
        "project_back",
        (frames,),
        [
            (slow_count, smem),
            (own_side, smem),
            (wide_grad, frame_spec(c_s)),
            (project, frame_spec(c_s)),
            (g_w, whole(g_w)),
            (h_w, whole(h_w)),
            (slow_project_norm, whole(slow_project_norm)),
            (own, frame_spec(c_s)),
            (lateral_act, frame_spec(c_l)),
            (slow_project, whole(slow_project)),
        ],
        [
            ((frames, cells, c_cat), BF, frame_spec(c_cat)),
            ((c_cat * c_s // b_s, b_s), BF, pl.BlockSpec((c_cat * c_s // b_s, b_s), lambda *_: (0, 0))),
        ],
        [pltpu.VMEM((c_cat, c_s), F32)],
        flops=4 * frames * cells * c_cat * c_s,
    )
    middle_low, narrow_grad, t_n = launch(
        narrow_back,
        "narrow_back",
        (frames,),
        [
            (slow_count, smem),
            (own_side, smem),
            (middle_grad, frame_spec(b_s)),
            (pre_m, frame_spec(b_s)),
            (g_m, whole(g_m)),
            (h_m, whole(h_m)),
            (slow_spatial_norm, whole(slow_spatial_norm)),
            (w_middle_back, whole(w_middle_back)),
            (pre_n, frame_spec(b_s)),
            (g_n, whole(g_n)),
            (slow_reduce_norm, whole(slow_reduce_norm)),
        ],
        [
            ((frames, cells, b_s), BF, frame_spec(b_s)),
            ((frames, cells, b_s), F32, frame_spec(b_s)),
            stat(2, b_s),
        ],
        [pltpu.VMEM((2, b_s), F32), slow_win],
    )
    h_n = gather_stats(t_n)
    (spatial_w_grad,) = launch(
        plane_weight,
        "plane_weight",
        (frames,),
        [(act_n, frame_spec(b_s)), (middle_low, frame_spec(b_s))],
        [((3, 3 * b_s, b_s), BF, pl.BlockSpec((3, 3 * b_s, b_s), lambda *_: (0, 0, 0)))],
        [pltpu.VMEM((3, 3 * b_s, b_s), F32), slow_win],
        flops=18 * frames * cells * b_s * b_s,
    )
    narrow_low, grad_packed, lateral_grad, t_l = launch(
        join_back,
        "join_back",
        (half,),
        [
            (slow_count, smem),
            (own_side, smem),
            (narrow_grad, whole(narrow_grad)),
            (pre_n, whole(pre_n)),
            (g_n, whole(g_n)),
            (h_n, whole(h_n)),
            (slow_reduce_norm, whole(slow_reduce_norm)),
            (slow_reduce, whole(slow_reduce)),
            (pairs(joined_part), pair_spec(c_cat)),
            (pairs(pre_l), pair_spec(c_l)),
            (g_l, whole(g_l)),
            (lateral_norm, whole(lateral_norm)),
        ],
        [
            (
                (frames + 2, cells, b_s),
                BF,
                pl.BlockSpec((frames + 2, cells, b_s), lambda *_: (0, 0, 0)),
            ),
            ((wa_count, half * cells, LANES), BF, got_spec),
            ((2, half, cells, c_l), F32, pair_spec(c_l)),
            stat(2, c_l),
        ],
        [pltpu.VMEM((2, c_l), F32)],
        after=(result_got,),
    )
    lateral_grad = lateral_grad.reshape(frames, cells, c_l)
    h_l = gather_stats(t_l)
    grad_got = exchange(grad_packed)
    slow_grad = unpack(grad_got, slow_in.shape)

    def time_weight(values):
        flat = values.reshape(frames * cells, values.shape[2])
        low = narrow_low.reshape((frames + 2) * cells, b_s)
        parts = []
        for tap in range(3):
            begin = (2 - tap) * cells
            parts.append(
                lax.dot_general(
                    flat,
                    lax.slice_in_dim(low, begin, begin + frames * cells, 1, 0),
                    (((0,), (0,)), ((), ())),
                    preferred_element_type=F32,
                )
            )
        return jnp.stack(parts).astype(BF)

    lateral_low, frames_back = launch(
        lateral_back,
        "lateral_back",
        (),
        [
            (slow_count, smem),
            (own_side, smem),
            (lateral_grad, whole(lateral_grad)),
            (pre_l, whole(pre_l)),
            (g_l, whole(g_l)),
            (h_l, whole(h_l)),
            (lateral_norm, whole(lateral_norm)),
            (lateral_weight, whole(lateral_weight)),
        ],
        [
            ((frames, cells, c_l), BF, pl.BlockSpec((frames, cells, c_l), lambda *_: (0, 0, 0))),
            ((4 * frames, cells, c_f), BF, pl.BlockSpec((4 * frames, cells, c_f), lambda *_: (0, 0, 0))),
        ],
    )
    back_got = exchange(frames_back.reshape(wa_count, 2 * cells, c_f)).reshape(x.shape)
    (lateral_w_grad,) = launch(
        lateral_weight_back,
        "lateral_weight_back",
        (),
        [(fast_got, whole(fast_got)), (lateral_low, whole(lateral_low))],
        [((5 * c_f, c_l), BF, pl.BlockSpec((5 * c_f, c_l), lambda *_: (0, 0)))],
        [pltpu.VMEM((5 * c_f, c_l), F32)],
    )

    weight_parts = [
        part.reshape(-1, b_s)
        for part in (
            project_w_grad,
            expand_w_grad,
            spatial_w_grad,
            time_weight(own),
            time_weight(lateral_act),
            lateral_w_grad,
        )
    ]
    sizes = [part.shape[0] for part in weight_parts]
    near = 4
    inner = [[near * k + j for j in range(near)] for k in range(wa_count // near)]
    outer = [[near * k + j for k in range(wa_count // near)] for j in range(near)]
    dp_count = lax.axis_size("dp")
    core = lax.axis_index("dp")
    swap = [(0, 1), (1, 0)]
    paired = dp_count == 2
    if paired:
        others = [lax.ppermute(part, "dp", swap) for part in weight_parts]
        rows = sum(sizes) // 2
        place_core = core.reshape(1)
        (weights,) = launch(
            weight_merge,
            "weight_merge",
            (),
            [(place_core, smem)] + [(part, whole(part)) for part in weight_parts + others],
            [((rows, b_s), BF, pl.BlockSpec((rows, b_s), lambda *_: (0, 0)))],
        )
    else:
        weights = jnp.concatenate(weight_parts, axis=0)
    first_stage = lax.psum_scatter(weights, "wa", axis_index_groups=inner, tiled=True)
    second_stage = lax.psum(first_stage, "wa", axis_index_groups=outer)

    cot = fast_cot.reshape(x.shape)
    fast_grad3, t3 = launch(
        fast_back_sum,
        "fast_back_sum",
        (packs,),
        [
            (fast_count, smem),
            (clip_side, smem),
            (cot, x_spec),
            (back_got, x_spec),
            (x, x_spec),
            (act2, packed_spec),
            (g3, whole(g3)),
            (fast_expand_norm, whole(fast_expand_norm)),
            (w_widen, whole(w_widen)),
        ],
        [(x.shape, F32, x_spec), stat8],
        [acc8],
        after=(first_stage,),
    )
    h3 = gather_stats(t3)
    fast_grad2, widen_blocks, t2 = launch(
        fast_back_widen,
        "fast_back_widen",
        (packs,),
        [
            (fast_count, smem),
            (clip_side, smem),
            (fast_grad3, x_spec),
            (act2, packed_spec),
            (g3, whole(g3)),
            (h3, whole(h3)),
            (fast_expand_norm, whole(fast_expand_norm)),
            (w_widen, whole(w_widen)),
            (pre2, packed_spec),
            (g2, whole(g2)),
            (params2, whole(params2)),
            (lane_sides, sides_spec),
        ],
        [
            (packed_shape, F32, packed_spec),
            ((GROUPS, LANES, c_f), F32, pl.BlockSpec((GROUPS, LANES, c_f), lambda *_: (0, 0, 0))),
            stat8,
        ],
        [acc8],
    )
    h2 = gather_stats(t2)
    fast_grad1, plane_blocks, t1 = launch(
        fast_back_plane,
        "fast_back_plane",
        (packs,),
        [
            (fast_count, smem),
            (fast_grad2, packed_spec),
            (pre2, packed_spec),
            (g2, whole(g2)),
            (h2, whole(h2)),
            (params2, whole(params2)),
            (act1, packed_spec),
            (pre1, packed_spec),
            (g1, whole(g1)),
            (params1, whole(params1)),
            (lane_sides, sides_spec),
            (w_plane_back, whole(w_plane_back)),
        ],
        [
            (packed_shape, F32, packed_spec),
            (
                (3, 3 * LANES, LANES),
                F32,
                pl.BlockSpec((3, 3 * LANES, LANES), lambda *_: (0, 0, 0)),
            ),
            stat8,
        ],
        [acc8, fast_win],
    )
    h1 = gather_stats(t1)
    (low1,) = launch(
        fast_back_first,
        "fast_back_first",
        (packs,),
        [
            (fast_count, smem),
            (fast_grad1, packed_spec),
            (pre1, packed_spec),
            (g1, whole(g1)),
            (h1, whole(h1)),
            (params1, whole(params1)),
            (lane_sides, sides_spec),
        ],
        [((2, packs, cells, LANES), BF, pl.BlockSpec((2, 1, cells, LANES), lambda i: (0, i, 0, 0)))],
    )
    low_prev = lax.ppermute(low1[1], "wa", forward)
    low_next = lax.ppermute(low1[0], "wa", backward)
    fast_grad, first_blocks, second_stage = launch(
        fast_back_out,
        "fast_back_out",
        (packs,),
        [
            (fast_grad3, x_spec),
            (low1, pl.BlockSpec((2, 1, cells, LANES), lambda i: (0, i, 0, 0))),
            (low_prev, rim_spec),
            (low_next, rim_spec),
            (x, x_spec),
            (w_first_back, whole(w_first_back)),
        ],
        [
            (x.shape, BF, x_spec),
            (
                (GROUPS, c_f, 3 * LANES),
                F32,
                pl.BlockSpec((GROUPS, c_f, 3 * LANES), lambda *_: (0, 0, 0)),
            ),
        ],
        after=(grad_got,),
        carry=(second_stage,),
    )
    pieces = [second_stage] + [
        lax.ppermute(second_stage, "wa", [(i, i ^ step) for i in range(wa_count)])
        for step in range(1, near)
    ]
    if paired:
        pieces = pieces + [lax.ppermute(piece, "dp", swap) for piece in pieces]
    else:
        pieces = [lax.psum(piece, "dp") for piece in pieces]

    final = [
        ((c_cat, c_s), F32),
        ((b_s, c_s), F32),
        ((9 * b_s, b_s), F32),
        ((3, c_cat, b_s), F32),
        ((5 * c_f, c_l), F32),
    ]
    project_all, expand_all, spatial_all, time_all, lateral_all = launch(
        weight_split,
        "weight_split",
        (),
        [(jnp.stack([core, place % near]), smem)] + [(piece, whole(piece)) for piece in pieces],
        [
            (shape, dtype, pl.BlockSpec(shape, lambda *_, rank=len(shape): (0,) * rank))
            for shape, dtype in final
        ],
        [pltpu.VMEM((sum(sizes), b_s), BF)],
    )
    expand_part = sum(widen_blocks[g, g * b_f : (g + 1) * b_f] for g in range(GROUPS))
    plane_view = plane_blocks.reshape(3, 3, GROUPS, b_f, GROUPS, b_f)
    spatial_part = sum(plane_view[:, :, g, :, g] for g in range(GROUPS))
    first_view = first_blocks.reshape(GROUPS, c_f, 3, GROUPS, b_f)
    reduce_part = sum(first_view[g, :, :, g] for g in range(GROUPS)).transpose(1, 0, 2)

    small = jnp.concatenate(
        [reduce_part.reshape(-1), spatial_part.reshape(-1), expand_part.reshape(-1)]
    )
    share = -(-small.shape[0] // (devices * LANES)) * LANES
    padded = jnp.pad(small, (0, share * devices - small.shape[0])).reshape(devices, share // LANES, LANES)
    mine = jnp.sum(gather_stats(padded), axis=0)
    small_all = gather_stats(jnp.broadcast_to(mine[None], padded.shape)).reshape(-1)
    first_size, plane_size = reduce_part.size, spatial_part.size
    fast_reduce_grad = small_all[:first_size].reshape(fast_reduce.shape)
    fast_spatial_grad = small_all[first_size : first_size + plane_size].reshape(fast_spatial.shape)
    fast_expand_grad = small_all[first_size + plane_size : small.shape[0]].reshape(fast_expand.shape)

    def norm_grad(sums, moments, count, folded=False):
        total, moment = jnp.sum(sums, axis=0), jnp.sum(moments, axis=0)
        if folded:
            total = total.reshape(total.shape[0], GROUPS, -1).sum(axis=1)
            moment = moment.reshape(moment.shape[0], GROUPS, -1).sum(axis=1)
        mean = moment[0] / count[0, 0]
        inv = lax.rsqrt(moment[1] / count[0, 0] - mean * mean + EPSILON)
        return jnp.stack([total[1] * inv, total[0]])

    h_project = jnp.concatenate([h_w[:, 0:1], h_w[:, 2:3]], axis=1)
    return (
        slow_result,
        fast_result.reshape(fast_in.shape),
        slow_grad,
        fast_grad.reshape(fast_in.shape),
        fast_reduce_grad,
        fast_spatial_grad,
        fast_expand_grad,
        lateral_all.reshape(lateral_weight.shape),
        time_all,
        spatial_all.reshape(slow_spatial.shape),
        expand_all,
        project_all,
        norm_grad(h1, g1, fast_count, True),
        norm_grad(h2, g2, fast_count, True),
        norm_grad(h3, g3, fast_count),
        norm_grad(h_l, g_l, slow_count),
        norm_grad(h_n, g_n, slow_count),
        norm_grad(h_m, g_m, slow_count),
        norm_grad(h_w[:, 0:2], g_w[:, 0:2], slow_count),
        norm_grad(h_project, g_w[:, 2:4], slow_count),
    )


def solution(mesh):
    wide = P("dp", None, None, None, "wa")
    fast = P("dp", "wa", None, None, None)
    same = P()
    return jax.shard_map(
        per_device,
        mesh=mesh,
        in_specs=(wide, fast, P("dp")) + (same,) * 16 + (wide, fast),
        out_specs=(wide, fast, wide, fast) + (same,) * 16,
        check_vma=False,
    )
```

```python
import functools

import jax
import jax.numpy as jnp
from jax import lax
from jax.experimental import pallas as pl
from jax.experimental.pallas import tpu as pltpu
from jax.sharding import PartitionSpec as P

EPSILON = 1e-05
BF = jnp.bfloat16
F32 = jnp.float32
LANES = 128
GROUPS = 4
VMEM_BYTES = 52 * 1024 * 1024


def whole(array):
    rank = len(array.shape)
    return pl.BlockSpec(array.shape, lambda *_: (0,) * rank)


def scalars():
    return pl.BlockSpec(memory_space=pltpu.SMEM)


def launch(body, name, grid, inputs, outputs, scratch=(), flops=0, after=(), carry=()):
    used, given = len(inputs), len(outputs)
    held = pl.BlockSpec(memory_space=pl.ANY)
    inputs = inputs + [(array, held) for array in (*after, *carry)]
    outputs = outputs + [(array.shape, array.dtype, held) for array in carry]
    first = used + len(after)
    aliases = {first + k: given + k for k in range(len(carry))}

    def kernel(*refs):
        outs = refs[len(inputs) :]
        body(*refs[:used], *outs[:given], *outs[len(outputs) :])

    traffic = sum(a.size * a.dtype.itemsize for a, _ in inputs)
    for shape, dtype, _ in outputs:
        count = 1
        for entry in shape:
            count *= entry
        traffic += count * jnp.dtype(dtype).itemsize
    return pl.pallas_call(
        kernel,
        name=name,
        grid=grid,
        in_specs=[spec for _, spec in inputs],
        out_specs=[spec for _, _, spec in outputs],
        out_shape=[jax.ShapeDtypeStruct(shape, dtype) for shape, dtype, _ in outputs],
        scratch_shapes=list(scratch),
        input_output_aliases=aliases,
        compiler_params=pltpu.CompilerParams(vmem_limit_bytes=VMEM_BYTES),
        cost_estimate=pl.CostEstimate(flops=flops, bytes_accessed=traffic, transcendentals=0),
    )(*[array for array, _ in inputs])


def dot(a, b):
    return lax.dot_general(a, b, (((1,), (0,)), ((), ())), preferred_element_type=F32)


def dot_nt(a, b):
    return lax.dot_general(a, b, (((1,), (1,)), ((), ())), preferred_element_type=F32)


def dot_tn(a, b):
    return lax.dot_general(a, b, (((0,), (0,)), ((), ())), preferred_element_type=F32)


def silu_half(v):
    return v * (1.0 + jnp.tanh(v))


def slope_half(v):
    h = 1.0 + jnp.tanh(v)
    return h + v * h * (2.0 - h)


def cell_ids(rows):
    ids = lax.broadcasted_iota(jnp.int32, (rows, 1), 0)
    return (ids >> 4) & 15, ids & 15


def clip_mask(side, rows):
    h, w = cell_ids(rows)
    return jnp.where((h < side) & (w < side), 1.0, 0.0).astype(F32)


def packed_mask(side_row, rows):
    ids = lax.broadcasted_iota(jnp.int32, (rows, LANES), 0)
    h, w = (ids >> 4) & 15, ids & 15
    return jnp.where((h < side_row) & (w < side_row), 1.0, 0.0).astype(F32)


def fold(row):
    width = LANES // GROUPS
    out = row
    for step in range(1, GROUPS):
        out = out + pltpu.roll(row, step * width, 1)
    return out


def norm_terms(gathered, params, count, folded=False):
    total = jnp.sum(gathered, axis=0)
    if folded:
        total = fold(total)
    mean = total[0:1] / count
    variance = total[1:2] / count - mean * mean
    inv = lax.rsqrt(variance + EPSILON)
    scale = 0.5 * params[0:1] * inv
    return mean, inv, scale, 0.5 * params[1:2] - mean * scale


def back_terms(gathered, params, count, mean, inv, folded=False):
    total = jnp.sum(gathered, axis=0)
    if folded:
        total = fold(total)
    a = params[0:1] * inv
    b = -a * inv * inv * (total[1:2] - mean * total[0:1]) / count
    return a, b, -a * total[0:1] / count - b * mean


def col_sum(v):
    return jnp.sum(v, axis=0, keepdims=True)


def add_stats(acc, first, rows, values):
    @pl.when(first)
    def _():
        acc[...] = jnp.zeros_like(acc)

    for row, value in zip(rows, values):
        acc[row : row + 1, :] += value


def send_stats(last, acc, out):
    @pl.when(last)
    def _():
        out[...] = jnp.broadcast_to(acc[...][None], out.shape)


def put_columns(wide, out):
    rows, width = wide.shape[0], out.shape[1]
    for block in range(wide.shape[1] // width):
        out[block * rows : (block + 1) * rows, :] = wide[:, block * width : (block + 1) * width].astype(BF)


def fill_windows(scratch, values, first, cells):
    rows = values.shape[0]
    w = lax.broadcasted_iota(jnp.int32, (rows, 1), 0) & (cells - 1)
    left = jnp.where(w == 0, 0.0, pltpu.roll(values, 1, 0))
    right = jnp.where(w == cells - 1, 0.0, pltpu.roll(values, rows - 1, 0))
    scratch[first : first + rows, :] = jnp.concatenate(
        [left.astype(BF), values.astype(BF), right.astype(BF)], axis=1
    )


def clear_gaps(scratch, frames, cells):
    pitch = cells * (cells + 1)
    for frame in range(frames + 1):
        scratch[frame * pitch : frame * pitch + cells, :] = jnp.zeros((cells, scratch.shape[1]), BF)


def plane_dot(scratch, weight, frames, cells):
    rows = frames * cells * (cells + 1) - cells
    out = dot(scratch[0:rows, :], weight[0])
    for tap in (1, 2):
        out = out + dot(scratch[tap * cells : tap * cells + rows, :], weight[tap])
    return out


def window_shape(frames, width):
    return pltpu.VMEM((frames * 272 + 16, width), BF)


def fast_first(x, w, y, to_next, to_prev):
    def over(frame, tap):
        out = dot(x[0, frame], w[tap, 0])
        for g in range(1, GROUPS):
            out = out + dot(x[g, frame], w[tap, g])
        return out

    y[0, 0] = over(0, 1) + over(1, 2)
    y[0, 1] = over(0, 0) + over(1, 1)
    to_next[0] = over(1, 0).astype(BF)
    to_prev[0] = over(0, 2).astype(BF)


def fast_join(y, from_prev, from_next, sides, pre, stats, acc):
    i = pl.program_id(0)
    mask = packed_mask(sides[0], 256)
    first = y[0, 0] + from_prev[0].astype(F32)
    second = y[0, 1] + from_next[0].astype(F32)
    pre[0, 0] = first
    pre[0, 1] = second
    m1, m2 = first * mask, second * mask
    add_stats(acc, i == 0, (0, 1), (col_sum(m1 + m2), col_sum(m1 * first + m2 * second)))
    send_stats(i == pl.num_programs(0) - 1, acc, stats)


def fast_plane(count, pre, g1, params, sides, w, act, out, stats, acc, win):
    i = pl.program_id(0)
    _, _, scale, shift = norm_terms(g1[...], params[...], count[0, 0], True)
    mask = packed_mask(sides[0], 256)

    @pl.when(i == 0)
    def _():
        clear_gaps(win, 2, 16)

    for frame in range(2):
        a = mask * silu_half(pre[0, frame] * scale + shift)
        act[0, frame] = a.astype(BF)
        fill_windows(win, a, 16 + 272 * frame, 16)
    both = plane_dot(win, w, 2, 16)
    v0, v1 = both[0:256], both[272:528]
    out[0, 0] = v0
    out[0, 1] = v1
    m0, m1 = mask * v0, mask * v1
    add_stats(acc, i == 0, (0, 1), (col_sum(m0 + m1), col_sum(m0 * v0 + m1 * v1)))
    send_stats(i == pl.num_programs(0) - 1, acc, stats)


def fast_widen(count, pre, g2, params, sides, w, act, stats, acc):
    i = pl.program_id(0)
    _, _, scale, shift = norm_terms(g2[...], params[...], count[0, 0], True)
    mask = packed_mask(sides[0], 512)
    a = (mask * silu_half(pre[0].reshape(512, LANES) * scale + shift)).astype(BF)
    act[0] = a.reshape(2, 256, LANES)
    total, square = None, None
    for g in range(GROUPS):
        v = dot(a, w[g])
        total = v if total is None else total + v
        square = v * v if square is None else square + v * v
    add_stats(acc, i == 0, (0, 1), (col_sum(total), col_sum(square)))
    send_stats(i == pl.num_programs(0) - 1, acc, stats)


def fast_out(count, sides, x, act, g3, params, w, result):
    i = pl.program_id(0)
    _, _, scale, shift = norm_terms(g3[...], params[...], count[0, 0])
    a = act[0].reshape(512, LANES)
    for g in range(GROUPS):
        mask = clip_mask(sides[i * GROUPS + g], 512)
        v = 0.5 * x[g].reshape(512, LANES).astype(F32) + (dot(a, w[g]) * scale + shift)
        result[g] = (mask * silu_half(v)).astype(BF).reshape(2, 256, LANES)


def fast_back_sum(count, sides, cot, back, x, act, g3, params, w, grad, stats, acc):
    i = pl.program_id(0)
    _, _, scale, shift = norm_terms(g3[...], params[...], count[0, 0])
    a = act[0].reshape(512, LANES)
    total, cross = None, None
    for g in range(GROUPS):
        mask = 0.5 * clip_mask(sides[i * GROUPS + g], 512)
        v = dot(a, w[g])
        u = 0.5 * x[g].reshape(512, LANES).astype(F32) + (v * scale + shift)
        given = cot[g].reshape(512, LANES).astype(F32) + back[g].reshape(512, LANES).astype(F32)
        e = given * (mask * slope_half(u))
        grad[g] = e.reshape(2, 256, LANES)
        total = e if total is None else total + e
        cross = e * v if cross is None else cross + e * v
    add_stats(acc, i == 0, (0, 1), (col_sum(total), col_sum(cross)))
    send_stats(i == pl.num_programs(0) - 1, acc, stats)


def fast_back_widen(
    count, sides, grad, act, g3, h3, params3, w, pre, g2, params2, lane_sides, out, w_grad, stats, acc
):
    i = pl.program_id(0)
    c = count[0, 0]
    mean3, inv3, _, _ = norm_terms(g3[...], params3[...], c)
    a, b, d = back_terms(h3[...], params3[...], c, mean3, inv3)
    _, _, scale2, shift2 = norm_terms(g2[...], params2[...], c, True)
    lane_mask = 0.5 * packed_mask(lane_sides[0], 512)

    @pl.when(i == 0)
    def _():
        w_grad[...] = jnp.zeros_like(w_grad)

    s = act[0].reshape(512, LANES)
    back = None
    for g in range(GROUPS):
        mask = clip_mask(sides[i * GROUPS + g], 512)
        v = dot(s, w[g])
        low = (mask * (grad[g].reshape(512, LANES) * a + v * b + d)).astype(BF)
        part = dot_nt(low, w[g])
        back = part if back is None else back + part
        w_grad[g] += dot_tn(s, low)
    p = pre[0].reshape(512, LANES)
    e = back * (lane_mask * slope_half(p * scale2 + shift2))
    out[0] = e.reshape(2, 256, LANES)
    add_stats(acc, i == 0, (0, 1), (col_sum(e), col_sum(e * p)))
    send_stats(i == pl.num_programs(0) - 1, acc, stats)


def fast_back_plane(
    count, e2, pre2, g2, h2, params2, act1, pre1, g1, params1, lane_sides, w, out, w_grad, stats, acc, win, low
):
    i = pl.program_id(0)
    c = count[0, 0]
    mean2, inv2, _, _ = norm_terms(g2[...], params2[...], c, True)
    a, b, d = back_terms(h2[...], params2[...], c, mean2, inv2, True)
    _, _, scale1, shift1 = norm_terms(g1[...], params1[...], c, True)
    mask = packed_mask(lane_sides[0], 256)

    @pl.when(i == 0)
    def _():
        w_grad[...] = jnp.zeros_like(w_grad)
        clear_gaps(win, 2, 16)
        low[256:272, :] = jnp.zeros((16, LANES), BF)

    for frame in range(2):
        part = mask * (e2[0, frame] * a + pre2[0, frame] * b + d)
        low[272 * frame : 272 * frame + 256, :] = part.astype(BF)
        fill_windows(win, part, 16 + 272 * frame, 16)
    both = plane_dot(win, w, 2, 16)
    total, cross = None, None
    for frame in range(2):
        p = pre1[0, frame]
        e = both[272 * frame : 272 * frame + 256] * (0.5 * mask * slope_half(p * scale1 + shift1))
        out[0, frame] = e
        total = e if total is None else total + e
        cross = e * p if cross is None else cross + e * p
        fill_windows(win, act1[0, frame].astype(F32), 16 + 272 * frame, 16)
    for tap in range(3):
        w_grad[tap] += dot_tn(win[16 * tap : 16 * tap + 528, :], low[...])
    add_stats(acc, i == 0, (0, 1), (col_sum(total), col_sum(cross)))
    send_stats(i == pl.num_programs(0) - 1, acc, stats)


def fast_back_first(count, e1, pre1, g1, h1, params1, lane_sides, low):
    c = count[0, 0]
    mean1, inv1, _, _ = norm_terms(g1[...], params1[...], c, True)
    a, b, d = back_terms(h1[...], params1[...], c, mean1, inv1, True)
    mask = packed_mask(lane_sides[0], 256)
    for frame in range(2):
        low[frame, 0] = (mask * (e1[0, frame] * a + pre1[0, frame] * b + d)).astype(BF)


def fast_back_out(grad, low, from_prev, from_next, x, w, out, w_grad):
    i = pl.program_id(0)

    @pl.when(i == 0)
    def _():
        w_grad[...] = jnp.zeros_like(w_grad)

    around = (from_prev[0], low[0, 0], low[1, 0], from_next[0])
    for frame in range(2):
        before, here, after = around[frame], around[frame + 1], around[frame + 2]
        joined = jnp.concatenate([after, here, before], axis=1)
        for g in range(GROUPS):
            out[g, frame] = (grad[g, frame] + dot_nt(joined, w[g])).astype(BF)
            w_grad[g] += dot_tn(x[g, frame], joined)


def pack_kernel(spot, x, *pieces):
    half = x.shape[1] // 2
    for step, piece in enumerate(pieces):
        clip = spot[0] ^ step
        piece[...] = jnp.concatenate([x[clip, :half], x[clip, half:]], axis=1)


def unpack_pieces(spot, *refs):
    out = refs[-1]
    whole_array = len(refs) == 2
    for k in range(out.shape[0]):
        clip = k if whole_array else spot[0] ^ k
        piece = refs[0][k] if whole_array else refs[k][...]
        half, width = piece.shape[0], piece.shape[1] // 2
        out[clip, :half] = piece[:, :width]
        out[clip, half:] = piece[:, width:]


def gather_halves(spot, pieces, x):
    for step, piece in enumerate(pieces):
        x[spot[0] ^ step] = piece[...]
    devices, _, lanes = x.shape
    width = lanes // 2
    low, high = [], []
    for j in range(devices):
        part = x[j]
        low.append(part[:, :width])
        high.append(part[:, width:])
    return jnp.concatenate(low, axis=1), jnp.concatenate(high, axis=1)


def scatter_halves(low, high, out):
    devices, _, lanes = out.shape
    width = lanes // 2
    for j in range(devices):
        out[j] = jnp.concatenate(
            [low[:, j * width : (j + 1) * width], high[:, j * width : (j + 1) * width]], axis=1
        )


def slow_enter(spot, w_time, w_project, *refs):
    *pieces, own, narrow, project, packed = refs
    i = pl.program_id(0)
    frames = narrow.shape[0] - 2

    @pl.when(i == 0)
    def _():
        narrow[...] = jnp.zeros_like(narrow)

    for half, frame in enumerate(gather_halves(spot, pieces, packed)):
        own[half, 0] = frame
        depth = frame.shape[1]
        project[half, 0] = dot(frame, w_project[:depth]).astype(BF)
        t = i + half * (frames // 2)
        for tap in range(3):
            narrow[t + 2 - tap] += dot(frame, w_time[tap, :depth])


def lateral_enter(side, fast, w, pre, stats, acc):
    frames = pre.shape[0]
    width = w.shape[1]
    mask = clip_mask(side[0], 256)
    for t in range(frames):
        taps = [k for k in range(5) if 0 <= 4 * t - 2 + k < 4 * frames]
        joined = jnp.concatenate([fast[4 * t - 2 + k] for k in taps], axis=1)
        v = dot(joined, w[taps[0] : taps[-1] + 1].reshape(len(taps) * width, w.shape[2]))
        pre[t] = v
        mv = mask * v
        add_stats(acc, t == 0, (0, 1), (col_sum(mv), col_sum(mv * v)))
    send_stats(True, acc, stats)


def narrow_enter(count, side, lateral, gl, params, base, w, act, pre, stats, acc):
    frames = pre.shape[0]
    _, _, scale, shift = norm_terms(gl[...], params[...], count[0, 0])
    mask = clip_mask(side[0], 256)
    for t in range(frames):
        act[t] = (mask * silu_half(lateral[t] * scale + shift)).astype(BF)
    width = act.shape[2]
    for t in range(frames):
        taps = [k for k in range(3) if 0 <= t - 1 + k < frames]
        joined = jnp.concatenate([act[t - 1 + k] for k in taps], axis=1)
        v = base[t + 1] + dot(joined, w[taps[0] * width : (taps[-1] + 1) * width, :])
        pre[t] = v
        mv = mask * v
        add_stats(acc, t == 0, (0, 1), (col_sum(mv), col_sum(mv * v)))
    send_stats(True, acc, stats)


def middle_enter(count, side, pre, gn, params, w, act, out, stats, acc, win):
    i = pl.program_id(0)
    frames = pre.shape[0]
    _, _, scale, shift = norm_terms(gn[...], params[...], count[0, 0])
    mask = clip_mask(side[0], 256)

    @pl.when(i == 0)
    def _():
        clear_gaps(win, frames, 16)

    for frame in range(frames):
        a = mask * silu_half(pre[frame] * scale + shift)
        act[frame] = a.astype(BF)
        fill_windows(win, a, 16 + 272 * frame, 16)
    v = plane_dot(win, w, frames, 16)
    total, square = None, None
    for frame in range(frames):
        part = v[272 * frame : 272 * frame + 256]
        out[frame] = part
        masked = mask * part
        total = masked if total is None else total + masked
        square = masked * part if square is None else square + masked * part
    add_stats(acc, i == 0, (0, 1), (col_sum(total), col_sum(square)))
    send_stats(i == pl.num_programs(0) - 1, acc, stats)


def flat(ref):
    block = ref[...]
    return block.reshape(block.shape[0] * block.shape[1], block.shape[2])


def wide_enter(count, side, pre, gm, params, base, lateral, w, w_project, act, project, acc):
    i = pl.program_id(0)
    _, _, scale, shift = norm_terms(gm[...], params[...], count[0, 0])
    rows = pre.shape[0] * pre.shape[1]
    mask = clip_mask(side[0], rows)
    a = (mask * silu_half(flat(pre) * scale + shift)).astype(BF)
    act[...] = a.reshape(act.shape)
    v = dot(a, w[...])
    p = flat(base).astype(F32) + dot(flat(lateral), w_project[...])
    project[...] = p.astype(BF).reshape(project.shape)
    mp = mask * p
    add_stats(
        acc, i == 0, (0, 1, 2, 3), (col_sum(v), col_sum(v * v), col_sum(mp), col_sum(mp * p))
    )


def wide_out(count, side, spot, act, project, g, params_w, params_p, w, *refs):
    devices = (len(refs) - 3) // 2
    cots, pieces, (grad, acc, packed) = refs[:devices], refs[devices : 2 * devices], refs[2 * devices :]
    i = pl.program_id(0)
    c = count[0, 0]
    gathered = g[...]
    _, _, scale_w, shift_w = norm_terms(gathered[:, 0:2], params_w[...], c)
    _, _, scale_p, shift_p = norm_terms(gathered[:, 2:4], params_p[...], c)
    mask = clip_mask(side[0], 256)
    half_mask = 0.5 * mask
    shift = shift_w + shift_p
    halves = []
    sums = [None, None, None]
    for half, cot_half in enumerate(gather_halves(spot, cots, packed)):
        v = dot(act[half, 0], w[...])
        p = project[half, 0].astype(F32)
        u = v * scale_w + (p * scale_p + shift)
        h = 1.0 + jnp.tanh(u)
        s = u * h
        halves.append((mask * s).astype(BF))
        e = (half_mask * cot_half.astype(F32)) * (h + s * (2.0 - h))
        grad[half, 0] = e
        for k, value in enumerate((e, e * v, e * p)):
            value = col_sum(value)
            sums[k] = value if sums[k] is None else sums[k] + value
    scatter_halves(halves[0], halves[1], packed)
    for step, piece in enumerate(pieces):
        piece[...] = packed[spot[0] ^ step]
    add_stats(acc, i == 0, (0, 1, 2), sums)


def middle_back(
    count, side, grad, act, g, h, params_w, w, pre, gm, params_m, out, w_grad, stats, acc, w_acc
):
    i = pl.program_id(0)
    c = count[0, 0]
    mean_w, inv_w, _, _ = norm_terms(g[...][:, 0:2], params_w[...], c)
    a, b, d = back_terms(h[...][:, 0:2], params_w[...], c, mean_w, inv_w)
    _, _, scale_m, shift_m = norm_terms(gm[...], params_m[...], c)
    mask = clip_mask(side[0], pre.shape[0] * pre.shape[1])
    s = flat(act)
    v = dot(s, w[...])
    low = (mask * (flat(grad) * a + v * b + d)).astype(BF)
    p = flat(pre)
    e = dot_nt(low, w[...]) * (0.5 * mask * slope_half(p * scale_m + shift_m))
    out[...] = e.reshape(out.shape)
    add_stats(acc, i == 0, (0, 1), (col_sum(e), col_sum(e * p)))
    send_stats(i == pl.num_programs(0) - 1, acc, stats)

    @pl.when(i == 0)
    def _():
        w_acc[...] = jnp.zeros_like(w_acc)

    w_acc[...] += dot_tn(s, low)

    @pl.when(i == pl.num_programs(0) - 1)
    def _():
        put_columns(w_acc, w_grad)


def project_back(
    count, side, grad, project, g, h, params_p, own, lateral, w, joined, w_grad, w_acc
):
    i = pl.program_id(0)
    c = count[0, 0]
    mean_p, inv_p, _, _ = norm_terms(g[...][:, 2:4], params_p[...], c)
    rows = h[...]
    total = jnp.concatenate([rows[:, 0:1], rows[:, 2:3]], axis=1)
    a, b, d = back_terms(total, params_p[...], c, mean_p, inv_p)
    mask = clip_mask(side[0], grad.shape[0] * grad.shape[1])
    low = (mask * (flat(grad) * a + flat(project).astype(F32) * b + d)).astype(BF)
    joined[...] = dot_nt(low, w[...]).astype(BF).reshape(joined.shape)

    @pl.when(i == 0)
    def _():
        w_acc[...] = jnp.zeros_like(w_acc)

    width = own.shape[2]
    w_acc[0:width, :] += dot_tn(flat(own), low)
    w_acc[width:, :] += dot_tn(flat(lateral), low)

    @pl.when(i == pl.num_programs(0) - 1)
    def _():
        put_columns(w_acc, w_grad)


def narrow_back(
    count, side, grad, pre_m, gm, hm, params_m, w, pre_n, gn, params_n, low_out, out, stats, acc, win
):
    i = pl.program_id(0)
    frames = grad.shape[0]
    c = count[0, 0]
    mean_m, inv_m, _, _ = norm_terms(gm[...], params_m[...], c)
    a, b, d = back_terms(hm[...], params_m[...], c, mean_m, inv_m)
    _, _, scale_n, shift_n = norm_terms(gn[...], params_n[...], c)
    mask = clip_mask(side[0], 256)

    @pl.when(i == 0)
    def _():
        clear_gaps(win, frames, 16)

    for frame in range(frames):
        low = mask * (grad[frame] * a + pre_m[frame] * b + d)
        low_out[frame] = low.astype(BF)
        fill_windows(win, low, 16 + 272 * frame, 16)
    back = plane_dot(win, w, frames, 16)
    half_mask = 0.5 * mask
    total, cross = None, None
    for frame in range(frames):
        p = pre_n[frame]
        e = back[272 * frame : 272 * frame + 256] * (half_mask * slope_half(p * scale_n + shift_n))
        out[frame] = e
        total = e if total is None else total + e
        cross = e * p if cross is None else cross + e * p
    add_stats(acc, i == 0, (0, 1), (col_sum(total), col_sum(cross)))
    send_stats(i == pl.num_programs(0) - 1, acc, stats)


def plane_weight(act, low, w_grad, w_acc, win, low_win):
    i = pl.program_id(0)
    frames = act.shape[0]

    @pl.when(i == 0)
    def _():
        w_acc[...] = jnp.zeros_like(w_acc)
        clear_gaps(win, frames, 16)
        low_win[...] = jnp.zeros_like(low_win)

    for frame in range(frames):
        fill_windows(win, act[frame].astype(F32), 16 + 272 * frame, 16)
        low_win[272 * frame : 272 * frame + 256, :] = low[frame]
    rows = low_win.shape[0]
    for tap in range(3):
        w_acc[tap] += dot_tn(win[16 * tap : 16 * tap + rows, :], low_win[...])

    @pl.when(i == pl.num_programs(0) - 1)
    def _():
        w_grad[...] = w_acc[...].astype(BF)


def join_back(
    count, side, grad, pre_n, gn, hn, params_n, w, joined, pre_l, gl, params_l, low, slow, out, stats, acc
):
    i = pl.program_id(0)
    steps = pl.num_programs(0)
    c = count[0, 0]
    frames = low.shape[0] - 2
    width = low.shape[2]
    mask = clip_mask(side[0], 256)

    @pl.when(i == 0)
    def _():
        mean_n, inv_n, _, _ = norm_terms(gn[...], params_n[...], c)
        a, b, d = back_terms(hn[...], params_n[...], c, mean_n, inv_n)
        low[0] = jnp.zeros((256, width), BF)
        low[frames + 1] = jnp.zeros((256, width), BF)
        for t in range(frames):
            low[t + 1] = (mask * (grad[t] * a + pre_n[t] * b + d)).astype(BF)

    _, _, scale_l, shift_l = norm_terms(gl[...], params_l[...], c)
    other = i + frames // 2
    j = jnp.concatenate([joined[0, 0], joined[1, 0]], axis=0).astype(F32)
    for tap in range(3):
        both = jnp.concatenate([low[i + 2 - tap], low[other + 2 - tap]], axis=0)
        j = j + dot_nt(both, w[tap])
    slow_width = j.shape[1] - out.shape[3]
    top = j[:, :slow_width].astype(BF)
    scatter_halves(top[0:256], top[256:512], slow)
    half_mask = 0.5 * mask
    total, cross = None, None
    for half in range(2):
        p = pre_l[half, 0]
        part = j[256 * half : 256 * half + 256, slow_width:]
        e = part * (half_mask * slope_half(p * scale_l + shift_l))
        out[half, 0] = e
        total = e if total is None else total + e
        cross = e * p if cross is None else cross + e * p
    add_stats(acc, i == 0, (0, 1), (col_sum(total), col_sum(cross)))
    send_stats(i == steps - 1, acc, stats)


def lateral_back(count, side, grad, pre_l, gl, hl, params_l, w, low, out):
    c = count[0, 0]
    frames = grad.shape[0]
    mean_l, inv_l, _, _ = norm_terms(gl[...], params_l[...], c)
    a, b, d = back_terms(hl[...], params_l[...], c, mean_l, inv_l)
    mask = clip_mask(side[0], 256)
    for t in range(frames):
        low[t] = (mask * (grad[t] * a + pre_l[t] * b + d)).astype(BF)
    for t in range(0, frames, 2):
        pair = jnp.concatenate([low[t], low[t + 1]], axis=0)
        last = t + 2 == frames
        after = jnp.zeros(low.shape[1:], BF) if last else low[t + 2]
        shifted = jnp.concatenate([low[t + 1], after], axis=0)
        results = (
            dot_nt(pair, w[2]),
            dot_nt(pair, w[3]),
            dot_nt(pair, w[4]) + dot_nt(shifted, w[0]),
            dot_nt(shifted, w[1]),
        )
        for k, result in enumerate(results):
            result = result.astype(BF)
            out[4 * t + k] = result[0:256]
            out[4 * t + 4 + k] = result[256:512]


def lateral_weight_back(fast, low, w_grad, w_acc):
    frames = low.shape[0]
    width = fast.shape[2]
    w_acc[...] = jnp.zeros_like(w_acc)
    for t in range(frames):
        taps = [k for k in range(5) if 0 <= 4 * t - 2 + k < 4 * frames]
        joined = jnp.concatenate([fast[4 * t - 2 + k] for k in taps], axis=1)
        w_acc[taps[0] * width : (taps[-1] + 1) * width, :] += dot_tn(joined, low[t])
    w_grad[...] = w_acc[...].astype(BF)


def weight_merge(core, *refs):
    out = refs[-1]
    count = (len(refs) - 1) // 2
    rows = out.shape[0]
    for half in range(2):

        @pl.when(core[0] == half)
        def _(half=half):
            begin = 0
            for mine, other in zip(refs[:count], refs[count : 2 * count]):
                end = begin + mine.shape[0]
                low, high = max(begin, half * rows), min(end, (half + 1) * rows)
                if low < high:
                    part = slice(low - begin, high - begin)
                    total = mine[part, :].astype(F32) + other[part, :].astype(F32)
                    out[low - half * rows : high - half * rows, :] = total.astype(BF)
                begin = end


def lateral_merge(place, mine, other, *outs):
    rows = outs[0].shape[0]
    near = len(outs)
    for step, out in enumerate(outs):
        begin = pl.multiple_of((place[0] * near + (place[1] ^ step)) * rows, 16)
        part = pl.ds(begin, rows)
        out[...] = (mine[part, :].astype(F32) + other[part, :].astype(F32)).astype(BF)


def weight_split(place, *refs):
    project, expand, spatial, time, lateral, full = refs[-6:]
    pieces = refs[:-6]
    near = 4
    share = lateral.shape[0] // len(pieces)
    rows = pieces[0].shape[0] - share
    for k, piece in enumerate(pieces):
        half = place[0] if k < near else 1 - place[0]
        if len(pieces) == near:
            half = 0
        spot = place[1] ^ (k % near)
        begin = pl.multiple_of((half * near + spot) * rows, 16)
        full[pl.ds(begin, rows), :] = piece[:rows, :]
        begin = pl.multiple_of((half * near + spot) * share, 8)
        lateral[pl.ds(begin, share), :] = piece[rows:, :].astype(F32)
    begin = 0
    for out in (project, expand):
        height, width = out.shape[0], full.shape[1]
        for block in range(out.shape[1] // width):
            out[:, block * width : (block + 1) * width] = full[begin : begin + height, :].astype(F32)
            begin += height
    spatial[...] = full[begin : begin + spatial.shape[0], :].astype(F32)
    begin += spatial.shape[0]
    height = project.shape[1]
    for tap in range(3):
        time[tap, :height] = full[begin : begin + height, :].astype(F32)
        begin += height
    rest = time.shape[1] - height
    for tap in range(3):
        time[tap, height:] = full[begin : begin + rest, :].astype(F32)
        begin += rest


def per_device(
    slow_in,
    fast_in,
    clip_side,
    fast_reduce,
    fast_spatial,
    fast_expand,
    lateral_weight,
    slow_reduce,
    slow_spatial,
    slow_expand,
    slow_project,
    fast_reduce_norm,
    fast_spatial_norm,
    fast_expand_norm,
    lateral_norm,
    slow_reduce_norm,
    slow_spatial_norm,
    slow_expand_norm,
    slow_project_norm,
    slow_cot,
    fast_cot,
):
    axes = ("dp", "wa")
    wa_count = lax.axis_size("wa")
    place = lax.axis_index("wa")
    devices = lax.axis_size("dp") * wa_count
    clips = fast_in.shape[0]
    cells = fast_in.shape[2] * fast_in.shape[3]
    frames = slow_in.shape[1]
    packs = clips // GROUPS
    c_f, b_f = fast_reduce.shape[1], fast_reduce.shape[2]
    c_l = lateral_weight.shape[2]
    b_s = slow_reduce.shape[2]
    c_s = slow_expand.shape[1]
    c_cat = slow_project.shape[0]
    half = frames // 2

    def exchange(array):
        return lax.all_to_all(array, "wa", 0, 0, tiled=True)

    def gather_stats(copies):
        return lax.all_to_all(copies, axes, 0, 0, tiled=True)

    def gather_wide(sums):
        dp_count = lax.axis_size("dp")
        if dp_count == 2:
            sums = sums + lax.ppermute(sums, "dp", [(0, 1), (1, 0)])
            copies = jnp.broadcast_to(sums[None], (wa_count,) + sums.shape)
            return lax.all_to_all(copies, "wa", 0, 0, tiled=True)
        return gather_stats(jnp.broadcast_to(sums[None], (devices,) + sums.shape))

    smem = scalars()

    area = jnp.sum(clip_side * clip_side)
    area_all = lax.psum(area, "dp").astype(F32)
    fast_count = (area_all * (fast_in.shape[1] * wa_count)).reshape(1, 1)
    slow_count = (area_all * frames).reshape(1, 1)
    own_side = lax.dynamic_slice_in_dim(clip_side, place, 1)
    lane_sides = jnp.repeat(clip_side.reshape(packs, GROUPS), LANES // GROUPS, axis=1)
    lane_sides = lane_sides.reshape(packs, 1, LANES)

    eye = jnp.eye(GROUPS, dtype=BF)
    w_first = jnp.einsum("kio,gh->kgiho", fast_reduce, eye).reshape(3, GROUPS, c_f, LANES)
    w_first_back = w_first.transpose(1, 2, 0, 3).reshape(GROUPS, c_f, 3 * LANES)
    w_plane = jnp.einsum("ijab,gh->ijgahb", fast_spatial, eye).reshape(3, 3 * LANES, LANES)
    flipped = fast_spatial[::-1, ::-1].transpose(0, 1, 3, 2)
    w_plane_back = jnp.einsum("ijab,gh->ijgahb", flipped, eye).reshape(3, 3 * LANES, LANES)
    w_widen = jnp.einsum("io,gh->ghio", fast_expand, eye).reshape(GROUPS, LANES, c_f)
    params1 = jnp.tile(fast_reduce_norm, (1, GROUPS))
    params2 = jnp.tile(fast_spatial_norm, (1, GROUPS))
    w_time_lateral = slow_reduce[:, c_s:].reshape(3 * c_l, b_s)
    w_middle = slow_spatial.reshape(3, 3 * b_s, b_s)
    w_middle_back = slow_spatial[::-1, ::-1].transpose(0, 1, 3, 2).reshape(3, 3 * b_s, b_s)

    spot = place.reshape(1)
    piece_shape = (half * cells, 2 * slow_in.shape[4])
    piece_spec = pl.BlockSpec((cells, piece_shape[1]), lambda i: (i, 0))
    flat_shape = (clips, frames * cells, slow_in.shape[4])

    def pack(array):
        flat = array.reshape(flat_shape)
        out = (piece_shape, BF, pl.BlockSpec(piece_shape, lambda *_: (0, 0)))
        return launch(pack_kernel, "pack", (), [(spot, smem), (flat, whole(flat))], [out] * wa_count)

    def exchange_pieces(pieces, begin=0, end=wa_count):
        return [
            lax.ppermute(pieces[step], "wa", [(i, i ^ step) for i in range(wa_count)])
            if step
            else pieces[0]
            for step in range(begin, end)
        ]

    def gate(arrays, ready):
        return list(launch(lambda: None, "gate", (), [], [], after=(ready,), carry=tuple(arrays)))

    def unpack(pieces):
        (flat,) = launch(
            unpack_pieces,
            "unpack",
            (),
            [(spot, smem)] + [(piece, whole(piece)) for piece in pieces],
            [(flat_shape, BF, pl.BlockSpec(flat_shape, lambda *_: (0, 0, 0)))],
        )
        return flat.reshape(slow_in.shape)

    slow_pieces = exchange_pieces(pack(slow_in))
    cot_out = pack(slow_cot)

    x = fast_in.reshape(clips, 2, cells, c_f)
    x_spec = pl.BlockSpec((GROUPS, 2, cells, c_f), lambda i: (i, 0, 0, 0))
    packed_shape = (packs, 2, cells, LANES)
    packed_spec = pl.BlockSpec((1, 2, cells, LANES), lambda i: (i, 0, 0, 0))
    rim_shape = (packs, cells, LANES)
    rim_spec = pl.BlockSpec((1, cells, LANES), lambda i: (i, 0, 0))
    sides_spec = pl.BlockSpec((1, 1, LANES), lambda i: (i, 0, 0))
    stat8 = ((devices, 8, LANES), F32, pl.BlockSpec((devices, 8, LANES), lambda *_: (0, 0, 0)))
    acc8 = pltpu.VMEM((8, LANES), F32)
    fast_win = window_shape(2, 3 * LANES)
    fast_low = pltpu.VMEM((528, LANES), BF)

    y, to_next, to_prev = launch(
        fast_first,
        "fast_first",
        (packs,),
        [(x, x_spec), (w_first, whole(w_first))],
        [(packed_shape, F32, packed_spec), (rim_shape, BF, rim_spec), (rim_shape, BF, rim_spec)],
    )
    forward = [(i, i + 1) for i in range(wa_count - 1)]
    backward = [(i + 1, i) for i in range(wa_count - 1)]
    from_prev = lax.ppermute(to_next, "wa", forward)
    from_next = lax.ppermute(to_prev, "wa", backward)
    pre1, s1 = launch(
        fast_join,
        "fast_join",
        (packs,),
        [(y, packed_spec), (from_prev, rim_spec), (from_next, rim_spec), (lane_sides, sides_spec)],
        [(packed_shape, F32, packed_spec), stat8],
        [acc8],
        after=tuple(slow_pieces[1:4]),
    )
    g1 = gather_stats(s1)
    act1, pre2, s2 = launch(
        fast_plane,
        "fast_plane",
        (packs,),
        [
            (fast_count, smem),
            (pre1, packed_spec),
            (g1, whole(g1)),
            (params1, whole(params1)),
            (lane_sides, sides_spec),
            (w_plane, whole(w_plane)),
        ],
        [(packed_shape, BF, packed_spec), (packed_shape, F32, packed_spec), stat8],
        [acc8, fast_win],
        after=tuple(slow_pieces[4:8]),
    )
    g2 = gather_stats(s2)
    act2, s3 = launch(
        fast_widen,
        "fast_widen",
        (packs,),
        [
            (fast_count, smem),
            (pre2, packed_spec),
            (g2, whole(g2)),
            (params2, whole(params2)),
            (lane_sides, sides_spec),
            (w_widen, whole(w_widen)),
        ],
        [(packed_shape, BF, packed_spec), stat8],
        [acc8],
        after=tuple(slow_pieces[8:12]),
    )
    g3 = gather_stats(s3)
    (fast_result,) = launch(
        fast_out,
        "fast_out",
        (packs,),
        [
            (fast_count, smem),
            (clip_side, smem),
            (x, x_spec),
            (act2, packed_spec),
            (g3, whole(g3)),
            (fast_expand_norm, whole(fast_expand_norm)),
            (w_widen, whole(w_widen)),
        ],
        [(x.shape, BF, x_spec)],
        after=tuple(slow_pieces[12:]),
    )

    fast_got = exchange(fast_result.reshape(clips, 2 * cells, c_f)).reshape(4 * frames, cells, c_f)

    def stat(rows, width):
        return ((devices, rows, width), F32, pl.BlockSpec((devices, rows, width), lambda *_: (0, 0, 0)))

    def pair_spec(width):
        return pl.BlockSpec((2, 1, cells, width), lambda i: (0, i, 0, 0))

    def frame_spec(width, count):
        return pl.BlockSpec((count, cells, width), lambda i: (i, 0, 0))

    def pairs(array):
        return array.reshape((2, half) + array.shape[1:])

    own, base_n, base_p = launch(
        slow_enter,
        "slow_enter",
        (half,),
        [(spot, smem), (slow_reduce, whole(slow_reduce)), (slow_project, whole(slow_project))]
        + [(piece, piece_spec) for piece in slow_pieces],
        [
            ((2, half, cells, c_s), BF, pair_spec(c_s)),
            (
                (frames + 2, cells, b_s),
                F32,
                pl.BlockSpec((frames + 2, cells, b_s), lambda *_: (0, 0, 0)),
            ),
            ((2, half, cells, c_s), BF, pair_spec(c_s)),
        ],
        [pltpu.VMEM((wa_count, cells, LANES), BF)],
        flops=2 * frames * cells * c_s * (3 * b_s + c_s),
    )
    own = own.reshape(frames, cells, c_s)
    base_p = base_p.reshape(frames, cells, c_s)
    pre_l, s_l = launch(
        lateral_enter,
        "lateral_enter",
        (),
        [(own_side, smem), (fast_got, whole(fast_got)), (lateral_weight, whole(lateral_weight))],
        [
            ((frames, cells, c_l), F32, pl.BlockSpec((frames, cells, c_l), lambda *_: (0, 0, 0))),
            stat(2, c_l),
        ],
        [pltpu.VMEM((2, c_l), F32)],
        after=(base_n,),
    )
    g_l = gather_stats(s_l)
    cot_pieces = exchange_pieces(gate(cot_out, g_l))

    lateral_act, pre_n, s_n = launch(
        narrow_enter,
        "narrow_enter",
        (),
        [
            (slow_count, smem),
            (own_side, smem),
            (pre_l, whole(pre_l)),
            (g_l, whole(g_l)),
            (lateral_norm, whole(lateral_norm)),
            (base_n, whole(base_n)),
            (w_time_lateral, whole(w_time_lateral)),
        ],
        [
            ((frames, cells, c_l), BF, pl.BlockSpec((frames, cells, c_l), lambda *_: (0, 0, 0))),
            ((frames, cells, b_s), F32, pl.BlockSpec((frames, cells, b_s), lambda *_: (0, 0, 0))),
            stat(2, b_s),
        ],
        [pltpu.VMEM((2, b_s), F32)],
    )
    g_n = gather_stats(s_n)
    slow_win = window_shape(4, 3 * b_s)
    slow_low = pltpu.VMEM((4 * 272 - 16, b_s), BF)
    act_n, pre_m, s_m = launch(
        middle_enter,
        "middle_enter",
        (frames // 4,),
        [
            (slow_count, smem),
            (own_side, smem),
            (pre_n, frame_spec(b_s, 4)),
            (g_n, whole(g_n)),
            (slow_reduce_norm, whole(slow_reduce_norm)),
            (w_middle, whole(w_middle)),
        ],
        [
            ((frames, cells, b_s), BF, frame_spec(b_s, 4)),
            ((frames, cells, b_s), F32, frame_spec(b_s, 4)),
            stat(2, b_s),
        ],
        [pltpu.VMEM((2, b_s), F32), slow_win],
        after=tuple(cot_pieces[1:5]),
    )
    g_m = gather_stats(s_m)
    act_m, project, s_w = launch(
        wide_enter,
        "wide_enter",
        (frames // 2,),
        [
            (slow_count, smem),
            (own_side, smem),
            (pre_m, frame_spec(b_s, 2)),
            (g_m, whole(g_m)),
            (slow_spatial_norm, whole(slow_spatial_norm)),
            (base_p, frame_spec(c_s, 2)),
            (lateral_act, frame_spec(c_l, 2)),
            (slow_expand, whole(slow_expand)),
            (slow_project, pl.BlockSpec((c_l, c_s), lambda i: (c_s // c_l, 0))),
        ],
        [
            ((frames, cells, b_s), BF, frame_spec(b_s, 2)),
            ((frames, cells, c_s), BF, frame_spec(c_s, 2)),
            ((4, c_s), F32, pl.BlockSpec((4, c_s), lambda *_: (0, 0))),
        ],
        after=tuple(cot_pieces[5:10]),
    )
    g_w = gather_wide(s_w)
    *out_pieces, wide_grad, t_w = launch(
        wide_out,
        "wide_out",
        (half,),
        [
            (slow_count, smem),
            (own_side, smem),
            (spot, smem),
            (pairs(act_m), pair_spec(b_s)),
            (pairs(project), pair_spec(c_s)),
            (g_w, whole(g_w)),
            (slow_expand_norm, whole(slow_expand_norm)),
            (slow_project_norm, whole(slow_project_norm)),
            (slow_expand, whole(slow_expand)),
            *[(piece, piece_spec) for piece in cot_pieces],
        ],
        [
            *[(piece_shape, BF, piece_spec)] * wa_count,
            ((2, half, cells, c_s), F32, pair_spec(c_s)),
            ((4, c_s), F32, pl.BlockSpec((4, c_s), lambda *_: (0, 0))),
        ],
        [pltpu.VMEM((wa_count, cells, LANES), BF)],
    )
    wide_grad = wide_grad.reshape(frames, cells, c_s)
    h_w = gather_wide(t_w)
    result_pieces = exchange_pieces(out_pieces)
    slow_result = unpack(result_pieces)

    middle_grad, expand_w_grad, t_m = launch(
        middle_back,
        "middle_back",
        (frames // 2,),
        [
            (slow_count, smem),
            (own_side, smem),
            (wide_grad, frame_spec(c_s, 2)),
            (act_m, frame_spec(b_s, 2)),
            (g_w, whole(g_w)),
            (h_w, whole(h_w)),
            (slow_expand_norm, whole(slow_expand_norm)),
            (slow_expand, whole(slow_expand)),
            (pre_m, frame_spec(b_s, 2)),
            (g_m, whole(g_m)),
            (slow_spatial_norm, whole(slow_spatial_norm)),
        ],
        [
            ((frames, cells, b_s), F32, frame_spec(b_s, 2)),
            ((c_s, b_s), BF, pl.BlockSpec((c_s, b_s), lambda *_: (0, 0))),
            stat(2, b_s),
        ],
        [pltpu.VMEM((2, b_s), F32), pltpu.VMEM((b_s, c_s), F32)],
        after=tuple(result_pieces[1:3]),
    )
    h_m = gather_stats(t_m)
    joined_part, project_w_grad = launch(
        project_back,
        "project_back",
        (frames // 2,),
        [
            (slow_count, smem),
            (own_side, smem),
            (wide_grad, frame_spec(c_s, 2)),
            (project, frame_spec(c_s, 2)),
            (g_w, whole(g_w)),
            (h_w, whole(h_w)),
            (slow_project_norm, whole(slow_project_norm)),
            (own, frame_spec(c_s, 2)),
            (lateral_act, frame_spec(c_l, 2)),
            (slow_project, whole(slow_project)),
        ],
        [
            ((frames, cells, c_cat), BF, frame_spec(c_cat, 2)),
            ((c_cat * c_s // b_s, b_s), BF, pl.BlockSpec((c_cat * c_s // b_s, b_s), lambda *_: (0, 0))),
        ],
        [pltpu.VMEM((c_cat, c_s), F32)],
        flops=4 * frames * cells * c_cat * c_s,
    )
    middle_low, narrow_grad, t_n = launch(
        narrow_back,
        "narrow_back",
        (frames // 4,),
        [
            (slow_count, smem),
            (own_side, smem),
            (middle_grad, frame_spec(b_s, 4)),
            (pre_m, frame_spec(b_s, 4)),
            (g_m, whole(g_m)),
            (h_m, whole(h_m)),
            (slow_spatial_norm, whole(slow_spatial_norm)),
            (w_middle_back, whole(w_middle_back)),
            (pre_n, frame_spec(b_s, 4)),
            (g_n, whole(g_n)),
            (slow_reduce_norm, whole(slow_reduce_norm)),
        ],
        [
            ((frames, cells, b_s), BF, frame_spec(b_s, 4)),
            ((frames, cells, b_s), F32, frame_spec(b_s, 4)),
            stat(2, b_s),
        ],
        [pltpu.VMEM((2, b_s), F32), slow_win],
        after=tuple(result_pieces[3:7]),
    )
    h_n = gather_stats(t_n)
    (spatial_w_grad,) = launch(
        plane_weight,
        "plane_weight",
        (frames // 4,),
        [(act_n, frame_spec(b_s, 4)), (middle_low, frame_spec(b_s, 4))],
        [((3, 3 * b_s, b_s), BF, pl.BlockSpec((3, 3 * b_s, b_s), lambda *_: (0, 0, 0)))],
        [pltpu.VMEM((3, 3 * b_s, b_s), F32), slow_win, slow_low],
        flops=18 * frames * cells * b_s * b_s,
    )
    narrow_low, grad_packed, lateral_grad, t_l = launch(
        join_back,
        "join_back",
        (half,),
        [
            (slow_count, smem),
            (own_side, smem),
            (narrow_grad, whole(narrow_grad)),
            (pre_n, whole(pre_n)),
            (g_n, whole(g_n)),
            (h_n, whole(h_n)),
            (slow_reduce_norm, whole(slow_reduce_norm)),
            (slow_reduce, whole(slow_reduce)),
            (pairs(joined_part), pair_spec(c_cat)),
            (pairs(pre_l), pair_spec(c_l)),
            (g_l, whole(g_l)),
            (lateral_norm, whole(lateral_norm)),
        ],
        [
            (
                (frames + 2, cells, b_s),
                BF,
                pl.BlockSpec((frames + 2, cells, b_s), lambda *_: (0, 0, 0)),
            ),
            (
                (wa_count,) + piece_shape,
                BF,
                pl.BlockSpec((wa_count, cells, piece_shape[1]), lambda i: (0, i, 0)),
            ),
            ((2, half, cells, c_l), F32, pair_spec(c_l)),
            stat(2, c_l),
        ],
        [pltpu.VMEM((2, c_l), F32)],
        after=tuple(result_pieces[7:13]),
    )
    lateral_grad = lateral_grad.reshape(frames, cells, c_l)
    h_l = gather_stats(t_l)
    grad_got = exchange(grad_packed)
    slow_grad = unpack([grad_got])

    def time_weight(values):
        flat = values.reshape(frames * cells, values.shape[2])
        low = narrow_low.reshape((frames + 2) * cells, b_s)
        parts = []
        for tap in range(3):
            begin = (2 - tap) * cells
            parts.append(
                lax.dot_general(
                    flat,
                    lax.slice_in_dim(low, begin, begin + frames * cells, 1, 0),
                    (((0,), (0,)), ((), ())),
                    preferred_element_type=F32,
                )
            )
        return jnp.stack(parts).astype(BF)

    lateral_low, frames_back = launch(
        lateral_back,
        "lateral_back",
        (),
        [
            (slow_count, smem),
            (own_side, smem),
            (lateral_grad, whole(lateral_grad)),
            (pre_l, whole(pre_l)),
            (g_l, whole(g_l)),
            (h_l, whole(h_l)),
            (lateral_norm, whole(lateral_norm)),
            (lateral_weight, whole(lateral_weight)),
        ],
        [
            ((frames, cells, c_l), BF, pl.BlockSpec((frames, cells, c_l), lambda *_: (0, 0, 0))),
            ((4 * frames, cells, c_f), BF, pl.BlockSpec((4 * frames, cells, c_f), lambda *_: (0, 0, 0))),
        ],
        after=tuple(result_pieces[13:]),
    )
    back_got = exchange(frames_back.reshape(wa_count, 2 * cells, c_f)).reshape(x.shape)
    (lateral_w_grad,) = launch(
        lateral_weight_back,
        "lateral_weight_back",
        (),
        [(fast_got, whole(fast_got)), (lateral_low, whole(lateral_low))],
        [((5 * c_f, c_l), BF, pl.BlockSpec((5 * c_f, c_l), lambda *_: (0, 0)))],
        [pltpu.VMEM((5 * c_f, c_l), F32)],
    )

    weight_parts = [
        part.reshape(-1, b_s)
        for part in (
            project_w_grad,
            expand_w_grad,
            spatial_w_grad,
            time_weight(own),
            time_weight(lateral_act),
        )
    ]
    sizes = [part.shape[0] for part in weight_parts]
    near = 4
    inner = [[near * k + j for j in range(near)] for k in range(wa_count // near)]
    outer = [[near * k + j for k in range(wa_count // near)] for j in range(near)]
    dp_count = lax.axis_size("dp")
    core = lax.axis_index("dp")
    swap = [(0, 1), (1, 0)]
    paired = dp_count == 2
    if paired:
        others = [lax.ppermute(part, "dp", swap) for part in weight_parts]
        rows = sum(sizes) // 2
        place_core = core.reshape(1)
        (weights,) = launch(
            weight_merge,
            "weight_merge",
            (),
            [(place_core, smem)] + [(part, whole(part)) for part in weight_parts + others],
            [((rows, b_s), BF, pl.BlockSpec((rows, b_s), lambda *_: (0, 0)))],
        )
    else:
        weights = jnp.concatenate(weight_parts, axis=0)
    first_stage = lax.psum_scatter(weights, "wa", axis_index_groups=inner, tiled=True)
    spot_in = place % near
    if paired:
        other = lax.ppermute(lateral_w_grad, "dp", swap)
        share = lateral_w_grad.shape[0] // (2 * near)
        out = ((share, c_l), BF, pl.BlockSpec((share, c_l), lambda *_: (0, 0)))
        lateral_out = launch(
            lateral_merge,
            "lateral_merge",
            (),
            [(jnp.stack([core, spot_in]), smem)]
            + [(part, whole(part)) for part in (lateral_w_grad, other)],
            [out] * near,
        )
    else:
        share = lateral_w_grad.shape[0] // near
        lateral_out = [
            lax.dynamic_slice_in_dim(lateral_w_grad, (spot_in ^ step) * share, share)
            for step in range(near)
        ]
    lateral_sum = lateral_out[0].astype(F32)
    for step in range(1, near):
        got = lax.ppermute(lateral_out[step], "wa", [(i, i ^ step) for i in range(wa_count)])
        lateral_sum = lateral_sum + got.astype(F32)
    second_stage = lax.psum(
        jnp.concatenate([first_stage, lateral_sum.astype(BF)], axis=0),
        "wa",
        axis_index_groups=outer,
    )

    cot = fast_cot.reshape(x.shape)
    fast_grad3, t3 = launch(
        fast_back_sum,
        "fast_back_sum",
        (packs,),
        [
            (fast_count, smem),
            (clip_side, smem),
            (cot, x_spec),
            (back_got, x_spec),
            (x, x_spec),
            (act2, packed_spec),
            (g3, whole(g3)),
            (fast_expand_norm, whole(fast_expand_norm)),
            (w_widen, whole(w_widen)),
        ],
        [(x.shape, F32, x_spec), stat8],
        [acc8],
    )
    h3 = gather_stats(t3)
    fast_grad2, widen_blocks, t2 = launch(
        fast_back_widen,
        "fast_back_widen",
        (packs,),
        [
            (fast_count, smem),
            (clip_side, smem),
            (fast_grad3, x_spec),
            (act2, packed_spec),
            (g3, whole(g3)),
            (h3, whole(h3)),
            (fast_expand_norm, whole(fast_expand_norm)),
            (w_widen, whole(w_widen)),
            (pre2, packed_spec),
            (g2, whole(g2)),
            (params2, whole(params2)),
            (lane_sides, sides_spec),
        ],
        [
            (packed_shape, F32, packed_spec),
            ((GROUPS, LANES, c_f), F32, pl.BlockSpec((GROUPS, LANES, c_f), lambda *_: (0, 0, 0))),
            stat8,
        ],
        [acc8],
        after=(second_stage,),
    )
    h2 = gather_stats(t2)
    pieces = [second_stage] + [
        lax.ppermute(second_stage, "wa", [(i, i ^ step) for i in range(wa_count)])
        for step in range(1, near)
    ]
    fast_grad1, plane_blocks, t1 = launch(
        fast_back_plane,
        "fast_back_plane",
        (packs,),
        [
            (fast_count, smem),
            (fast_grad2, packed_spec),
            (pre2, packed_spec),
            (g2, whole(g2)),
            (h2, whole(h2)),
            (params2, whole(params2)),
            (act1, packed_spec),
            (pre1, packed_spec),
            (g1, whole(g1)),
            (params1, whole(params1)),
            (lane_sides, sides_spec),
            (w_plane_back, whole(w_plane_back)),
        ],
        [
            (packed_shape, F32, packed_spec),
            (
                (3, 3 * LANES, LANES),
                F32,
                pl.BlockSpec((3, 3 * LANES, LANES), lambda *_: (0, 0, 0)),
            ),
            stat8,
        ],
        [acc8, fast_win, fast_low],
        after=tuple(pieces),
    )
    h1 = gather_stats(t1)
    (low1,) = launch(
        fast_back_first,
        "fast_back_first",
        (packs,),
        [
            (fast_count, smem),
            (fast_grad1, packed_spec),
            (pre1, packed_spec),
            (g1, whole(g1)),
            (h1, whole(h1)),
            (params1, whole(params1)),
            (lane_sides, sides_spec),
        ],
        [((2, packs, cells, LANES), BF, pl.BlockSpec((2, 1, cells, LANES), lambda i: (0, i, 0, 0)))],
    )
    low_prev = lax.ppermute(low1[1], "wa", forward)
    low_next = lax.ppermute(low1[0], "wa", backward)
    fast_grad, first_blocks = launch(
        fast_back_out,
        "fast_back_out",
        (packs,),
        [
            (fast_grad3, x_spec),
            (low1, pl.BlockSpec((2, 1, cells, LANES), lambda i: (0, i, 0, 0))),
            (low_prev, rim_spec),
            (low_next, rim_spec),
            (x, x_spec),
            (w_first_back, whole(w_first_back)),
        ],
        [
            (x.shape, BF, x_spec),
            (
                (GROUPS, c_f, 3 * LANES),
                F32,
                pl.BlockSpec((GROUPS, c_f, 3 * LANES), lambda *_: (0, 0, 0)),
            ),
        ],
        after=(grad_got,),
    )
    expand_part = sum(widen_blocks[g, g * b_f : (g + 1) * b_f] for g in range(GROUPS))
    plane_view = plane_blocks.reshape(3, 3, GROUPS, b_f, GROUPS, b_f)
    spatial_part = sum(plane_view[:, :, g, :, g] for g in range(GROUPS))
    first_view = first_blocks.reshape(GROUPS, c_f, 3, GROUPS, b_f)
    reduce_part = sum(first_view[g, :, :, g] for g in range(GROUPS)).transpose(1, 0, 2)

    small = jnp.concatenate(
        [reduce_part.reshape(-1), spatial_part.reshape(-1), expand_part.reshape(-1)]
    )
    share = -(-small.shape[0] // (devices * LANES)) * LANES
    padded = jnp.pad(small, (0, share * devices - small.shape[0])).reshape(devices, share // LANES, LANES)
    mine = jnp.sum(gather_stats(padded), axis=0)
    small_all = gather_stats(jnp.broadcast_to(mine[None], padded.shape)).reshape(-1)
    if paired:
        pieces = pieces + [lax.ppermute(piece, "dp", swap) for piece in pieces]
    else:
        pieces = [lax.psum(piece, "dp") for piece in pieces]
    final = [
        ((c_cat, c_s), F32),
        ((b_s, c_s), F32),
        ((9 * b_s, b_s), F32),
        ((3, c_cat, b_s), F32),
        ((5 * c_f, c_l), F32),
    ]
    project_all, expand_all, spatial_all, time_all, lateral_all = launch(
        weight_split,
        "weight_split",
        (),
        [(jnp.stack([core, place % near]), smem)] + [(piece, whole(piece)) for piece in pieces],
        [
            (shape, dtype, pl.BlockSpec(shape, lambda *_, rank=len(shape): (0,) * rank))
            for shape, dtype in final
        ],
        [pltpu.VMEM((sum(sizes), b_s), BF)],
    )
    first_size, plane_size = reduce_part.size, spatial_part.size
    fast_reduce_grad = small_all[:first_size].reshape(fast_reduce.shape)
    fast_spatial_grad = small_all[first_size : first_size + plane_size].reshape(fast_spatial.shape)
    fast_expand_grad = small_all[first_size + plane_size : small.shape[0]].reshape(fast_expand.shape)

    def norm_grad(sums, moments, count, folded=False):
        total, moment = jnp.sum(sums, axis=0), jnp.sum(moments, axis=0)
        if folded:
            total = total.reshape(total.shape[0], GROUPS, -1).sum(axis=1)
            moment = moment.reshape(moment.shape[0], GROUPS, -1).sum(axis=1)
        mean = moment[0] / count[0, 0]
        inv = lax.rsqrt(moment[1] / count[0, 0] - mean * mean + EPSILON)
        return jnp.stack([(total[1] - mean * total[0]) * inv, total[0]])

    h_project = jnp.concatenate([h_w[:, 0:1], h_w[:, 2:3]], axis=1)
    return (
        slow_result,
        fast_result.reshape(fast_in.shape),
        slow_grad,
        fast_grad.reshape(fast_in.shape),
        fast_reduce_grad,
        fast_spatial_grad,
        fast_expand_grad,
        lateral_all.reshape(lateral_weight.shape),
        time_all,
        spatial_all.reshape(slow_spatial.shape),
        expand_all,
        project_all,
        norm_grad(h1, g1, fast_count, True),
        norm_grad(h2, g2, fast_count, True),
        norm_grad(h3, g3, fast_count),
        norm_grad(h_l, g_l, slow_count),
        norm_grad(h_n, g_n, slow_count),
        norm_grad(h_m, g_m, slow_count),
        norm_grad(h_w[:, 0:2], g_w[:, 0:2], slow_count),
        norm_grad(h_project, g_w[:, 2:4], slow_count),
    )


def solution(mesh):
    wide = P("dp", None, None, None, "wa")
    fast = P("dp", "wa", None, None, None)
    same = P()
    return jax.shard_map(
        per_device,
        mesh=mesh,
        in_specs=(wide, fast, P("dp")) + (same,) * 16 + (wide, fast),
        out_specs=(wide, fast, wide, fast) + (same,) * 16,
        check_vma=False,
    )
```

```python
import functools

import jax
import jax.numpy as jnp
from jax import lax
from jax.experimental import pallas as pl
from jax.experimental.pallas import tpu as pltpu
from jax.sharding import PartitionSpec as P

EPSILON = 1e-05
BF = jnp.bfloat16
F32 = jnp.float32
LANES = 128
GROUPS = 4
VMEM_BYTES = 52 * 1024 * 1024
CUT_SLOW = (3, 7, 11, 15)
CUT_COT = (0, 4, 10)
CUT_RESULT = (0, 3, 9)
GATE_COT = 8
GATE_RESULT = 5


def whole(array):
    rank = len(array.shape)
    return pl.BlockSpec(array.shape, lambda *_: (0,) * rank)


def scalars():
    return pl.BlockSpec(memory_space=pltpu.SMEM)


def launch(body, name, grid, inputs, outputs, scratch=(), flops=0, after=(), carry=()):
    used, given = len(inputs), len(outputs)
    held = pl.BlockSpec(memory_space=pl.ANY)
    inputs = inputs + [(array, held) for array in (*after, *carry)]
    outputs = outputs + [(array.shape, array.dtype, held) for array in carry]
    first = used + len(after)
    aliases = {first + k: given + k for k in range(len(carry))}

    def kernel(*refs):
        outs = refs[len(inputs) :]
        body(*refs[:used], *outs[:given], *outs[len(outputs) :])

    traffic = sum(a.size * a.dtype.itemsize for a, _ in inputs)
    for shape, dtype, _ in outputs:
        count = 1
        for entry in shape:
            count *= entry
        traffic += count * jnp.dtype(dtype).itemsize
    return pl.pallas_call(
        kernel,
        name=name,
        grid=grid,
        in_specs=[spec for _, spec in inputs],
        out_specs=[spec for _, _, spec in outputs],
        out_shape=[jax.ShapeDtypeStruct(shape, dtype) for shape, dtype, _ in outputs],
        scratch_shapes=list(scratch),
        input_output_aliases=aliases,
        compiler_params=pltpu.CompilerParams(vmem_limit_bytes=VMEM_BYTES),
        cost_estimate=pl.CostEstimate(flops=flops, bytes_accessed=traffic, transcendentals=0),
    )(*[array for array, _ in inputs])


def dot(a, b):
    return lax.dot_general(a, b, (((1,), (0,)), ((), ())), preferred_element_type=F32)


def dot_nt(a, b):
    return lax.dot_general(a, b, (((1,), (1,)), ((), ())), preferred_element_type=F32)


def dot_tn(a, b):
    return lax.dot_general(a, b, (((0,), (0,)), ((), ())), preferred_element_type=F32)


def silu_half(v):
    return v * (1.0 + jnp.tanh(v))


def slope_half(v):
    h = 1.0 + jnp.tanh(v)
    return h + v * h * (2.0 - h)


def cell_ids(rows):
    ids = lax.broadcasted_iota(jnp.int32, (rows, 1), 0)
    return (ids >> 4) & 15, ids & 15


def clip_mask(side, rows):
    h, w = cell_ids(rows)
    return jnp.where((h < side) & (w < side), 1.0, 0.0).astype(F32)


def packed_mask(side_row, rows):
    ids = lax.broadcasted_iota(jnp.int32, (rows, LANES), 0)
    h, w = (ids >> 4) & 15, ids & 15
    return jnp.where((h < side_row) & (w < side_row), 1.0, 0.0).astype(F32)


def fold(row):
    width = LANES // GROUPS
    out = row
    for step in range(1, GROUPS):
        out = out + pltpu.roll(row, step * width, 1)
    return out


def norm_terms(gathered, params, count, folded=False):
    total = jnp.sum(gathered, axis=0)
    if folded:
        total = fold(total)
    mean = total[0:1] / count
    variance = total[1:2] / count - mean * mean
    inv = lax.rsqrt(variance + EPSILON)
    scale = 0.5 * params[0:1] * inv
    return mean, inv, scale, 0.5 * params[1:2] - mean * scale


def back_terms(gathered, params, count, mean, inv, folded=False):
    total = jnp.sum(gathered, axis=0)
    if folded:
        total = fold(total)
    a = params[0:1] * inv
    b = -a * inv * inv * (total[1:2] - mean * total[0:1]) / count
    return a, b, -a * total[0:1] / count - b * mean


def col_sum(v):
    return jnp.sum(v, axis=0, keepdims=True)


def add_stats(acc, first, rows, values):
    @pl.when(first)
    def _():
        acc[...] = jnp.zeros_like(acc)

    for row, value in zip(rows, values):
        acc[row : row + 1, :] += value


def send_stats(last, acc, out):
    @pl.when(last)
    def _():
        out[...] = jnp.broadcast_to(acc[...][None], out.shape)


def put_columns(wide, out):
    rows, width = wide.shape[0], out.shape[1]
    for block in range(wide.shape[1] // width):
        out[block * rows : (block + 1) * rows, :] = wide[:, block * width : (block + 1) * width].astype(BF)


def fill_windows(scratch, values, first, cells):
    rows = values.shape[0]
    w = lax.broadcasted_iota(jnp.int32, (rows, 1), 0) & (cells - 1)
    left = jnp.where(w == 0, 0.0, pltpu.roll(values, 1, 0))
    right = jnp.where(w == cells - 1, 0.0, pltpu.roll(values, rows - 1, 0))
    scratch[first : first + rows, :] = jnp.concatenate(
        [left.astype(BF), values.astype(BF), right.astype(BF)], axis=1
    )


def clear_gaps(scratch, frames, cells):
    pitch = cells * (cells + 1)
    for frame in range(frames + 1):
        scratch[frame * pitch : frame * pitch + cells, :] = jnp.zeros((cells, scratch.shape[1]), BF)


def plane_dot(scratch, weight, frames, cells):
    rows = frames * cells * (cells + 1) - cells
    out = dot(scratch[0:rows, :], weight[0])
    for tap in (1, 2):
        out = out + dot(scratch[tap * cells : tap * cells + rows, :], weight[tap])
    return out


def window_shape(frames, width):
    return pltpu.VMEM((frames * 272 + 16, width), BF)


def fast_first(x, w, y, to_next, to_prev):
    def over(frame, tap):
        out = dot(x[0, frame], w[tap, 0])
        for g in range(1, GROUPS):
            out = out + dot(x[g, frame], w[tap, g])
        return out

    y[0, 0] = over(0, 1) + over(1, 2)
    y[0, 1] = over(0, 0) + over(1, 1)
    to_next[0] = over(1, 0).astype(BF)
    to_prev[0] = over(0, 2).astype(BF)


def fast_join(y, from_prev, from_next, sides, pre, stats, acc):
    i = pl.program_id(0)
    mask = packed_mask(sides[0], 256)
    first = y[0, 0] + from_prev[0].astype(F32)
    second = y[0, 1] + from_next[0].astype(F32)
    pre[0, 0] = first
    pre[0, 1] = second
    m1, m2 = first * mask, second * mask
    add_stats(acc, i == 0, (0, 1), (col_sum(m1 + m2), col_sum(m1 * first + m2 * second)))
    send_stats(i == pl.num_programs(0) - 1, acc, stats)


def fast_plane(count, pre, g1, params, sides, w, act, out, stats, acc, win):
    i = pl.program_id(0)
    _, _, scale, shift = norm_terms(g1[...], params[...], count[0, 0], True)
    mask = packed_mask(sides[0], 256)

    @pl.when(i == 0)
    def _():
        clear_gaps(win, 2, 16)

    for frame in range(2):
        a = mask * silu_half(pre[0, frame] * scale + shift)
        act[0, frame] = a.astype(BF)
        fill_windows(win, a, 16 + 272 * frame, 16)
    both = plane_dot(win, w, 2, 16)
    v0, v1 = both[0:256], both[272:528]
    out[0, 0] = v0
    out[0, 1] = v1
    m0, m1 = mask * v0, mask * v1
    add_stats(acc, i == 0, (0, 1), (col_sum(m0 + m1), col_sum(m0 * v0 + m1 * v1)))
    send_stats(i == pl.num_programs(0) - 1, acc, stats)


def fast_widen(count, pre, g2, params, sides, w, act, stats, acc):
    i = pl.program_id(0)
    _, _, scale, shift = norm_terms(g2[...], params[...], count[0, 0], True)
    mask = packed_mask(sides[0], 512)
    a = (mask * silu_half(pre[0].reshape(512, LANES) * scale + shift)).astype(BF)
    act[0] = a.reshape(2, 256, LANES)
    total, square = None, None
    for g in range(GROUPS):
        v = dot(a, w[g])
        total = v if total is None else total + v
        square = v * v if square is None else square + v * v
    add_stats(acc, i == 0, (0, 1), (col_sum(total), col_sum(square)))
    send_stats(i == pl.num_programs(0) - 1, acc, stats)


def fast_out(count, sides, x, act, g3, params, w, result):
    i = pl.program_id(0)
    _, _, scale, shift = norm_terms(g3[...], params[...], count[0, 0])
    a = act[0].reshape(512, LANES)
    for g in range(GROUPS):
        mask = clip_mask(sides[i * GROUPS + g], 512)
        v = 0.5 * x[g].reshape(512, LANES).astype(F32) + (dot(a, w[g]) * scale + shift)
        result[g] = (mask * silu_half(v)).astype(BF).reshape(2, 256, LANES)


def fast_back_sum(count, sides, cot, back, x, act, g3, params, w, grad, stats, acc):
    i = pl.program_id(0)
    _, _, scale, shift = norm_terms(g3[...], params[...], count[0, 0])
    a = act[0].reshape(512, LANES)
    total, cross = None, None
    for g in range(GROUPS):
        mask = 0.5 * clip_mask(sides[i * GROUPS + g], 512)
        v = dot(a, w[g])
        u = 0.5 * x[g].reshape(512, LANES).astype(F32) + (v * scale + shift)
        given = cot[g].reshape(512, LANES).astype(F32) + back[g].reshape(512, LANES).astype(F32)
        e = given * (mask * slope_half(u))
        grad[g] = e.reshape(2, 256, LANES)
        total = e if total is None else total + e
        cross = e * v if cross is None else cross + e * v
    add_stats(acc, i == 0, (0, 1), (col_sum(total), col_sum(cross)))
    send_stats(i == pl.num_programs(0) - 1, acc, stats)


def fast_back_widen(
    count, sides, grad, act, g3, h3, params3, w, pre, g2, params2, lane_sides, out, w_grad, stats, acc
):
    i = pl.program_id(0)
    c = count[0, 0]
    mean3, inv3, _, _ = norm_terms(g3[...], params3[...], c)
    a, b, d = back_terms(h3[...], params3[...], c, mean3, inv3)
    _, _, scale2, shift2 = norm_terms(g2[...], params2[...], c, True)
    lane_mask = 0.5 * packed_mask(lane_sides[0], 512)

    @pl.when(i == 0)
    def _():
        w_grad[...] = jnp.zeros_like(w_grad)

    s = act[0].reshape(512, LANES)
    back = None
    for g in range(GROUPS):
        mask = clip_mask(sides[i * GROUPS + g], 512)
        v = dot(s, w[g])
        low = (mask * (grad[g].reshape(512, LANES) * a + v * b + d)).astype(BF)
        part = dot_nt(low, w[g])
        back = part if back is None else back + part
        w_grad[g] += dot_tn(s, low)
    p = pre[0].reshape(512, LANES)
    e = back * (lane_mask * slope_half(p * scale2 + shift2))
    out[0] = e.reshape(2, 256, LANES)
    add_stats(acc, i == 0, (0, 1), (col_sum(e), col_sum(e * p)))
    send_stats(i == pl.num_programs(0) - 1, acc, stats)


def fast_back_plane(
    count, e2, pre2, g2, h2, params2, act1, pre1, g1, params1, lane_sides, w, out, w_grad, stats, acc, win, low
):
    i = pl.program_id(0)
    c = count[0, 0]
    mean2, inv2, _, _ = norm_terms(g2[...], params2[...], c, True)
    a, b, d = back_terms(h2[...], params2[...], c, mean2, inv2, True)
    _, _, scale1, shift1 = norm_terms(g1[...], params1[...], c, True)
    mask = packed_mask(lane_sides[0], 256)

    @pl.when(i == 0)
    def _():
        w_grad[...] = jnp.zeros_like(w_grad)
        clear_gaps(win, 2, 16)
        low[256:272, :] = jnp.zeros((16, LANES), BF)

    for frame in range(2):
        part = mask * (e2[0, frame] * a + pre2[0, frame] * b + d)
        low[272 * frame : 272 * frame + 256, :] = part.astype(BF)
        fill_windows(win, part, 16 + 272 * frame, 16)
    both = plane_dot(win, w, 2, 16)
    total, cross = None, None
    for frame in range(2):
        p = pre1[0, frame]
        e = both[272 * frame : 272 * frame + 256] * (0.5 * mask * slope_half(p * scale1 + shift1))
        out[0, frame] = e
        total = e if total is None else total + e
        cross = e * p if cross is None else cross + e * p
        fill_windows(win, act1[0, frame].astype(F32), 16 + 272 * frame, 16)
    for tap in range(3):
        w_grad[tap] += dot_tn(win[16 * tap : 16 * tap + 528, :], low[...])
    add_stats(acc, i == 0, (0, 1), (col_sum(total), col_sum(cross)))
    send_stats(i == pl.num_programs(0) - 1, acc, stats)


def fast_back_first(count, e1, pre1, g1, h1, params1, lane_sides, low):
    c = count[0, 0]
    mean1, inv1, _, _ = norm_terms(g1[...], params1[...], c, True)
    a, b, d = back_terms(h1[...], params1[...], c, mean1, inv1, True)
    mask = packed_mask(lane_sides[0], 256)
    for frame in range(2):
        low[frame, 0] = (mask * (e1[0, frame] * a + pre1[0, frame] * b + d)).astype(BF)


def fast_back_out(grad, low, from_prev, from_next, x, w, out, w_grad):
    i = pl.program_id(0)

    @pl.when(i == 0)
    def _():
        w_grad[...] = jnp.zeros_like(w_grad)

    around = (from_prev[0], low[0, 0], low[1, 0], from_next[0])
    for frame in range(2):
        before, here, after = around[frame], around[frame + 1], around[frame + 2]
        joined = jnp.concatenate([after, here, before], axis=1)
        for g in range(GROUPS):
            out[g, frame] = (grad[g, frame] + dot_nt(joined, w[g])).astype(BF)
            w_grad[g] += dot_tn(x[g, frame], joined)


def pack_kernel(spot, x, *pieces):
    half = x.shape[1] // 2
    for step, piece in enumerate(pieces):
        clip = spot[0] ^ step
        piece[...] = jnp.concatenate([x[clip, :half], x[clip, half:]], axis=1)


def unpack_pieces(spot, *refs):
    out = refs[-1]
    whole_array = len(refs) == 2
    for k in range(out.shape[0]):
        clip = k if whole_array else spot[0] ^ k
        piece = refs[0][k] if whole_array else refs[k][...]
        half, width = piece.shape[0], piece.shape[1] // 2
        out[clip, :half] = piece[:, :width]
        out[clip, half:] = piece[:, width:]


def gather_halves(spot, pieces, x):
    for step, piece in enumerate(pieces):
        x[spot[0] ^ step] = piece[...]
    devices, _, lanes = x.shape
    width = lanes // 2
    low, high = [], []
    for j in range(devices):
        part = x[j]
        low.append(part[:, :width])
        high.append(part[:, width:])
    return jnp.concatenate(low, axis=1), jnp.concatenate(high, axis=1)


def scatter_halves(low, high, out):
    devices, _, lanes = out.shape
    width = lanes // 2
    for j in range(devices):
        out[j] = jnp.concatenate(
            [low[:, j * width : (j + 1) * width], high[:, j * width : (j + 1) * width]], axis=1
        )


def slow_enter(spot, w_time, w_project, *refs):
    *pieces, own, narrow, project, packed = refs
    i = pl.program_id(0)
    frames = narrow.shape[0] - 2

    @pl.when(i == 0)
    def _():
        narrow[...] = jnp.zeros_like(narrow)

    for half, frame in enumerate(gather_halves(spot, pieces, packed)):
        own[half, 0] = frame
        depth = frame.shape[1]
        project[half, 0] = dot(frame, w_project[:depth]).astype(BF)
        t = i + half * (frames // 2)
        for tap in range(3):
            narrow[t + 2 - tap] += dot(frame, w_time[tap, :depth])


def lateral_enter(side, fast, w, pre, stats, acc):
    frames = pre.shape[0]
    width = w.shape[1]
    mask = clip_mask(side[0], 256)
    for t in range(frames):
        taps = [k for k in range(5) if 0 <= 4 * t - 2 + k < 4 * frames]
        joined = jnp.concatenate([fast[4 * t - 2 + k] for k in taps], axis=1)
        v = dot(joined, w[taps[0] : taps[-1] + 1].reshape(len(taps) * width, w.shape[2]))
        pre[t] = v
        mv = mask * v
        add_stats(acc, t == 0, (0, 1), (col_sum(mv), col_sum(mv * v)))
    send_stats(True, acc, stats)


def narrow_enter(count, side, lateral, gl, params, base, w, act, pre, stats, acc):
    frames = pre.shape[0]
    _, _, scale, shift = norm_terms(gl[...], params[...], count[0, 0])
    mask = clip_mask(side[0], 256)
    for t in range(frames):
        act[t] = (mask * silu_half(lateral[t] * scale + shift)).astype(BF)
    width = act.shape[2]
    for t in range(frames):
        taps = [k for k in range(3) if 0 <= t - 1 + k < frames]
        joined = jnp.concatenate([act[t - 1 + k] for k in taps], axis=1)
        v = base[t + 1] + dot(joined, w[taps[0] * width : (taps[-1] + 1) * width, :])
        pre[t] = v
        mv = mask * v
        add_stats(acc, t == 0, (0, 1), (col_sum(mv), col_sum(mv * v)))
    send_stats(True, acc, stats)


def middle_enter(count, side, pre, gn, params, w, act, out, stats, acc, win):
    i = pl.program_id(0)
    frames = pre.shape[0]
    _, _, scale, shift = norm_terms(gn[...], params[...], count[0, 0])
    mask = clip_mask(side[0], 256)

    @pl.when(i == 0)
    def _():
        clear_gaps(win, frames, 16)

    for frame in range(frames):
        a = mask * silu_half(pre[frame] * scale + shift)
        act[frame] = a.astype(BF)
        fill_windows(win, a, 16 + 272 * frame, 16)
    v = plane_dot(win, w, frames, 16)
    total, square = None, None
    for frame in range(frames):
        part = v[272 * frame : 272 * frame + 256]
        out[frame] = part
        masked = mask * part
        total = masked if total is None else total + masked
        square = masked * part if square is None else square + masked * part
    add_stats(acc, i == 0, (0, 1), (col_sum(total), col_sum(square)))
    send_stats(i == pl.num_programs(0) - 1, acc, stats)


def flat(ref):
    block = ref[...]
    return block.reshape(block.shape[0] * block.shape[1], block.shape[2])


def wide_enter(count, side, pre, gm, params, base, lateral, w, w_project, act, project, acc):
    i = pl.program_id(0)
    _, _, scale, shift = norm_terms(gm[...], params[...], count[0, 0])
    rows = pre.shape[0] * pre.shape[1]
    mask = clip_mask(side[0], rows)
    a = (mask * silu_half(flat(pre) * scale + shift)).astype(BF)
    act[...] = a.reshape(act.shape)
    v = dot(a, w[...])
    p = flat(base).astype(F32) + dot(flat(lateral), w_project[...])
    project[...] = p.astype(BF).reshape(project.shape)
    mp = mask * p
    add_stats(
        acc, i == 0, (0, 1, 2, 3), (col_sum(v), col_sum(v * v), col_sum(mp), col_sum(mp * p))
    )


def wide_out(count, side, spot, act, project, g, params_w, params_p, w, *refs):
    devices = (len(refs) - 3) // 2
    cots, pieces, (grad, acc, packed) = refs[:devices], refs[devices : 2 * devices], refs[2 * devices :]
    i = pl.program_id(0)
    c = count[0, 0]
    gathered = g[...]
    _, _, scale_w, shift_w = norm_terms(gathered[:, 0:2], params_w[...], c)
    _, _, scale_p, shift_p = norm_terms(gathered[:, 2:4], params_p[...], c)
    mask = clip_mask(side[0], 256)
    half_mask = 0.5 * mask
    shift = shift_w + shift_p
    halves = []
    sums = [None, None, None]
    for half, cot_half in enumerate(gather_halves(spot, cots, packed)):
        v = dot(act[half, 0], w[...])
        p = project[half, 0].astype(F32)
        u = v * scale_w + (p * scale_p + shift)
        h = 1.0 + jnp.tanh(u)
        s = u * h
        halves.append((mask * s).astype(BF))
        e = (half_mask * cot_half.astype(F32)) * (h + s * (2.0 - h))
        grad[half, 0] = e
        for k, value in enumerate((e, e * v, e * p)):
            value = col_sum(value)
            sums[k] = value if sums[k] is None else sums[k] + value
    scatter_halves(halves[0], halves[1], packed)
    for step, piece in enumerate(pieces):
        piece[...] = packed[spot[0] ^ step]
    add_stats(acc, i == 0, (0, 1, 2), sums)


def middle_back(
    count, side, grad, act, g, h, params_w, w, pre, gm, params_m, out, w_grad, stats, acc, w_acc
):
    i = pl.program_id(0)
    c = count[0, 0]
    mean_w, inv_w, _, _ = norm_terms(g[...][:, 0:2], params_w[...], c)
    a, b, d = back_terms(h[...][:, 0:2], params_w[...], c, mean_w, inv_w)
    _, _, scale_m, shift_m = norm_terms(gm[...], params_m[...], c)
    mask = clip_mask(side[0], pre.shape[0] * pre.shape[1])
    s = flat(act)
    v = dot(s, w[...])
    low = (mask * (flat(grad) * a + v * b + d)).astype(BF)
    p = flat(pre)
    e = dot_nt(low, w[...]) * (0.5 * mask * slope_half(p * scale_m + shift_m))
    out[...] = e.reshape(out.shape)
    add_stats(acc, i == 0, (0, 1), (col_sum(e), col_sum(e * p)))
    send_stats(i == pl.num_programs(0) - 1, acc, stats)

    @pl.when(i == 0)
    def _():
        w_acc[...] = jnp.zeros_like(w_acc)

    w_acc[...] += dot_tn(s, low)

    @pl.when(i == pl.num_programs(0) - 1)
    def _():
        put_columns(w_acc, w_grad)


def project_back(
    count, side, grad, project, g, h, params_p, own, lateral, w, joined, w_grad, w_acc
):
    i = pl.program_id(0)
    c = count[0, 0]
    mean_p, inv_p, _, _ = norm_terms(g[...][:, 2:4], params_p[...], c)
    rows = h[...]
    total = jnp.concatenate([rows[:, 0:1], rows[:, 2:3]], axis=1)
    a, b, d = back_terms(total, params_p[...], c, mean_p, inv_p)
    mask = clip_mask(side[0], grad.shape[0] * grad.shape[1])
    low = (mask * (flat(grad) * a + flat(project).astype(F32) * b + d)).astype(BF)
    joined[...] = dot_nt(low, w[...]).astype(BF).reshape(joined.shape)

    @pl.when(i == 0)
    def _():
        w_acc[...] = jnp.zeros_like(w_acc)

    width = own.shape[2]
    w_acc[0:width, :] += dot_tn(flat(own), low)
    w_acc[width:, :] += dot_tn(flat(lateral), low)

    @pl.when(i == pl.num_programs(0) - 1)
    def _():
        put_columns(w_acc, w_grad)


def narrow_back(
    count, side, grad, pre_m, gm, hm, params_m, w, pre_n, gn, params_n, low_out, out, stats, acc, win
):
    i = pl.program_id(0)
    frames = grad.shape[0]
    c = count[0, 0]
    mean_m, inv_m, _, _ = norm_terms(gm[...], params_m[...], c)
    a, b, d = back_terms(hm[...], params_m[...], c, mean_m, inv_m)
    _, _, scale_n, shift_n = norm_terms(gn[...], params_n[...], c)
    mask = clip_mask(side[0], 256)

    @pl.when(i == 0)
    def _():
        clear_gaps(win, frames, 16)

    for frame in range(frames):
        low = mask * (grad[frame] * a + pre_m[frame] * b + d)
        low_out[frame] = low.astype(BF)
        fill_windows(win, low, 16 + 272 * frame, 16)
    back = plane_dot(win, w, frames, 16)
    half_mask = 0.5 * mask
    total, cross = None, None
    for frame in range(frames):
        p = pre_n[frame]
        e = back[272 * frame : 272 * frame + 256] * (half_mask * slope_half(p * scale_n + shift_n))
        out[frame] = e
        total = e if total is None else total + e
        cross = e * p if cross is None else cross + e * p
    add_stats(acc, i == 0, (0, 1), (col_sum(total), col_sum(cross)))
    send_stats(i == pl.num_programs(0) - 1, acc, stats)


def plane_weight(act, low, w_grad, w_acc, win, low_win):
    i = pl.program_id(0)
    frames = act.shape[0]

    @pl.when(i == 0)
    def _():
        w_acc[...] = jnp.zeros_like(w_acc)
        clear_gaps(win, frames, 16)
        low_win[...] = jnp.zeros_like(low_win)

    for frame in range(frames):
        fill_windows(win, act[frame].astype(F32), 16 + 272 * frame, 16)
        low_win[272 * frame : 272 * frame + 256, :] = low[frame]
    rows = low_win.shape[0]
    for tap in range(3):
        w_acc[tap] += dot_tn(win[16 * tap : 16 * tap + rows, :], low_win[...])

    @pl.when(i == pl.num_programs(0) - 1)
    def _():
        w_grad[...] = w_acc[...].astype(BF)


def join_back(
    count, side, grad, pre_n, gn, hn, params_n, w, joined, pre_l, gl, params_l, low, slow, out, stats, acc
):
    i = pl.program_id(0)
    steps = pl.num_programs(0)
    c = count[0, 0]
    frames = low.shape[0] - 2
    width = low.shape[2]
    mask = clip_mask(side[0], 256)

    @pl.when(i == 0)
    def _():
        mean_n, inv_n, _, _ = norm_terms(gn[...], params_n[...], c)
        a, b, d = back_terms(hn[...], params_n[...], c, mean_n, inv_n)
        low[0] = jnp.zeros((256, width), BF)
        low[frames + 1] = jnp.zeros((256, width), BF)
        for t in range(frames):
            low[t + 1] = (mask * (grad[t] * a + pre_n[t] * b + d)).astype(BF)

    _, _, scale_l, shift_l = norm_terms(gl[...], params_l[...], c)
    other = i + frames // 2
    j = jnp.concatenate([joined[0, 0], joined[1, 0]], axis=0).astype(F32)
    for tap in range(3):
        both = jnp.concatenate([low[i + 2 - tap], low[other + 2 - tap]], axis=0)
        j = j + dot_nt(both, w[tap])
    slow_width = j.shape[1] - out.shape[3]
    top = j[:, :slow_width].astype(BF)
    scatter_halves(top[0:256], top[256:512], slow)
    half_mask = 0.5 * mask
    total, cross = None, None
    for half in range(2):
        p = pre_l[half, 0]
        part = j[256 * half : 256 * half + 256, slow_width:]
        e = part * (half_mask * slope_half(p * scale_l + shift_l))
        out[half, 0] = e
        total = e if total is None else total + e
        cross = e * p if cross is None else cross + e * p
    add_stats(acc, i == 0, (0, 1), (col_sum(total), col_sum(cross)))
    send_stats(i == steps - 1, acc, stats)


def lateral_back(count, side, grad, pre_l, gl, hl, params_l, w, low, out):
    c = count[0, 0]
    frames = grad.shape[0]
    mean_l, inv_l, _, _ = norm_terms(gl[...], params_l[...], c)
    a, b, d = back_terms(hl[...], params_l[...], c, mean_l, inv_l)
    mask = clip_mask(side[0], 256)
    for t in range(frames):
        low[t] = (mask * (grad[t] * a + pre_l[t] * b + d)).astype(BF)
    for t in range(0, frames, 2):
        pair = jnp.concatenate([low[t], low[t + 1]], axis=0)
        last = t + 2 == frames
        after = jnp.zeros(low.shape[1:], BF) if last else low[t + 2]
        shifted = jnp.concatenate([low[t + 1], after], axis=0)
        results = (
            dot_nt(pair, w[2]),
            dot_nt(pair, w[3]),
            dot_nt(pair, w[4]) + dot_nt(shifted, w[0]),
            dot_nt(shifted, w[1]),
        )
        for k, result in enumerate(results):
            result = result.astype(BF)
            out[4 * t + k] = result[0:256]
            out[4 * t + 4 + k] = result[256:512]


def lateral_weight_back(fast, low, w_grad, w_acc):
    frames = low.shape[0]
    width = fast.shape[2]
    w_acc[...] = jnp.zeros_like(w_acc)
    for t in range(frames):
        taps = [k for k in range(5) if 0 <= 4 * t - 2 + k < 4 * frames]
        joined = jnp.concatenate([fast[4 * t - 2 + k] for k in taps], axis=1)
        w_acc[taps[0] * width : (taps[-1] + 1) * width, :] += dot_tn(joined, low[t])
    w_grad[...] = w_acc[...].astype(BF)


def weight_merge(core, *refs):
    out = refs[-1]
    count = (len(refs) - 1) // 2
    rows = out.shape[0]
    for half in range(2):

        @pl.when(core[0] == half)
        def _(half=half):
            begin = 0
            for mine, other in zip(refs[:count], refs[count : 2 * count]):
                end = begin + mine.shape[0]
                low, high = max(begin, half * rows), min(end, (half + 1) * rows)
                if low < high:
                    part = slice(low - begin, high - begin)
                    total = mine[part, :].astype(F32) + other[part, :].astype(F32)
                    out[low - half * rows : high - half * rows, :] = total.astype(BF)
                begin = end


def lateral_merge(place, mine, other, *outs):
    rows = outs[0].shape[0]
    near = len(outs)
    for step, out in enumerate(outs):
        begin = pl.multiple_of((place[0] * near + (place[1] ^ step)) * rows, 16)
        part = pl.ds(begin, rows)
        out[...] = (mine[part, :].astype(F32) + other[part, :].astype(F32)).astype(BF)


def weight_split(place, *refs):
    project, expand, spatial, time, lateral, full = refs[-6:]
    pieces = refs[:-6]
    near = 4
    share = lateral.shape[0] // len(pieces)
    rows = pieces[0].shape[0] - share
    for k, piece in enumerate(pieces):
        half = place[0] if k < near else 1 - place[0]
        if len(pieces) == near:
            half = 0
        spot = place[1] ^ (k % near)
        begin = pl.multiple_of((half * near + spot) * rows, 16)
        full[pl.ds(begin, rows), :] = piece[:rows, :]
        begin = pl.multiple_of((half * near + spot) * share, 8)
        lateral[pl.ds(begin, share), :] = piece[rows:, :].astype(F32)
    begin = 0
    for out in (project, expand):
        height, width = out.shape[0], full.shape[1]
        for block in range(out.shape[1] // width):
            out[:, block * width : (block + 1) * width] = full[begin : begin + height, :].astype(F32)
            begin += height
    spatial[...] = full[begin : begin + spatial.shape[0], :].astype(F32)
    begin += spatial.shape[0]
    height = project.shape[1]
    for tap in range(3):
        time[tap, :height] = full[begin : begin + height, :].astype(F32)
        begin += height
    rest = time.shape[1] - height
    for tap in range(3):
        time[tap, height:] = full[begin : begin + rest, :].astype(F32)
        begin += rest


def per_device(
    slow_in,
    fast_in,
    clip_side,
    fast_reduce,
    fast_spatial,
    fast_expand,
    lateral_weight,
    slow_reduce,
    slow_spatial,
    slow_expand,
    slow_project,
    fast_reduce_norm,
    fast_spatial_norm,
    fast_expand_norm,
    lateral_norm,
    slow_reduce_norm,
    slow_spatial_norm,
    slow_expand_norm,
    slow_project_norm,
    slow_cot,
    fast_cot,
):
    axes = ("dp", "wa")
    wa_count = lax.axis_size("wa")
    place = lax.axis_index("wa")
    devices = lax.axis_size("dp") * wa_count
    clips = fast_in.shape[0]
    cells = fast_in.shape[2] * fast_in.shape[3]
    frames = slow_in.shape[1]
    packs = clips // GROUPS
    c_f, b_f = fast_reduce.shape[1], fast_reduce.shape[2]
    c_l = lateral_weight.shape[2]
    b_s = slow_reduce.shape[2]
    c_s = slow_expand.shape[1]
    c_cat = slow_project.shape[0]
    half = frames // 2

    def exchange(array):
        return lax.all_to_all(array, "wa", 0, 0, tiled=True)

    def gather_stats(copies):
        return lax.all_to_all(copies, axes, 0, 0, tiled=True)

    def gather_wide(sums):
        dp_count = lax.axis_size("dp")
        if dp_count == 2:
            sums = sums + lax.ppermute(sums, "dp", [(0, 1), (1, 0)])
            copies = jnp.broadcast_to(sums[None], (wa_count,) + sums.shape)
            return lax.all_to_all(copies, "wa", 0, 0, tiled=True)
        return gather_stats(jnp.broadcast_to(sums[None], (devices,) + sums.shape))

    smem = scalars()

    area = jnp.sum(clip_side * clip_side)
    area_all = lax.psum(area, "dp").astype(F32)
    fast_count = (area_all * (fast_in.shape[1] * wa_count)).reshape(1, 1)
    slow_count = (area_all * frames).reshape(1, 1)
    own_side = lax.dynamic_slice_in_dim(clip_side, place, 1)
    lane_sides = jnp.repeat(clip_side.reshape(packs, GROUPS), LANES // GROUPS, axis=1)
    lane_sides = lane_sides.reshape(packs, 1, LANES)

    eye = jnp.eye(GROUPS, dtype=BF)
    w_first = jnp.einsum("kio,gh->kgiho", fast_reduce, eye).reshape(3, GROUPS, c_f, LANES)
    w_first_back = w_first.transpose(1, 2, 0, 3).reshape(GROUPS, c_f, 3 * LANES)
    w_plane = jnp.einsum("ijab,gh->ijgahb", fast_spatial, eye).reshape(3, 3 * LANES, LANES)
    flipped = fast_spatial[::-1, ::-1].transpose(0, 1, 3, 2)
    w_plane_back = jnp.einsum("ijab,gh->ijgahb", flipped, eye).reshape(3, 3 * LANES, LANES)
    w_widen = jnp.einsum("io,gh->ghio", fast_expand, eye).reshape(GROUPS, LANES, c_f)
    params1 = jnp.tile(fast_reduce_norm, (1, GROUPS))
    params2 = jnp.tile(fast_spatial_norm, (1, GROUPS))
    w_time_lateral = slow_reduce[:, c_s:].reshape(3 * c_l, b_s)
    w_middle = slow_spatial.reshape(3, 3 * b_s, b_s)
    w_middle_back = slow_spatial[::-1, ::-1].transpose(0, 1, 3, 2).reshape(3, 3 * b_s, b_s)

    spot = place.reshape(1)
    piece_shape = (half * cells, 2 * slow_in.shape[4])
    piece_spec = pl.BlockSpec((cells, piece_shape[1]), lambda i: (i, 0))
    flat_shape = (clips, frames * cells, slow_in.shape[4])

    def pack(array):
        flat = array.reshape(flat_shape)
        out = (piece_shape, BF, pl.BlockSpec(piece_shape, lambda *_: (0, 0)))
        return launch(pack_kernel, "pack", (), [(spot, smem), (flat, whole(flat))], [out] * wa_count)

    def exchange_pieces(pieces, begin=0, end=wa_count):
        return [
            lax.ppermute(pieces[step], "wa", [(i, i ^ step) for i in range(wa_count)])
            if step
            else pieces[0]
            for step in range(begin, end)
        ]

    far, close = list(range(wa_count // 2, wa_count)), list(range(1, wa_count // 2))
    turns = [step for pair in zip(far, close) for step in pair] + [far[-1]]

    def turn(pieces, begin, end):
        return tuple(pieces[step] for step in turns[begin:end])

    def gate(arrays, ready):
        return list(launch(lambda: None, "gate", (), [], [], after=(ready,), carry=tuple(arrays)))

    def send(piece, step):
        return lax.ppermute(piece, "wa", [(i, i ^ step) for i in range(wa_count)])

    def send_turns(pieces, begin, end):
        sent = {step: send(pieces[step], step) for step in turns[begin:end]}
        sent[0] = pieces[0]
        return sent

    def send_late(pieces, begin, ready):
        steps = turns[begin:]
        held = gate([pieces[step] for step in steps], ready) if steps else []
        return {step: send(piece, step) for step, piece in zip(steps, held)}

    def by_step(pieces):
        return [pieces[step] for step in range(wa_count)]

    def unpack(pieces):
        (flat,) = launch(
            unpack_pieces,
            "unpack",
            (),
            [(spot, smem)] + [(piece, whole(piece)) for piece in pieces],
            [(flat_shape, BF, pl.BlockSpec(flat_shape, lambda *_: (0, 0, 0)))],
        )
        return flat.reshape(slow_in.shape)

    slow_pieces = exchange_pieces(pack(slow_in))
    cot_out = pack(slow_cot)

    x = fast_in.reshape(clips, 2, cells, c_f)
    x_spec = pl.BlockSpec((GROUPS, 2, cells, c_f), lambda i: (i, 0, 0, 0))
    packed_shape = (packs, 2, cells, LANES)
    packed_spec = pl.BlockSpec((1, 2, cells, LANES), lambda i: (i, 0, 0, 0))
    rim_shape = (packs, cells, LANES)
    rim_spec = pl.BlockSpec((1, cells, LANES), lambda i: (i, 0, 0))
    sides_spec = pl.BlockSpec((1, 1, LANES), lambda i: (i, 0, 0))
    stat8 = ((devices, 8, LANES), F32, pl.BlockSpec((devices, 8, LANES), lambda *_: (0, 0, 0)))
    acc8 = pltpu.VMEM((8, LANES), F32)
    fast_win = window_shape(2, 3 * LANES)
    fast_low = pltpu.VMEM((528, LANES), BF)

    y, to_next, to_prev = launch(
        fast_first,
        "fast_first",
        (packs,),
        [(x, x_spec), (w_first, whole(w_first))],
        [(packed_shape, F32, packed_spec), (rim_shape, BF, rim_spec), (rim_shape, BF, rim_spec)],
    )
    forward = [(i, i + 1) for i in range(wa_count - 1)]
    backward = [(i + 1, i) for i in range(wa_count - 1)]
    from_prev = lax.ppermute(to_next, "wa", forward)
    from_next = lax.ppermute(to_prev, "wa", backward)
    pre1, s1 = launch(
        fast_join,
        "fast_join",
        (packs,),
        [(y, packed_spec), (from_prev, rim_spec), (from_next, rim_spec), (lane_sides, sides_spec)],
        [(packed_shape, F32, packed_spec), stat8],
        [acc8],
        after=turn(slow_pieces, 0, CUT_SLOW[0]),
    )
    g1 = gather_stats(s1)
    act1, pre2, s2 = launch(
        fast_plane,
        "fast_plane",
        (packs,),
        [
            (fast_count, smem),
            (pre1, packed_spec),
            (g1, whole(g1)),
            (params1, whole(params1)),
            (lane_sides, sides_spec),
            (w_plane, whole(w_plane)),
        ],
        [(packed_shape, BF, packed_spec), (packed_shape, F32, packed_spec), stat8],
        [acc8, fast_win],
        after=turn(slow_pieces, CUT_SLOW[0], CUT_SLOW[1]),
    )
    g2 = gather_stats(s2)
    act2, s3 = launch(
        fast_widen,
        "fast_widen",
        (packs,),
        [
            (fast_count, smem),
            (pre2, packed_spec),
            (g2, whole(g2)),
            (params2, whole(params2)),
            (lane_sides, sides_spec),
            (w_widen, whole(w_widen)),
        ],
        [(packed_shape, BF, packed_spec), stat8],
        [acc8],
        after=turn(slow_pieces, CUT_SLOW[1], CUT_SLOW[2]),
    )
    g3 = gather_stats(s3)
    (fast_result,) = launch(
        fast_out,
        "fast_out",
        (packs,),
        [
            (fast_count, smem),
            (clip_side, smem),
            (x, x_spec),
            (act2, packed_spec),
            (g3, whole(g3)),
            (fast_expand_norm, whole(fast_expand_norm)),
            (w_widen, whole(w_widen)),
        ],
        [(x.shape, BF, x_spec)],
        after=turn(slow_pieces, CUT_SLOW[2], CUT_SLOW[3]),
    )

    fast_got = exchange(fast_result.reshape(clips, 2 * cells, c_f)).reshape(4 * frames, cells, c_f)

    def stat(rows, width):
        return ((devices, rows, width), F32, pl.BlockSpec((devices, rows, width), lambda *_: (0, 0, 0)))

    def pair_spec(width):
        return pl.BlockSpec((2, 1, cells, width), lambda i: (0, i, 0, 0))

    def frame_spec(width, count):
        return pl.BlockSpec((count, cells, width), lambda i: (i, 0, 0))

    def pairs(array):
        return array.reshape((2, half) + array.shape[1:])

    own, base_n, base_p = launch(
        slow_enter,
        "slow_enter",
        (half,),
        [(spot, smem), (slow_reduce, whole(slow_reduce)), (slow_project, whole(slow_project))]
        + [(piece, piece_spec) for piece in slow_pieces],
        [
            ((2, half, cells, c_s), BF, pair_spec(c_s)),
            (
                (frames + 2, cells, b_s),
                F32,
                pl.BlockSpec((frames + 2, cells, b_s), lambda *_: (0, 0, 0)),
            ),
            ((2, half, cells, c_s), BF, pair_spec(c_s)),
        ],
        [pltpu.VMEM((wa_count, cells, LANES), BF)],
        flops=2 * frames * cells * c_s * (3 * b_s + c_s),
    )
    own = own.reshape(frames, cells, c_s)
    base_p = base_p.reshape(frames, cells, c_s)
    pre_l, s_l = launch(
        lateral_enter,
        "lateral_enter",
        (),
        [(own_side, smem), (fast_got, whole(fast_got)), (lateral_weight, whole(lateral_weight))],
        [
            ((frames, cells, c_l), F32, pl.BlockSpec((frames, cells, c_l), lambda *_: (0, 0, 0))),
            stat(2, c_l),
        ],
        [pltpu.VMEM((2, c_l), F32)],
        after=(base_n,),
    )
    g_l = gather_stats(s_l)
    cot_out = gate(cot_out, g_l)
    cot_pieces = send_turns(cot_out, 0, GATE_COT)

    lateral_act, pre_n, s_n = launch(
        narrow_enter,
        "narrow_enter",
        (),
        [
            (slow_count, smem),
            (own_side, smem),
            (pre_l, whole(pre_l)),
            (g_l, whole(g_l)),
            (lateral_norm, whole(lateral_norm)),
            (base_n, whole(base_n)),
            (w_time_lateral, whole(w_time_lateral)),
        ],
        [
            ((frames, cells, c_l), BF, pl.BlockSpec((frames, cells, c_l), lambda *_: (0, 0, 0))),
            ((frames, cells, b_s), F32, pl.BlockSpec((frames, cells, b_s), lambda *_: (0, 0, 0))),
            stat(2, b_s),
        ],
        [pltpu.VMEM((2, b_s), F32)],
        after=turn(cot_pieces, 0, CUT_COT[0]),
    )
    g_n = gather_stats(s_n)
    cot_pieces.update(send_late(cot_out, GATE_COT, g_n))
    slow_win = window_shape(4, 3 * b_s)
    slow_low = pltpu.VMEM((4 * 272 - 16, b_s), BF)
    act_n, pre_m, s_m = launch(
        middle_enter,
        "middle_enter",
        (frames // 4,),
        [
            (slow_count, smem),
            (own_side, smem),
            (pre_n, frame_spec(b_s, 4)),
            (g_n, whole(g_n)),
            (slow_reduce_norm, whole(slow_reduce_norm)),
            (w_middle, whole(w_middle)),
        ],
        [
            ((frames, cells, b_s), BF, frame_spec(b_s, 4)),
            ((frames, cells, b_s), F32, frame_spec(b_s, 4)),
            stat(2, b_s),
        ],
        [pltpu.VMEM((2, b_s), F32), slow_win],
        after=turn(cot_pieces, CUT_COT[0], CUT_COT[1]),
    )
    g_m = gather_stats(s_m)
    act_m, project, s_w = launch(
        wide_enter,
        "wide_enter",
        (frames // 2,),
        [
            (slow_count, smem),
            (own_side, smem),
            (pre_m, frame_spec(b_s, 2)),
            (g_m, whole(g_m)),
            (slow_spatial_norm, whole(slow_spatial_norm)),
            (base_p, frame_spec(c_s, 2)),
            (lateral_act, frame_spec(c_l, 2)),
            (slow_expand, whole(slow_expand)),
            (slow_project, pl.BlockSpec((c_l, c_s), lambda i: (c_s // c_l, 0))),
        ],
        [
            ((frames, cells, b_s), BF, frame_spec(b_s, 2)),
            ((frames, cells, c_s), BF, frame_spec(c_s, 2)),
            ((4, c_s), F32, pl.BlockSpec((4, c_s), lambda *_: (0, 0))),
        ],
        after=turn(cot_pieces, CUT_COT[1], CUT_COT[2]),
    )
    g_w = gather_wide(s_w)
    *out_pieces, wide_grad, t_w = launch(
        wide_out,
        "wide_out",
        (half,),
        [
            (slow_count, smem),
            (own_side, smem),
            (spot, smem),
            (pairs(act_m), pair_spec(b_s)),
            (pairs(project), pair_spec(c_s)),
            (g_w, whole(g_w)),
            (slow_expand_norm, whole(slow_expand_norm)),
            (slow_project_norm, whole(slow_project_norm)),
            (slow_expand, whole(slow_expand)),
            *[(piece, piece_spec) for piece in by_step(cot_pieces)],
        ],
        [
            *[(piece_shape, BF, piece_spec)] * wa_count,
            ((2, half, cells, c_s), F32, pair_spec(c_s)),
            ((4, c_s), F32, pl.BlockSpec((4, c_s), lambda *_: (0, 0))),
        ],
        [pltpu.VMEM((wa_count, cells, LANES), BF)],
    )
    wide_grad = wide_grad.reshape(frames, cells, c_s)
    h_w = gather_wide(t_w)
    result_pieces = send_turns(out_pieces, 0, GATE_RESULT)

    middle_grad, expand_w_grad, t_m = launch(
        middle_back,
        "middle_back",
        (frames // 2,),
        [
            (slow_count, smem),
            (own_side, smem),
            (wide_grad, frame_spec(c_s, 2)),
            (act_m, frame_spec(b_s, 2)),
            (g_w, whole(g_w)),
            (h_w, whole(h_w)),
            (slow_expand_norm, whole(slow_expand_norm)),
            (slow_expand, whole(slow_expand)),
            (pre_m, frame_spec(b_s, 2)),
            (g_m, whole(g_m)),
            (slow_spatial_norm, whole(slow_spatial_norm)),
        ],
        [
            ((frames, cells, b_s), F32, frame_spec(b_s, 2)),
            ((c_s, b_s), BF, pl.BlockSpec((c_s, b_s), lambda *_: (0, 0))),
            stat(2, b_s),
        ],
        [pltpu.VMEM((2, b_s), F32), pltpu.VMEM((b_s, c_s), F32)],
        after=turn(result_pieces, 0, CUT_RESULT[0]),
    )
    h_m = gather_stats(t_m)
    result_pieces.update(send_late(out_pieces, GATE_RESULT, h_m))
    slow_result = unpack(by_step(result_pieces))
    joined_part, project_w_grad = launch(
        project_back,
        "project_back",
        (frames // 2,),
        [
            (slow_count, smem),
            (own_side, smem),
            (wide_grad, frame_spec(c_s, 2)),
            (project, frame_spec(c_s, 2)),
            (g_w, whole(g_w)),
            (h_w, whole(h_w)),
            (slow_project_norm, whole(slow_project_norm)),
            (own, frame_spec(c_s, 2)),
            (lateral_act, frame_spec(c_l, 2)),
            (slow_project, whole(slow_project)),
        ],
        [
            ((frames, cells, c_cat), BF, frame_spec(c_cat, 2)),
            ((c_cat * c_s // b_s, b_s), BF, pl.BlockSpec((c_cat * c_s // b_s, b_s), lambda *_: (0, 0))),
        ],
        [pltpu.VMEM((c_cat, c_s), F32)],
        flops=4 * frames * cells * c_cat * c_s,
    )
    middle_low, narrow_grad, t_n = launch(
        narrow_back,
        "narrow_back",
        (frames // 4,),
        [
            (slow_count, smem),
            (own_side, smem),
            (middle_grad, frame_spec(b_s, 4)),
            (pre_m, frame_spec(b_s, 4)),
            (g_m, whole(g_m)),
            (h_m, whole(h_m)),
            (slow_spatial_norm, whole(slow_spatial_norm)),
            (w_middle_back, whole(w_middle_back)),
            (pre_n, frame_spec(b_s, 4)),
            (g_n, whole(g_n)),
            (slow_reduce_norm, whole(slow_reduce_norm)),
        ],
        [
            ((frames, cells, b_s), BF, frame_spec(b_s, 4)),
            ((frames, cells, b_s), F32, frame_spec(b_s, 4)),
            stat(2, b_s),
        ],
        [pltpu.VMEM((2, b_s), F32), slow_win],
        after=turn(result_pieces, CUT_RESULT[0], CUT_RESULT[1]),
    )
    h_n = gather_stats(t_n)
    (spatial_w_grad,) = launch(
        plane_weight,
        "plane_weight",
        (frames // 4,),
        [(act_n, frame_spec(b_s, 4)), (middle_low, frame_spec(b_s, 4))],
        [((3, 3 * b_s, b_s), BF, pl.BlockSpec((3, 3 * b_s, b_s), lambda *_: (0, 0, 0)))],
        [pltpu.VMEM((3, 3 * b_s, b_s), F32), slow_win, slow_low],
        flops=18 * frames * cells * b_s * b_s,
    )
    narrow_low, grad_packed, lateral_grad, t_l = launch(
        join_back,
        "join_back",
        (half,),
        [
            (slow_count, smem),
            (own_side, smem),
            (narrow_grad, whole(narrow_grad)),
            (pre_n, whole(pre_n)),
            (g_n, whole(g_n)),
            (h_n, whole(h_n)),
            (slow_reduce_norm, whole(slow_reduce_norm)),
            (slow_reduce, whole(slow_reduce)),
            (pairs(joined_part), pair_spec(c_cat)),
            (pairs(pre_l), pair_spec(c_l)),
            (g_l, whole(g_l)),
            (lateral_norm, whole(lateral_norm)),
        ],
        [
            (
                (frames + 2, cells, b_s),
                BF,
                pl.BlockSpec((frames + 2, cells, b_s), lambda *_: (0, 0, 0)),
            ),
            (
                (wa_count,) + piece_shape,
                BF,
                pl.BlockSpec((wa_count, cells, piece_shape[1]), lambda i: (0, i, 0)),
            ),
            ((2, half, cells, c_l), F32, pair_spec(c_l)),
            stat(2, c_l),
        ],
        [pltpu.VMEM((2, c_l), F32)],
        after=turn(result_pieces, CUT_RESULT[1], CUT_RESULT[2]),
    )
    lateral_grad = lateral_grad.reshape(frames, cells, c_l)
    h_l = gather_stats(t_l)
    grad_got = exchange(grad_packed)
    slow_grad = unpack([grad_got])

    def time_weight(values):
        flat = values.reshape(frames * cells, values.shape[2])
        low = narrow_low.reshape((frames + 2) * cells, b_s)
        parts = []
        for tap in range(3):
            begin = (2 - tap) * cells
            parts.append(
                lax.dot_general(
                    flat,
                    lax.slice_in_dim(low, begin, begin + frames * cells, 1, 0),
                    (((0,), (0,)), ((), ())),
                    preferred_element_type=F32,
                )
            )
        return jnp.stack(parts).astype(BF)

    lateral_low, frames_back = launch(
        lateral_back,
        "lateral_back",
        (),
        [
            (slow_count, smem),
            (own_side, smem),
            (lateral_grad, whole(lateral_grad)),
            (pre_l, whole(pre_l)),
            (g_l, whole(g_l)),
            (h_l, whole(h_l)),
            (lateral_norm, whole(lateral_norm)),
            (lateral_weight, whole(lateral_weight)),
        ],
        [
            ((frames, cells, c_l), BF, pl.BlockSpec((frames, cells, c_l), lambda *_: (0, 0, 0))),
            ((4 * frames, cells, c_f), BF, pl.BlockSpec((4 * frames, cells, c_f), lambda *_: (0, 0, 0))),
        ],
        after=turn(result_pieces, CUT_RESULT[2], 15),
    )
    back_got = exchange(frames_back.reshape(wa_count, 2 * cells, c_f)).reshape(x.shape)
    (lateral_w_grad,) = launch(
        lateral_weight_back,
        "lateral_weight_back",
        (),
        [(fast_got, whole(fast_got)), (lateral_low, whole(lateral_low))],
        [((5 * c_f, c_l), BF, pl.BlockSpec((5 * c_f, c_l), lambda *_: (0, 0)))],
        [pltpu.VMEM((5 * c_f, c_l), F32)],
    )

    weight_parts = [
        part.reshape(-1, b_s)
        for part in (
            project_w_grad,
            expand_w_grad,
            spatial_w_grad,
            time_weight(own),
            time_weight(lateral_act),
        )
    ]
    sizes = [part.shape[0] for part in weight_parts]
    near = 4
    inner = [[near * k + j for j in range(near)] for k in range(wa_count // near)]
    outer = [[near * k + j for k in range(wa_count // near)] for j in range(near)]
    dp_count = lax.axis_size("dp")
    core = lax.axis_index("dp")
    swap = [(0, 1), (1, 0)]
    paired = dp_count == 2
    if paired:
        others = [lax.ppermute(part, "dp", swap) for part in weight_parts]
        rows = sum(sizes) // 2
        place_core = core.reshape(1)
        (weights,) = launch(
            weight_merge,
            "weight_merge",
            (),
            [(place_core, smem)] + [(part, whole(part)) for part in weight_parts + others],
            [((rows, b_s), BF, pl.BlockSpec((rows, b_s), lambda *_: (0, 0)))],
        )
    else:
        weights = jnp.concatenate(weight_parts, axis=0)
    first_stage = lax.psum_scatter(weights, "wa", axis_index_groups=inner, tiled=True)
    spot_in = place % near
    if paired:
        other = lax.ppermute(lateral_w_grad, "dp", swap)
        share = lateral_w_grad.shape[0] // (2 * near)
        out = ((share, c_l), BF, pl.BlockSpec((share, c_l), lambda *_: (0, 0)))
        lateral_out = launch(
            lateral_merge,
            "lateral_merge",
            (),
            [(jnp.stack([core, spot_in]), smem)]
            + [(part, whole(part)) for part in (lateral_w_grad, other)],
            [out] * near,
        )
    else:
        share = lateral_w_grad.shape[0] // near
        lateral_out = [
            lax.dynamic_slice_in_dim(lateral_w_grad, (spot_in ^ step) * share, share)
            for step in range(near)
        ]
    lateral_sum = lateral_out[0].astype(F32)
    for step in range(1, near):
        got = lax.ppermute(lateral_out[step], "wa", [(i, i ^ step) for i in range(wa_count)])
        lateral_sum = lateral_sum + got.astype(F32)
    second_stage = lax.psum(
        jnp.concatenate([first_stage, lateral_sum.astype(BF)], axis=0),
        "wa",
        axis_index_groups=outer,
    )

    cot = fast_cot.reshape(x.shape)
    fast_grad3, t3 = launch(
        fast_back_sum,
        "fast_back_sum",
        (packs,),
        [
            (fast_count, smem),
            (clip_side, smem),
            (cot, x_spec),
            (back_got, x_spec),
            (x, x_spec),
            (act2, packed_spec),
            (g3, whole(g3)),
            (fast_expand_norm, whole(fast_expand_norm)),
            (w_widen, whole(w_widen)),
        ],
        [(x.shape, F32, x_spec), stat8],
        [acc8],
    )
    h3 = gather_stats(t3)
    fast_grad2, widen_blocks, t2 = launch(
        fast_back_widen,
        "fast_back_widen",
        (packs,),
        [
            (fast_count, smem),
            (clip_side, smem),
            (fast_grad3, x_spec),
            (act2, packed_spec),
            (g3, whole(g3)),
            (h3, whole(h3)),
            (fast_expand_norm, whole(fast_expand_norm)),
            (w_widen, whole(w_widen)),
            (pre2, packed_spec),
            (g2, whole(g2)),
            (params2, whole(params2)),
            (lane_sides, sides_spec),
        ],
        [
            (packed_shape, F32, packed_spec),
            ((GROUPS, LANES, c_f), F32, pl.BlockSpec((GROUPS, LANES, c_f), lambda *_: (0, 0, 0))),
            stat8,
        ],
        [acc8],
        after=(second_stage,),
    )
    h2 = gather_stats(t2)
    pieces = [second_stage] + [
        lax.ppermute(second_stage, "wa", [(i, i ^ step) for i in range(wa_count)])
        for step in range(1, near)
    ]
    fast_grad1, plane_blocks, t1 = launch(
        fast_back_plane,
        "fast_back_plane",
        (packs,),
        [
            (fast_count, smem),
            (fast_grad2, packed_spec),
            (pre2, packed_spec),
            (g2, whole(g2)),
            (h2, whole(h2)),
            (params2, whole(params2)),
            (act1, packed_spec),
            (pre1, packed_spec),
            (g1, whole(g1)),
            (params1, whole(params1)),
            (lane_sides, sides_spec),
            (w_plane_back, whole(w_plane_back)),
        ],
        [
            (packed_shape, F32, packed_spec),
            (
                (3, 3 * LANES, LANES),
                F32,
                pl.BlockSpec((3, 3 * LANES, LANES), lambda *_: (0, 0, 0)),
            ),
            stat8,
        ],
        [acc8, fast_win, fast_low],
        after=tuple(pieces),
    )
    h1 = gather_stats(t1)
    if paired:
        pieces = pieces + [lax.ppermute(piece, "dp", swap) for piece in pieces]
    else:
        pieces = [lax.psum(piece, "dp") for piece in pieces]
    final = [
        ((c_cat, c_s), F32),
        ((b_s, c_s), F32),
        ((9 * b_s, b_s), F32),
        ((3, c_cat, b_s), F32),
        ((5 * c_f, c_l), F32),
    ]
    project_all, expand_all, spatial_all, time_all, lateral_all = launch(
        weight_split,
        "weight_split",
        (),
        [(jnp.stack([core, place % near]), smem)] + [(piece, whole(piece)) for piece in pieces],
        [
            (shape, dtype, pl.BlockSpec(shape, lambda *_, rank=len(shape): (0,) * rank))
            for shape, dtype in final
        ],
        [pltpu.VMEM((sum(sizes), b_s), BF)],
    )
    (low1,) = launch(
        fast_back_first,
        "fast_back_first",
        (packs,),
        [
            (fast_count, smem),
            (fast_grad1, packed_spec),
            (pre1, packed_spec),
            (g1, whole(g1)),
            (h1, whole(h1)),
            (params1, whole(params1)),
            (lane_sides, sides_spec),
        ],
        [((2, packs, cells, LANES), BF, pl.BlockSpec((2, 1, cells, LANES), lambda i: (0, i, 0, 0)))],
    )
    low_prev = lax.ppermute(low1[1], "wa", forward)
    low_next = lax.ppermute(low1[0], "wa", backward)
    fast_grad, first_blocks = launch(
        fast_back_out,
        "fast_back_out",
        (packs,),
        [
            (fast_grad3, x_spec),
            (low1, pl.BlockSpec((2, 1, cells, LANES), lambda i: (0, i, 0, 0))),
            (low_prev, rim_spec),
            (low_next, rim_spec),
            (x, x_spec),
            (w_first_back, whole(w_first_back)),
        ],
        [
            (x.shape, BF, x_spec),
            (
                (GROUPS, c_f, 3 * LANES),
                F32,
                pl.BlockSpec((GROUPS, c_f, 3 * LANES), lambda *_: (0, 0, 0)),
            ),
        ],
        after=(grad_got,),
    )
    expand_part = sum(widen_blocks[g, g * b_f : (g + 1) * b_f] for g in range(GROUPS))
    plane_view = plane_blocks.reshape(3, 3, GROUPS, b_f, GROUPS, b_f)
    spatial_part = sum(plane_view[:, :, g, :, g] for g in range(GROUPS))
    first_view = first_blocks.reshape(GROUPS, c_f, 3, GROUPS, b_f)
    reduce_part = sum(first_view[g, :, :, g] for g in range(GROUPS)).transpose(1, 0, 2)

    small = jnp.concatenate(
        [reduce_part.reshape(-1), spatial_part.reshape(-1), expand_part.reshape(-1)]
    )
    share = -(-small.shape[0] // (devices * LANES)) * LANES
    padded = jnp.pad(small, (0, share * devices - small.shape[0])).reshape(devices, share // LANES, LANES)
    mine = jnp.sum(gather_stats(padded), axis=0)
    copies = jnp.broadcast_to(mine[None], padded.shape)
    (small_all,) = gate([gather_stats(copies)], slow_grad)
    small_all = small_all.reshape(-1)
    first_size, plane_size = reduce_part.size, spatial_part.size
    fast_reduce_grad = small_all[:first_size].reshape(fast_reduce.shape)
    fast_spatial_grad = small_all[first_size : first_size + plane_size].reshape(fast_spatial.shape)
    fast_expand_grad = small_all[first_size + plane_size : small.shape[0]].reshape(fast_expand.shape)

    def norm_grad(sums, moments, count, folded=False):
        total, moment = jnp.sum(sums, axis=0), jnp.sum(moments, axis=0)
        if folded:
            total = total.reshape(total.shape[0], GROUPS, -1).sum(axis=1)
            moment = moment.reshape(moment.shape[0], GROUPS, -1).sum(axis=1)
        mean = moment[0] / count[0, 0]
        inv = lax.rsqrt(moment[1] / count[0, 0] - mean * mean + EPSILON)
        return jnp.stack([(total[1] - mean * total[0]) * inv, total[0]])

    h_project = jnp.concatenate([h_w[:, 0:1], h_w[:, 2:3]], axis=1)
    return (
        slow_result,
        fast_result.reshape(fast_in.shape),
        slow_grad,
        fast_grad.reshape(fast_in.shape),
        fast_reduce_grad,
        fast_spatial_grad,
        fast_expand_grad,
        lateral_all.reshape(lateral_weight.shape),
        time_all,
        spatial_all.reshape(slow_spatial.shape),
        expand_all,
        project_all,
        norm_grad(h1, g1, fast_count, True),
        norm_grad(h2, g2, fast_count, True),
        norm_grad(h3, g3, fast_count),
        norm_grad(h_l, g_l, slow_count),
        norm_grad(h_n, g_n, slow_count),
        norm_grad(h_m, g_m, slow_count),
        norm_grad(h_w[:, 0:2], g_w[:, 0:2], slow_count),
        norm_grad(h_project, g_w[:, 2:4], slow_count),
    )


def solution(mesh):
    wide = P("dp", None, None, None, "wa")
    fast = P("dp", "wa", None, None, None)
    same = P()
    return jax.shard_map(
        per_device,
        mesh=mesh,
        in_specs=(wide, fast, P("dp")) + (same,) * 16 + (wide, fast),
        out_specs=(wide, fast, wide, fast) + (same,) * 16,
        check_vma=False,
    )
```

```python
import functools

import jax
import jax.numpy as jnp
from jax import lax
from jax.experimental import pallas as pl
from jax.experimental.pallas import tpu as pltpu
from jax.sharding import PartitionSpec as P

EPSILON = 1e-05
BF = jnp.bfloat16
F32 = jnp.float32
LANES = 128
GROUPS = 4
VMEM_BYTES = 52 * 1024 * 1024
CUT_SLOW = (2, 6, 10, 15)
CUT_COT = (0, 4, 10)
CUT_RESULT = (0, 3, 9)
GATE_COT = 8
GATE_RESULT = 5


def whole(array):
    rank = len(array.shape)
    return pl.BlockSpec(array.shape, lambda *_: (0,) * rank)


def scalars():
    return pl.BlockSpec(memory_space=pltpu.SMEM)


def launch(body, name, grid, inputs, outputs, scratch=(), flops=0, after=(), carry=()):
    used, given = len(inputs), len(outputs)
    held = pl.BlockSpec(memory_space=pl.ANY)
    inputs = inputs + [(array, held) for array in (*after, *carry)]
    outputs = outputs + [(array.shape, array.dtype, held) for array in carry]
    first = used + len(after)
    aliases = {first + k: given + k for k in range(len(carry))}

    def kernel(*refs):
        outs = refs[len(inputs) :]
        body(*refs[:used], *outs[:given], *outs[len(outputs) :])

    traffic = sum(a.size * a.dtype.itemsize for a, _ in inputs)
    for shape, dtype, _ in outputs:
        count = 1
        for entry in shape:
            count *= entry
        traffic += count * jnp.dtype(dtype).itemsize
    return pl.pallas_call(
        kernel,
        name=name,
        grid=grid,
        in_specs=[spec for _, spec in inputs],
        out_specs=[spec for _, _, spec in outputs],
        out_shape=[jax.ShapeDtypeStruct(shape, dtype) for shape, dtype, _ in outputs],
        scratch_shapes=list(scratch),
        input_output_aliases=aliases,
        compiler_params=pltpu.CompilerParams(vmem_limit_bytes=VMEM_BYTES),
        cost_estimate=pl.CostEstimate(flops=flops, bytes_accessed=traffic, transcendentals=0),
    )(*[array for array, _ in inputs])


def dot(a, b):
    return lax.dot_general(a, b, (((1,), (0,)), ((), ())), preferred_element_type=F32)


def dot_nt(a, b):
    return lax.dot_general(a, b, (((1,), (1,)), ((), ())), preferred_element_type=F32)


def dot_tn(a, b):
    return lax.dot_general(a, b, (((0,), (0,)), ((), ())), preferred_element_type=F32)


def silu_half(v):
    return v * (1.0 + jnp.tanh(v))


def slope_half(v):
    h = 1.0 + jnp.tanh(v)
    return h + v * h * (2.0 - h)


def cell_ids(rows):
    ids = lax.broadcasted_iota(jnp.int32, (rows, 1), 0)
    return (ids >> 4) & 15, ids & 15


def clip_mask(side, rows):
    h, w = cell_ids(rows)
    return jnp.where((h < side) & (w < side), 1.0, 0.0).astype(F32)


def packed_mask(side_row, rows):
    ids = lax.broadcasted_iota(jnp.int32, (rows, LANES), 0)
    h, w = (ids >> 4) & 15, ids & 15
    return jnp.where((h < side_row) & (w < side_row), 1.0, 0.0).astype(F32)


def fold(row):
    width = LANES // GROUPS
    out = row
    for step in range(1, GROUPS):
        out = out + pltpu.roll(row, step * width, 1)
    return out


def norm_terms(gathered, params, count, folded=False):
    total = jnp.sum(gathered, axis=0)
    if folded:
        total = fold(total)
    mean = total[0:1] / count
    variance = total[1:2] / count - mean * mean
    inv = lax.rsqrt(variance + EPSILON)
    scale = 0.5 * params[0:1] * inv
    return mean, inv, scale, 0.5 * params[1:2] - mean * scale


def back_terms(gathered, params, count, mean, inv, folded=False):
    total = jnp.sum(gathered, axis=0)
    if folded:
        total = fold(total)
    a = params[0:1] * inv
    b = -a * inv * inv * (total[1:2] - mean * total[0:1]) / count
    return a, b, -a * total[0:1] / count - b * mean


def col_sum(v):
    return jnp.sum(v, axis=0, keepdims=True)


def add_stats(acc, first, rows, values):
    @pl.when(first)
    def _():
        acc[...] = jnp.zeros_like(acc)

    for row, value in zip(rows, values):
        acc[row : row + 1, :] += value


def send_stats(last, acc, out):
    @pl.when(last)
    def _():
        out[...] = jnp.broadcast_to(acc[...][None], out.shape)


def put_columns(wide, out):
    rows, width = wide.shape[0], out.shape[1]
    for block in range(wide.shape[1] // width):
        out[block * rows : (block + 1) * rows, :] = wide[:, block * width : (block + 1) * width].astype(BF)


def fill_windows(scratch, values, first, cells):
    rows = values.shape[0]
    w = lax.broadcasted_iota(jnp.int32, (rows, 1), 0) & (cells - 1)
    left = jnp.where(w == 0, 0.0, pltpu.roll(values, 1, 0))
    right = jnp.where(w == cells - 1, 0.0, pltpu.roll(values, rows - 1, 0))
    scratch[first : first + rows, :] = jnp.concatenate(
        [left.astype(BF), values.astype(BF), right.astype(BF)], axis=1
    )


def clear_gaps(scratch, frames, cells):
    pitch = cells * (cells + 1)
    for frame in range(frames + 1):
        scratch[frame * pitch : frame * pitch + cells, :] = jnp.zeros((cells, scratch.shape[1]), BF)


def plane_dot(scratch, weight, frames, cells):
    rows = frames * cells * (cells + 1) - cells
    out = dot(scratch[0:rows, :], weight[0])
    for tap in (1, 2):
        out = out + dot(scratch[tap * cells : tap * cells + rows, :], weight[tap])
    return out


def window_shape(frames, width):
    return pltpu.VMEM((frames * 272 + 16, width), BF)


def fast_first(x, w, y, to_next, to_prev):
    def over(frame, tap):
        out = dot(x[0, frame], w[tap, 0])
        for g in range(1, GROUPS):
            out = out + dot(x[g, frame], w[tap, g])
        return out

    y[0, 0] = over(0, 1) + over(1, 2)
    y[0, 1] = over(0, 0) + over(1, 1)
    to_next[0] = over(1, 0).astype(BF)
    to_prev[0] = over(0, 2).astype(BF)


def fast_join(y, from_prev, from_next, sides, pre, stats, acc):
    i = pl.program_id(0)
    mask = packed_mask(sides[0], 256)
    first = y[0, 0] + from_prev[0].astype(F32)
    second = y[0, 1] + from_next[0].astype(F32)
    pre[0, 0] = first
    pre[0, 1] = second
    m1, m2 = first * mask, second * mask
    add_stats(acc, i == 0, (0, 1), (col_sum(m1 + m2), col_sum(m1 * first + m2 * second)))
    send_stats(i == pl.num_programs(0) - 1, acc, stats)


def fast_plane(count, pre, g1, params, sides, w, act, out, stats, acc, win):
    i = pl.program_id(0)
    _, _, scale, shift = norm_terms(g1[...], params[...], count[0, 0], True)
    mask = packed_mask(sides[0], 256)

    @pl.when(i == 0)
    def _():
        clear_gaps(win, 2, 16)

    for frame in range(2):
        a = mask * silu_half(pre[0, frame] * scale + shift)
        act[0, frame] = a.astype(BF)
        fill_windows(win, a, 16 + 272 * frame, 16)
    both = plane_dot(win, w, 2, 16)
    v0, v1 = both[0:256], both[272:528]
    out[0, 0] = v0
    out[0, 1] = v1
    m0, m1 = mask * v0, mask * v1
    add_stats(acc, i == 0, (0, 1), (col_sum(m0 + m1), col_sum(m0 * v0 + m1 * v1)))
    send_stats(i == pl.num_programs(0) - 1, acc, stats)


def fast_widen(count, pre, g2, params, sides, w, act, stats, acc):
    i = pl.program_id(0)
    _, _, scale, shift = norm_terms(g2[...], params[...], count[0, 0], True)
    mask = packed_mask(sides[0], 512)
    a = (mask * silu_half(pre[0].reshape(512, LANES) * scale + shift)).astype(BF)
    act[0] = a.reshape(2, 256, LANES)
    total, square = None, None
    for g in range(GROUPS):
        v = dot(a, w[g])
        total = v if total is None else total + v
        square = v * v if square is None else square + v * v
    add_stats(acc, i == 0, (0, 1), (col_sum(total), col_sum(square)))
    send_stats(i == pl.num_programs(0) - 1, acc, stats)


def fast_out(count, sides, x, act, g3, params, w, result):
    i = pl.program_id(0)
    _, _, scale, shift = norm_terms(g3[...], params[...], count[0, 0])
    a = act[0].reshape(512, LANES)
    for g in range(GROUPS):
        mask = clip_mask(sides[i * GROUPS + g], 512)
        v = 0.5 * x[g].reshape(512, LANES).astype(F32) + (dot(a, w[g]) * scale + shift)
        result[g] = (mask * silu_half(v)).astype(BF).reshape(2, 256, LANES)


def fast_back_sum(count, sides, cot, back, x, act, g3, params, w, grad, stats, acc):
    i = pl.program_id(0)
    _, _, scale, shift = norm_terms(g3[...], params[...], count[0, 0])
    a = act[0].reshape(512, LANES)
    total, cross = None, None
    for g in range(GROUPS):
        mask = 0.5 * clip_mask(sides[i * GROUPS + g], 512)
        v = dot(a, w[g])
        u = 0.5 * x[g].reshape(512, LANES).astype(F32) + (v * scale + shift)
        given = cot[g].reshape(512, LANES).astype(F32) + back[g].reshape(512, LANES).astype(F32)
        e = given * (mask * slope_half(u))
        grad[g] = e.reshape(2, 256, LANES)
        total = e if total is None else total + e
        cross = e * v if cross is None else cross + e * v
    add_stats(acc, i == 0, (0, 1), (col_sum(total), col_sum(cross)))
    send_stats(i == pl.num_programs(0) - 1, acc, stats)


def fast_back_widen(
    count, sides, grad, act, g3, h3, params3, w, pre, g2, params2, lane_sides, out, w_grad, stats, acc
):
    i = pl.program_id(0)
    c = count[0, 0]
    mean3, inv3, _, _ = norm_terms(g3[...], params3[...], c)
    a, b, d = back_terms(h3[...], params3[...], c, mean3, inv3)
    _, _, scale2, shift2 = norm_terms(g2[...], params2[...], c, True)
    lane_mask = 0.5 * packed_mask(lane_sides[0], 512)

    @pl.when(i == 0)
    def _():
        w_grad[...] = jnp.zeros_like(w_grad)

    s = act[0].reshape(512, LANES)
    back = None
    for g in range(GROUPS):
        mask = clip_mask(sides[i * GROUPS + g], 512)
        v = dot(s, w[g])
        low = (mask * (grad[g].reshape(512, LANES) * a + v * b + d)).astype(BF)
        part = dot_nt(low, w[g])
        back = part if back is None else back + part
        w_grad[g] += dot_tn(s, low)
    p = pre[0].reshape(512, LANES)
    e = back * (lane_mask * slope_half(p * scale2 + shift2))
    out[0] = e.reshape(2, 256, LANES)
    add_stats(acc, i == 0, (0, 1), (col_sum(e), col_sum(e * p)))
    send_stats(i == pl.num_programs(0) - 1, acc, stats)


def fast_back_plane(
    count, e2, pre2, g2, h2, params2, act1, pre1, g1, params1, lane_sides, w, out, w_grad, stats, acc, win, low
):
    i = pl.program_id(0)
    c = count[0, 0]
    mean2, inv2, _, _ = norm_terms(g2[...], params2[...], c, True)
    a, b, d = back_terms(h2[...], params2[...], c, mean2, inv2, True)
    _, _, scale1, shift1 = norm_terms(g1[...], params1[...], c, True)
    mask = packed_mask(lane_sides[0], 256)

    @pl.when(i == 0)
    def _():
        w_grad[...] = jnp.zeros_like(w_grad)
        clear_gaps(win, 2, 16)
        low[256:272, :] = jnp.zeros((16, LANES), BF)

    for frame in range(2):
        part = mask * (e2[0, frame] * a + pre2[0, frame] * b + d)
        low[272 * frame : 272 * frame + 256, :] = part.astype(BF)
        fill_windows(win, part, 16 + 272 * frame, 16)
    both = plane_dot(win, w, 2, 16)
    total, cross = None, None
    for frame in range(2):
        p = pre1[0, frame]
        e = both[272 * frame : 272 * frame + 256] * (0.5 * mask * slope_half(p * scale1 + shift1))
        out[0, frame] = e
        total = e if total is None else total + e
        cross = e * p if cross is None else cross + e * p
        fill_windows(win, act1[0, frame].astype(F32), 16 + 272 * frame, 16)
    for tap in range(3):
        w_grad[tap] += dot_tn(win[16 * tap : 16 * tap + 528, :], low[...])
    add_stats(acc, i == 0, (0, 1), (col_sum(total), col_sum(cross)))
    send_stats(i == pl.num_programs(0) - 1, acc, stats)


def fast_back_first(count, e1, pre1, g1, h1, params1, lane_sides, low):
    c = count[0, 0]
    mean1, inv1, _, _ = norm_terms(g1[...], params1[...], c, True)
    a, b, d = back_terms(h1[...], params1[...], c, mean1, inv1, True)
    mask = packed_mask(lane_sides[0], 256)
    for frame in range(2):
        low[frame, 0] = (mask * (e1[0, frame] * a + pre1[0, frame] * b + d)).astype(BF)


def fast_back_out(grad, low, from_prev, from_next, x, w, out, w_grad):
    i = pl.program_id(0)

    @pl.when(i == 0)
    def _():
        w_grad[...] = jnp.zeros_like(w_grad)

    around = (from_prev[0], low[0, 0], low[1, 0], from_next[0])
    for frame in range(2):
        before, here, after = around[frame], around[frame + 1], around[frame + 2]
        joined = jnp.concatenate([after, here, before], axis=1)
        for g in range(GROUPS):
            out[g, frame] = (grad[g, frame] + dot_nt(joined, w[g])).astype(BF)
            w_grad[g] += dot_tn(x[g, frame], joined)


def pack_kernel(spot, x, *pieces):
    half = x.shape[1] // 2
    for step, piece in enumerate(pieces):
        clip = spot[0] ^ step
        piece[...] = jnp.concatenate([x[clip, :half], x[clip, half:]], axis=1)


def unpack_pieces(spot, *refs):
    out = refs[-1]
    whole_array = len(refs) == 2
    for k in range(out.shape[0]):
        clip = k if whole_array else spot[0] ^ k
        piece = refs[0][k] if whole_array else refs[k][...]
        half, width = piece.shape[0], piece.shape[1] // 2
        out[clip, :half] = piece[:, :width]
        out[clip, half:] = piece[:, width:]


def gather_halves(spot, pieces, x):
    for step, piece in enumerate(pieces):
        x[spot[0] ^ step] = piece[...]
    devices, _, lanes = x.shape
    width = lanes // 2
    low, high = [], []
    for j in range(devices):
        part = x[j]
        low.append(part[:, :width])
        high.append(part[:, width:])
    return jnp.concatenate(low, axis=1), jnp.concatenate(high, axis=1)


def scatter_halves(low, high, out):
    devices, _, lanes = out.shape
    width = lanes // 2
    for j in range(devices):
        out[j] = jnp.concatenate(
            [low[:, j * width : (j + 1) * width], high[:, j * width : (j + 1) * width]], axis=1
        )


def slow_enter(spot, w_time, w_project, *refs):
    *pieces, own, narrow, project, packed = refs
    i = pl.program_id(0)
    frames = narrow.shape[0] - 2

    @pl.when(i == 0)
    def _():
        narrow[...] = jnp.zeros_like(narrow)

    for half, frame in enumerate(gather_halves(spot, pieces, packed)):
        own[half, 0] = frame
        depth = frame.shape[1]
        project[half, 0] = dot(frame, w_project[:depth]).astype(BF)
        t = i + half * (frames // 2)
        for tap in range(3):
            narrow[t + 2 - tap] += dot(frame, w_time[tap, :depth])


def lateral_enter(side, fast, w, pre, stats, acc):
    frames = pre.shape[0]
    width = w.shape[1]
    mask = clip_mask(side[0], 256)
    for t in range(frames):
        taps = [k for k in range(5) if 0 <= 4 * t - 2 + k < 4 * frames]
        joined = jnp.concatenate([fast[4 * t - 2 + k] for k in taps], axis=1)
        v = dot(joined, w[taps[0] : taps[-1] + 1].reshape(len(taps) * width, w.shape[2]))
        pre[t] = v
        mv = mask * v
        add_stats(acc, t == 0, (0, 1), (col_sum(mv), col_sum(mv * v)))
    send_stats(True, acc, stats)


def narrow_enter(count, side, lateral, gl, params, base, w, act, pre, stats, acc):
    frames = pre.shape[0]
    _, _, scale, shift = norm_terms(gl[...], params[...], count[0, 0])
    mask = clip_mask(side[0], 256)
    for t in range(frames):
        act[t] = (mask * silu_half(lateral[t] * scale + shift)).astype(BF)
    width = act.shape[2]
    for t in range(frames):
        taps = [k for k in range(3) if 0 <= t - 1 + k < frames]
        joined = jnp.concatenate([act[t - 1 + k] for k in taps], axis=1)
        v = base[t + 1] + dot(joined, w[taps[0] * width : (taps[-1] + 1) * width, :])
        pre[t] = v
        mv = mask * v
        add_stats(acc, t == 0, (0, 1), (col_sum(mv), col_sum(mv * v)))
    send_stats(True, acc, stats)


def middle_enter(count, side, pre, gn, params, w, act, out, stats, acc, win):
    i = pl.program_id(0)
    frames = pre.shape[0]
    _, _, scale, shift = norm_terms(gn[...], params[...], count[0, 0])
    mask = clip_mask(side[0], 256)

    @pl.when(i == 0)
    def _():
        clear_gaps(win, frames, 16)

    for frame in range(frames):
        a = mask * silu_half(pre[frame] * scale + shift)
        act[frame] = a.astype(BF)
        fill_windows(win, a, 16 + 272 * frame, 16)
    v = plane_dot(win, w, frames, 16)
    total, square = None, None
    for frame in range(frames):
        part = v[272 * frame : 272 * frame + 256]
        out[frame] = part
        masked = mask * part
        total = masked if total is None else total + masked
        square = masked * part if square is None else square + masked * part
    add_stats(acc, i == 0, (0, 1), (col_sum(total), col_sum(square)))
    send_stats(i == pl.num_programs(0) - 1, acc, stats)


def flat(ref):
    block = ref[...]
    return block.reshape(block.shape[0] * block.shape[1], block.shape[2])


def wide_enter(count, side, pre, gm, params, base, lateral, w, w_project, act, project, acc):
    i = pl.program_id(0)
    _, _, scale, shift = norm_terms(gm[...], params[...], count[0, 0])
    rows = pre.shape[0] * pre.shape[1]
    mask = clip_mask(side[0], rows)
    a = (mask * silu_half(flat(pre) * scale + shift)).astype(BF)
    act[...] = a.reshape(act.shape)
    v = dot(a, w[...])
    p = flat(base).astype(F32) + dot(flat(lateral), w_project[...])
    project[...] = p.astype(BF).reshape(project.shape)
    mp = mask * p
    add_stats(
        acc, i == 0, (0, 1, 2, 3), (col_sum(v), col_sum(v * v), col_sum(mp), col_sum(mp * p))
    )


def wide_out(count, side, spot, act, project, g, params_w, params_p, w, *refs):
    devices = (len(refs) - 3) // 2
    cots, pieces, (grad, acc, packed) = refs[:devices], refs[devices : 2 * devices], refs[2 * devices :]
    i = pl.program_id(0)
    c = count[0, 0]
    gathered = g[...]
    _, _, scale_w, shift_w = norm_terms(gathered[:, 0:2], params_w[...], c)
    _, _, scale_p, shift_p = norm_terms(gathered[:, 2:4], params_p[...], c)
    mask = clip_mask(side[0], 256)
    half_mask = 0.5 * mask
    shift = shift_w + shift_p
    halves = []
    sums = [None, None, None]
    for half, cot_half in enumerate(gather_halves(spot, cots, packed)):
        v = dot(act[half, 0], w[...])
        p = project[half, 0].astype(F32)
        u = v * scale_w + (p * scale_p + shift)
        h = 1.0 + jnp.tanh(u)
        s = u * h
        halves.append((mask * s).astype(BF))
        e = (half_mask * cot_half.astype(F32)) * (h + s * (2.0 - h))
        grad[half, 0] = e
        for k, value in enumerate((e, e * v, e * p)):
            value = col_sum(value)
            sums[k] = value if sums[k] is None else sums[k] + value
    scatter_halves(halves[0], halves[1], packed)
    for step, piece in enumerate(pieces):
        piece[...] = packed[spot[0] ^ step]
    add_stats(acc, i == 0, (0, 1, 2), sums)


def middle_back(
    count, side, grad, act, g, h, params_w, w, pre, gm, params_m, out, w_grad, stats, acc, w_acc
):
    i = pl.program_id(0)
    c = count[0, 0]
    mean_w, inv_w, _, _ = norm_terms(g[...][:, 0:2], params_w[...], c)
    a, b, d = back_terms(h[...][:, 0:2], params_w[...], c, mean_w, inv_w)
    _, _, scale_m, shift_m = norm_terms(gm[...], params_m[...], c)
    mask = clip_mask(side[0], pre.shape[0] * pre.shape[1])
    s = flat(act)
    v = dot(s, w[...])
    low = (mask * (flat(grad) * a + v * b + d)).astype(BF)
    p = flat(pre)
    e = dot_nt(low, w[...]) * (0.5 * mask * slope_half(p * scale_m + shift_m))
    out[...] = e.reshape(out.shape)
    add_stats(acc, i == 0, (0, 1), (col_sum(e), col_sum(e * p)))
    send_stats(i == pl.num_programs(0) - 1, acc, stats)

    @pl.when(i == 0)
    def _():
        w_acc[...] = jnp.zeros_like(w_acc)

    w_acc[...] += dot_tn(s, low)

    @pl.when(i == pl.num_programs(0) - 1)
    def _():
        put_columns(w_acc, w_grad)


def project_back(
    count, side, grad, project, g, h, params_p, own, lateral, w, joined, w_grad, w_acc
):
    i = pl.program_id(0)
    c = count[0, 0]
    mean_p, inv_p, _, _ = norm_terms(g[...][:, 2:4], params_p[...], c)
    rows = h[...]
    total = jnp.concatenate([rows[:, 0:1], rows[:, 2:3]], axis=1)
    a, b, d = back_terms(total, params_p[...], c, mean_p, inv_p)
    mask = clip_mask(side[0], grad.shape[0] * grad.shape[1])
    low = (mask * (flat(grad) * a + flat(project).astype(F32) * b + d)).astype(BF)
    joined[...] = dot_nt(low, w[...]).astype(BF).reshape(joined.shape)

    @pl.when(i == 0)
    def _():
        w_acc[...] = jnp.zeros_like(w_acc)

    width = own.shape[2]
    w_acc[0:width, :] += dot_tn(flat(own), low)
    w_acc[width:, :] += dot_tn(flat(lateral), low)

    @pl.when(i == pl.num_programs(0) - 1)
    def _():
        put_columns(w_acc, w_grad)


def narrow_back(
    count, side, grad, pre_m, gm, hm, params_m, w, pre_n, gn, params_n, low_out, out, stats, acc, win
):
    i = pl.program_id(0)
    frames = grad.shape[0]
    c = count[0, 0]
    mean_m, inv_m, _, _ = norm_terms(gm[...], params_m[...], c)
    a, b, d = back_terms(hm[...], params_m[...], c, mean_m, inv_m)
    _, _, scale_n, shift_n = norm_terms(gn[...], params_n[...], c)
    mask = clip_mask(side[0], 256)

    @pl.when(i == 0)
    def _():
        clear_gaps(win, frames, 16)

    for frame in range(frames):
        low = mask * (grad[frame] * a + pre_m[frame] * b + d)
        low_out[frame] = low.astype(BF)
        fill_windows(win, low, 16 + 272 * frame, 16)
    back = plane_dot(win, w, frames, 16)
    half_mask = 0.5 * mask
    total, cross = None, None
    for frame in range(frames):
        p = pre_n[frame]
        e = back[272 * frame : 272 * frame + 256] * (half_mask * slope_half(p * scale_n + shift_n))
        out[frame] = e
        total = e if total is None else total + e
        cross = e * p if cross is None else cross + e * p
    add_stats(acc, i == 0, (0, 1), (col_sum(total), col_sum(cross)))
    send_stats(i == pl.num_programs(0) - 1, acc, stats)


def plane_weight(act, low, w_grad, w_acc, win, low_win):
    i = pl.program_id(0)
    frames = act.shape[0]

    @pl.when(i == 0)
    def _():
        w_acc[...] = jnp.zeros_like(w_acc)
        clear_gaps(win, frames, 16)
        low_win[...] = jnp.zeros_like(low_win)

    for frame in range(frames):
        fill_windows(win, act[frame].astype(F32), 16 + 272 * frame, 16)
        low_win[272 * frame : 272 * frame + 256, :] = low[frame]
    rows = low_win.shape[0]
    for tap in range(3):
        w_acc[tap] += dot_tn(win[16 * tap : 16 * tap + rows, :], low_win[...])

    @pl.when(i == pl.num_programs(0) - 1)
    def _():
        w_grad[...] = w_acc[...].astype(BF)


def join_back(
    count, side, grad, pre_n, gn, hn, params_n, w, joined, pre_l, gl, params_l, low, slow, out, stats, acc
):
    i = pl.program_id(0)
    steps = pl.num_programs(0)
    c = count[0, 0]
    frames = low.shape[0] - 2
    width = low.shape[2]
    mask = clip_mask(side[0], 256)

    @pl.when(i == 0)
    def _():
        mean_n, inv_n, _, _ = norm_terms(gn[...], params_n[...], c)
        a, b, d = back_terms(hn[...], params_n[...], c, mean_n, inv_n)
        low[0] = jnp.zeros((256, width), BF)
        low[frames + 1] = jnp.zeros((256, width), BF)
        for t in range(frames):
            low[t + 1] = (mask * (grad[t] * a + pre_n[t] * b + d)).astype(BF)

    _, _, scale_l, shift_l = norm_terms(gl[...], params_l[...], c)
    other = i + frames // 2
    j = jnp.concatenate([joined[0, 0], joined[1, 0]], axis=0).astype(F32)
    for tap in range(3):
        both = jnp.concatenate([low[i + 2 - tap], low[other + 2 - tap]], axis=0)
        j = j + dot_nt(both, w[tap])
    slow_width = j.shape[1] - out.shape[3]
    top = j[:, :slow_width].astype(BF)
    scatter_halves(top[0:256], top[256:512], slow)
    half_mask = 0.5 * mask
    total, cross = None, None
    for half in range(2):
        p = pre_l[half, 0]
        part = j[256 * half : 256 * half + 256, slow_width:]
        e = part * (half_mask * slope_half(p * scale_l + shift_l))
        out[half, 0] = e
        total = e if total is None else total + e
        cross = e * p if cross is None else cross + e * p
    add_stats(acc, i == 0, (0, 1), (col_sum(total), col_sum(cross)))
    send_stats(i == steps - 1, acc, stats)


def lateral_back(count, side, grad, pre_l, gl, hl, params_l, w, low, out):
    c = count[0, 0]
    frames = grad.shape[0]
    mean_l, inv_l, _, _ = norm_terms(gl[...], params_l[...], c)
    a, b, d = back_terms(hl[...], params_l[...], c, mean_l, inv_l)
    mask = clip_mask(side[0], 256)
    for t in range(frames):
        low[t] = (mask * (grad[t] * a + pre_l[t] * b + d)).astype(BF)
    for t in range(0, frames, 2):
        pair = jnp.concatenate([low[t], low[t + 1]], axis=0)
        last = t + 2 == frames
        after = jnp.zeros(low.shape[1:], BF) if last else low[t + 2]
        shifted = jnp.concatenate([low[t + 1], after], axis=0)
        results = (
            dot_nt(pair, w[2]),
            dot_nt(pair, w[3]),
            dot_nt(pair, w[4]) + dot_nt(shifted, w[0]),
            dot_nt(shifted, w[1]),
        )
        for k, result in enumerate(results):
            result = result.astype(BF)
            out[4 * t + k] = result[0:256]
            out[4 * t + 4 + k] = result[256:512]


def lateral_weight_back(fast, low, w_grad, w_acc):
    frames = low.shape[0]
    width = fast.shape[2]
    w_acc[...] = jnp.zeros_like(w_acc)
    for t in range(frames):
        taps = [k for k in range(5) if 0 <= 4 * t - 2 + k < 4 * frames]
        joined = jnp.concatenate([fast[4 * t - 2 + k] for k in taps], axis=1)
        w_acc[taps[0] * width : (taps[-1] + 1) * width, :] += dot_tn(joined, low[t])
    w_grad[...] = w_acc[...].astype(BF)


def weight_merge(core, *refs):
    out = refs[-1]
    count = (len(refs) - 1) // 2
    rows = out.shape[0]
    for half in range(2):

        @pl.when(core[0] == half)
        def _(half=half):
            begin = 0
            for mine, other in zip(refs[:count], refs[count : 2 * count]):
                end = begin + mine.shape[0]
                low, high = max(begin, half * rows), min(end, (half + 1) * rows)
                if low < high:
                    part = slice(low - begin, high - begin)
                    total = mine[part, :].astype(F32) + other[part, :].astype(F32)
                    out[low - half * rows : high - half * rows, :] = total.astype(BF)
                begin = end


def lateral_merge(place, mine, other, *outs):
    rows = outs[0].shape[0]
    near = len(outs)
    for step, out in enumerate(outs):
        begin = pl.multiple_of((place[0] * near + (place[1] ^ step)) * rows, 16)
        part = pl.ds(begin, rows)
        out[...] = (mine[part, :].astype(F32) + other[part, :].astype(F32)).astype(BF)


def weight_split(place, *refs):
    project, expand, spatial, time, lateral, full = refs[-6:]
    pieces = refs[:-6]
    near = 4
    share = lateral.shape[0] // len(pieces)
    rows = pieces[0].shape[0] - share
    for k, piece in enumerate(pieces):
        half = place[0] if k < near else 1 - place[0]
        if len(pieces) == near:
            half = 0
        spot = place[1] ^ (k % near)
        begin = pl.multiple_of((half * near + spot) * rows, 16)
        full[pl.ds(begin, rows), :] = piece[:rows, :]
        begin = pl.multiple_of((half * near + spot) * share, 8)
        lateral[pl.ds(begin, share), :] = piece[rows:, :].astype(F32)
    begin = 0
    for out in (project, expand):
        height, width = out.shape[0], full.shape[1]
        for block in range(out.shape[1] // width):
            out[:, block * width : (block + 1) * width] = full[begin : begin + height, :].astype(F32)
            begin += height
    spatial[...] = full[begin : begin + spatial.shape[0], :].astype(F32)
    begin += spatial.shape[0]
    height = project.shape[1]
    for tap in range(3):
        time[tap, :height] = full[begin : begin + height, :].astype(F32)
        begin += height
    rest = time.shape[1] - height
    for tap in range(3):
        time[tap, height:] = full[begin : begin + rest, :].astype(F32)
        begin += rest


def per_device(
    slow_in,
    fast_in,
    clip_side,
    fast_reduce,
    fast_spatial,
    fast_expand,
    lateral_weight,
    slow_reduce,
    slow_spatial,
    slow_expand,
    slow_project,
    fast_reduce_norm,
    fast_spatial_norm,
    fast_expand_norm,
    lateral_norm,
    slow_reduce_norm,
    slow_spatial_norm,
    slow_expand_norm,
    slow_project_norm,
    slow_cot,
    fast_cot,
):
    axes = ("dp", "wa")
    wa_count = lax.axis_size("wa")
    place = lax.axis_index("wa")
    devices = lax.axis_size("dp") * wa_count
    clips = fast_in.shape[0]
    cells = fast_in.shape[2] * fast_in.shape[3]
    frames = slow_in.shape[1]
    packs = clips // GROUPS
    c_f, b_f = fast_reduce.shape[1], fast_reduce.shape[2]
    c_l = lateral_weight.shape[2]
    b_s = slow_reduce.shape[2]
    c_s = slow_expand.shape[1]
    c_cat = slow_project.shape[0]
    half = frames // 2

    def exchange(array):
        return lax.all_to_all(array, "wa", 0, 0, tiled=True)

    def gather_stats(copies):
        return lax.all_to_all(copies, axes, 0, 0, tiled=True)

    def gather_wide(sums):
        dp_count = lax.axis_size("dp")
        if dp_count == 2:
            sums = sums + lax.ppermute(sums, "dp", [(0, 1), (1, 0)])
            copies = jnp.broadcast_to(sums[None], (wa_count,) + sums.shape)
            return lax.all_to_all(copies, "wa", 0, 0, tiled=True)
        return gather_stats(jnp.broadcast_to(sums[None], (devices,) + sums.shape))

    smem = scalars()

    area = jnp.sum(clip_side * clip_side)
    area_all = lax.psum(area, "dp").astype(F32)
    fast_count = (area_all * (fast_in.shape[1] * wa_count)).reshape(1, 1)
    slow_count = (area_all * frames).reshape(1, 1)
    own_side = lax.dynamic_slice_in_dim(clip_side, place, 1)
    lane_sides = jnp.repeat(clip_side.reshape(packs, GROUPS), LANES // GROUPS, axis=1)
    lane_sides = lane_sides.reshape(packs, 1, LANES)

    eye = jnp.eye(GROUPS, dtype=BF)
    w_first = jnp.einsum("kio,gh->kgiho", fast_reduce, eye).reshape(3, GROUPS, c_f, LANES)
    w_first_back = w_first.transpose(1, 2, 0, 3).reshape(GROUPS, c_f, 3 * LANES)
    w_plane = jnp.einsum("ijab,gh->ijgahb", fast_spatial, eye).reshape(3, 3 * LANES, LANES)
    flipped = fast_spatial[::-1, ::-1].transpose(0, 1, 3, 2)
    w_plane_back = jnp.einsum("ijab,gh->ijgahb", flipped, eye).reshape(3, 3 * LANES, LANES)
    w_widen = jnp.einsum("io,gh->ghio", fast_expand, eye).reshape(GROUPS, LANES, c_f)
    params1 = jnp.tile(fast_reduce_norm, (1, GROUPS))
    params2 = jnp.tile(fast_spatial_norm, (1, GROUPS))
    w_time_lateral = slow_reduce[:, c_s:].reshape(3 * c_l, b_s)
    w_middle = slow_spatial.reshape(3, 3 * b_s, b_s)
    w_middle_back = slow_spatial[::-1, ::-1].transpose(0, 1, 3, 2).reshape(3, 3 * b_s, b_s)

    spot = place.reshape(1)
    piece_shape = (half * cells, 2 * slow_in.shape[4])
    piece_spec = pl.BlockSpec((cells, piece_shape[1]), lambda i: (i, 0))
    flat_shape = (clips, frames * cells, slow_in.shape[4])

    def pack(array):
        flat = array.reshape(flat_shape)
        out = (piece_shape, BF, pl.BlockSpec(piece_shape, lambda *_: (0, 0)))
        return launch(pack_kernel, "pack", (), [(spot, smem), (flat, whole(flat))], [out] * wa_count)

    def exchange_pieces(pieces, begin=0, end=wa_count):
        return [
            lax.ppermute(pieces[step], "wa", [(i, i ^ step) for i in range(wa_count)])
            if step
            else pieces[0]
            for step in range(begin, end)
        ]

    far, close = list(range(wa_count // 2, wa_count)), list(range(1, wa_count // 2))
    turns = [step for pair in zip(far, close) for step in pair] + [far[-1]]

    def turn(pieces, begin, end):
        return tuple(pieces[step] for step in turns[begin:end])

    def gate(arrays, ready):
        return list(launch(lambda: None, "gate", (), [], [], after=(ready,), carry=tuple(arrays)))

    def send(piece, step):
        return lax.ppermute(piece, "wa", [(i, i ^ step) for i in range(wa_count)])

    def send_turns(pieces, begin, end):
        sent = {step: send(pieces[step], step) for step in turns[begin:end]}
        sent[0] = pieces[0]
        return sent

    def send_late(pieces, begin, ready):
        steps = turns[begin:]
        held = gate([pieces[step] for step in steps], ready) if steps else []
        return {step: send(piece, step) for step, piece in zip(steps, held)}

    def by_step(pieces):
        return [pieces[step] for step in range(wa_count)]

    def unpack(pieces):
        (flat,) = launch(
            unpack_pieces,
            "unpack",
            (),
            [(spot, smem)] + [(piece, whole(piece)) for piece in pieces],
            [(flat_shape, BF, pl.BlockSpec(flat_shape, lambda *_: (0, 0, 0)))],
        )
        return flat.reshape(slow_in.shape)

    slow_pieces = exchange_pieces(pack(slow_in))
    cot_out = pack(slow_cot)

    x = fast_in.reshape(clips, 2, cells, c_f)
    x_spec = pl.BlockSpec((GROUPS, 2, cells, c_f), lambda i: (i, 0, 0, 0))
    packed_shape = (packs, 2, cells, LANES)
    packed_spec = pl.BlockSpec((1, 2, cells, LANES), lambda i: (i, 0, 0, 0))
    rim_shape = (packs, cells, LANES)
    rim_spec = pl.BlockSpec((1, cells, LANES), lambda i: (i, 0, 0))
    sides_spec = pl.BlockSpec((1, 1, LANES), lambda i: (i, 0, 0))
    stat8 = ((devices, 8, LANES), F32, pl.BlockSpec((devices, 8, LANES), lambda *_: (0, 0, 0)))
    acc8 = pltpu.VMEM((8, LANES), F32)
    fast_win = window_shape(2, 3 * LANES)
    fast_low = pltpu.VMEM((528, LANES), BF)

    y, to_next, to_prev = launch(
        fast_first,
        "fast_first",
        (packs,),
        [(x, x_spec), (w_first, whole(w_first))],
        [(packed_shape, F32, packed_spec), (rim_shape, BF, rim_spec), (rim_shape, BF, rim_spec)],
    )
    forward = [(i, i + 1) for i in range(wa_count - 1)]
    backward = [(i + 1, i) for i in range(wa_count - 1)]
    from_prev = lax.ppermute(to_next, "wa", forward)
    from_next = lax.ppermute(to_prev, "wa", backward)
    pre1, s1 = launch(
        fast_join,
        "fast_join",
        (packs,),
        [(y, packed_spec), (from_prev, rim_spec), (from_next, rim_spec), (lane_sides, sides_spec)],
        [(packed_shape, F32, packed_spec), stat8],
        [acc8],
        after=turn(slow_pieces, 0, CUT_SLOW[0]),
    )
    g1 = gather_stats(s1)
    act1, pre2, s2 = launch(
        fast_plane,
        "fast_plane",
        (packs,),
        [
            (fast_count, smem),
            (pre1, packed_spec),
            (g1, whole(g1)),
            (params1, whole(params1)),
            (lane_sides, sides_spec),
            (w_plane, whole(w_plane)),
        ],
        [(packed_shape, BF, packed_spec), (packed_shape, F32, packed_spec), stat8],
        [acc8, fast_win],
        after=turn(slow_pieces, CUT_SLOW[0], CUT_SLOW[1]),
    )
    g2 = gather_stats(s2)
    act2, s3 = launch(
        fast_widen,
        "fast_widen",
        (packs,),
        [
            (fast_count, smem),
            (pre2, packed_spec),
            (g2, whole(g2)),
            (params2, whole(params2)),
            (lane_sides, sides_spec),
            (w_widen, whole(w_widen)),
        ],
        [(packed_shape, BF, packed_spec), stat8],
        [acc8],
        after=turn(slow_pieces, CUT_SLOW[1], CUT_SLOW[2]),
    )
    g3 = gather_stats(s3)
    (fast_result,) = launch(
        fast_out,
        "fast_out",
        (packs,),
        [
            (fast_count, smem),
            (clip_side, smem),
            (x, x_spec),
            (act2, packed_spec),
            (g3, whole(g3)),
            (fast_expand_norm, whole(fast_expand_norm)),
            (w_widen, whole(w_widen)),
        ],
        [(x.shape, BF, x_spec)],
        after=turn(slow_pieces, CUT_SLOW[2], CUT_SLOW[3]),
    )

    fast_got = exchange(fast_result.reshape(clips, 2 * cells, c_f)).reshape(4 * frames, cells, c_f)

    def stat(rows, width):
        return ((devices, rows, width), F32, pl.BlockSpec((devices, rows, width), lambda *_: (0, 0, 0)))

    def pair_spec(width):
        return pl.BlockSpec((2, 1, cells, width), lambda i: (0, i, 0, 0))

    def frame_spec(width, count):
        return pl.BlockSpec((count, cells, width), lambda i: (i, 0, 0))

    def pairs(array):
        return array.reshape((2, half) + array.shape[1:])

    own, base_n, base_p = launch(
        slow_enter,
        "slow_enter",
        (half,),
        [(spot, smem), (slow_reduce, whole(slow_reduce)), (slow_project, whole(slow_project))]
        + [(piece, piece_spec) for piece in slow_pieces],
        [
            ((2, half, cells, c_s), BF, pair_spec(c_s)),
            (
                (frames + 2, cells, b_s),
                F32,
                pl.BlockSpec((frames + 2, cells, b_s), lambda *_: (0, 0, 0)),
            ),
            ((2, half, cells, c_s), BF, pair_spec(c_s)),
        ],
        [pltpu.VMEM((wa_count, cells, LANES), BF)],
        flops=2 * frames * cells * c_s * (3 * b_s + c_s),
    )
    own = own.reshape(frames, cells, c_s)
    base_p = base_p.reshape(frames, cells, c_s)
    pre_l, s_l = launch(
        lateral_enter,
        "lateral_enter",
        (),
        [(own_side, smem), (fast_got, whole(fast_got)), (lateral_weight, whole(lateral_weight))],
        [
            ((frames, cells, c_l), F32, pl.BlockSpec((frames, cells, c_l), lambda *_: (0, 0, 0))),
            stat(2, c_l),
        ],
        [pltpu.VMEM((2, c_l), F32)],
        after=(base_n,),
    )
    g_l = gather_stats(s_l)
    cot_out = gate(cot_out, g_l)
    cot_pieces = send_turns(cot_out, 0, GATE_COT)

    lateral_act, pre_n, s_n = launch(
        narrow_enter,
        "narrow_enter",
        (),
        [
            (slow_count, smem),
            (own_side, smem),
            (pre_l, whole(pre_l)),
            (g_l, whole(g_l)),
            (lateral_norm, whole(lateral_norm)),
            (base_n, whole(base_n)),
            (w_time_lateral, whole(w_time_lateral)),
        ],
        [
            ((frames, cells, c_l), BF, pl.BlockSpec((frames, cells, c_l), lambda *_: (0, 0, 0))),
            ((frames, cells, b_s), F32, pl.BlockSpec((frames, cells, b_s), lambda *_: (0, 0, 0))),
            stat(2, b_s),
        ],
        [pltpu.VMEM((2, b_s), F32)],
        after=turn(cot_pieces, 0, CUT_COT[0]),
    )
    g_n = gather_stats(s_n)
    cot_pieces.update(send_late(cot_out, GATE_COT, g_n))
    slow_win = window_shape(4, 3 * b_s)
    slow_low = pltpu.VMEM((4 * 272 - 16, b_s), BF)
    act_n, pre_m, s_m = launch(
        middle_enter,
        "middle_enter",
        (frames // 4,),
        [
            (slow_count, smem),
            (own_side, smem),
            (pre_n, frame_spec(b_s, 4)),
            (g_n, whole(g_n)),
            (slow_reduce_norm, whole(slow_reduce_norm)),
            (w_middle, whole(w_middle)),
        ],
        [
            ((frames, cells, b_s), BF, frame_spec(b_s, 4)),
            ((frames, cells, b_s), F32, frame_spec(b_s, 4)),
            stat(2, b_s),
        ],
        [pltpu.VMEM((2, b_s), F32), slow_win],
        after=turn(cot_pieces, CUT_COT[0], CUT_COT[1]),
    )
    g_m = gather_stats(s_m)
    act_m, project, s_w = launch(
        wide_enter,
        "wide_enter",
        (frames // 2,),
        [
            (slow_count, smem),
            (own_side, smem),
            (pre_m, frame_spec(b_s, 2)),
            (g_m, whole(g_m)),
            (slow_spatial_norm, whole(slow_spatial_norm)),
            (base_p, frame_spec(c_s, 2)),
            (lateral_act, frame_spec(c_l, 2)),
            (slow_expand, whole(slow_expand)),
            (slow_project, pl.BlockSpec((c_l, c_s), lambda i: (c_s // c_l, 0))),
        ],
        [
            ((frames, cells, b_s), BF, frame_spec(b_s, 2)),
            ((frames, cells, c_s), BF, frame_spec(c_s, 2)),
            ((4, c_s), F32, pl.BlockSpec((4, c_s), lambda *_: (0, 0))),
        ],
        after=turn(cot_pieces, CUT_COT[1], CUT_COT[2]),
    )
    g_w = gather_wide(s_w)
    *out_pieces, wide_grad, t_w = launch(
        wide_out,
        "wide_out",
        (half,),
        [
            (slow_count, smem),
            (own_side, smem),
            (spot, smem),
            (pairs(act_m), pair_spec(b_s)),
            (pairs(project), pair_spec(c_s)),
            (g_w, whole(g_w)),
            (slow_expand_norm, whole(slow_expand_norm)),
            (slow_project_norm, whole(slow_project_norm)),
            (slow_expand, whole(slow_expand)),
            *[(piece, piece_spec) for piece in by_step(cot_pieces)],
        ],
        [
            *[(piece_shape, BF, piece_spec)] * wa_count,
            ((2, half, cells, c_s), F32, pair_spec(c_s)),
            ((4, c_s), F32, pl.BlockSpec((4, c_s), lambda *_: (0, 0))),
        ],
        [pltpu.VMEM((wa_count, cells, LANES), BF)],
    )
    wide_grad = wide_grad.reshape(frames, cells, c_s)
    h_w = gather_wide(t_w)
    result_pieces = send_turns(out_pieces, 0, GATE_RESULT)

    middle_grad, expand_w_grad, t_m = launch(
        middle_back,
        "middle_back",
        (frames // 2,),
        [
            (slow_count, smem),
            (own_side, smem),
            (wide_grad, frame_spec(c_s, 2)),
            (act_m, frame_spec(b_s, 2)),
            (g_w, whole(g_w)),
            (h_w, whole(h_w)),
            (slow_expand_norm, whole(slow_expand_norm)),
            (slow_expand, whole(slow_expand)),
            (pre_m, frame_spec(b_s, 2)),
            (g_m, whole(g_m)),
            (slow_spatial_norm, whole(slow_spatial_norm)),
        ],
        [
            ((frames, cells, b_s), F32, frame_spec(b_s, 2)),
            ((c_s, b_s), BF, pl.BlockSpec((c_s, b_s), lambda *_: (0, 0))),
            stat(2, b_s),
        ],
        [pltpu.VMEM((2, b_s), F32), pltpu.VMEM((b_s, c_s), F32)],
        after=turn(result_pieces, 0, CUT_RESULT[0]),
    )
    h_m = gather_stats(t_m)
    result_pieces.update(send_late(out_pieces, GATE_RESULT, h_m))
    slow_result = unpack(by_step(result_pieces))
    joined_part, project_w_grad = launch(
        project_back,
        "project_back",
        (frames // 2,),
        [
            (slow_count, smem),
            (own_side, smem),
            (wide_grad, frame_spec(c_s, 2)),
            (project, frame_spec(c_s, 2)),
            (g_w, whole(g_w)),
            (h_w, whole(h_w)),
            (slow_project_norm, whole(slow_project_norm)),
            (own, frame_spec(c_s, 2)),
            (lateral_act, frame_spec(c_l, 2)),
            (slow_project, whole(slow_project)),
        ],
        [
            ((frames, cells, c_cat), BF, frame_spec(c_cat, 2)),
            ((c_cat * c_s // b_s, b_s), BF, pl.BlockSpec((c_cat * c_s // b_s, b_s), lambda *_: (0, 0))),
        ],
        [pltpu.VMEM((c_cat, c_s), F32)],
        flops=4 * frames * cells * c_cat * c_s,
    )
    middle_low, narrow_grad, t_n = launch(
        narrow_back,
        "narrow_back",
        (frames // 4,),
        [
            (slow_count, smem),
            (own_side, smem),
            (middle_grad, frame_spec(b_s, 4)),
            (pre_m, frame_spec(b_s, 4)),
            (g_m, whole(g_m)),
            (h_m, whole(h_m)),
            (slow_spatial_norm, whole(slow_spatial_norm)),
            (w_middle_back, whole(w_middle_back)),
            (pre_n, frame_spec(b_s, 4)),
            (g_n, whole(g_n)),
            (slow_reduce_norm, whole(slow_reduce_norm)),
        ],
        [
            ((frames, cells, b_s), BF, frame_spec(b_s, 4)),
            ((frames, cells, b_s), F32, frame_spec(b_s, 4)),
            stat(2, b_s),
        ],
        [pltpu.VMEM((2, b_s), F32), slow_win],
        after=turn(result_pieces, CUT_RESULT[0], CUT_RESULT[1]),
    )
    h_n = gather_stats(t_n)
    (spatial_w_grad,) = launch(
        plane_weight,
        "plane_weight",
        (frames // 4,),
        [(act_n, frame_spec(b_s, 4)), (middle_low, frame_spec(b_s, 4))],
        [((3, 3 * b_s, b_s), BF, pl.BlockSpec((3, 3 * b_s, b_s), lambda *_: (0, 0, 0)))],
        [pltpu.VMEM((3, 3 * b_s, b_s), F32), slow_win, slow_low],
        flops=18 * frames * cells * b_s * b_s,
    )
    narrow_low, grad_packed, lateral_grad, t_l = launch(
        join_back,
        "join_back",
        (half,),
        [
            (slow_count, smem),
            (own_side, smem),
            (narrow_grad, whole(narrow_grad)),
            (pre_n, whole(pre_n)),
            (g_n, whole(g_n)),
            (h_n, whole(h_n)),
            (slow_reduce_norm, whole(slow_reduce_norm)),
            (slow_reduce, whole(slow_reduce)),
            (pairs(joined_part), pair_spec(c_cat)),
            (pairs(pre_l), pair_spec(c_l)),
            (g_l, whole(g_l)),
            (lateral_norm, whole(lateral_norm)),
        ],
        [
            (
                (frames + 2, cells, b_s),
                BF,
                pl.BlockSpec((frames + 2, cells, b_s), lambda *_: (0, 0, 0)),
            ),
            (
                (wa_count,) + piece_shape,
                BF,
                pl.BlockSpec((wa_count, cells, piece_shape[1]), lambda i: (0, i, 0)),
            ),
            ((2, half, cells, c_l), F32, pair_spec(c_l)),
            stat(2, c_l),
        ],
        [pltpu.VMEM((2, c_l), F32)],
        after=turn(result_pieces, CUT_RESULT[1], CUT_RESULT[2]),
    )
    lateral_grad = lateral_grad.reshape(frames, cells, c_l)
    h_l = gather_stats(t_l)
    grad_got = exchange(grad_packed)
    slow_grad = unpack([grad_got])

    def time_weight(values):
        flat = values.reshape(frames * cells, values.shape[2])
        low = narrow_low.reshape((frames + 2) * cells, b_s)
        parts = []
        for tap in range(3):
            begin = (2 - tap) * cells
            parts.append(
                lax.dot_general(
                    flat,
                    lax.slice_in_dim(low, begin, begin + frames * cells, 1, 0),
                    (((0,), (0,)), ((), ())),
                    preferred_element_type=F32,
                )
            )
        return jnp.stack(parts).astype(BF)

    lateral_low, frames_back = launch(
        lateral_back,
        "lateral_back",
        (),
        [
            (slow_count, smem),
            (own_side, smem),
            (lateral_grad, whole(lateral_grad)),
            (pre_l, whole(pre_l)),
            (g_l, whole(g_l)),
            (h_l, whole(h_l)),
            (lateral_norm, whole(lateral_norm)),
            (lateral_weight, whole(lateral_weight)),
        ],
        [
            ((frames, cells, c_l), BF, pl.BlockSpec((frames, cells, c_l), lambda *_: (0, 0, 0))),
            ((4 * frames, cells, c_f), BF, pl.BlockSpec((4 * frames, cells, c_f), lambda *_: (0, 0, 0))),
        ],
        after=turn(result_pieces, CUT_RESULT[2], 15),
    )
    back_got = exchange(frames_back.reshape(wa_count, 2 * cells, c_f)).reshape(x.shape)
    (lateral_w_grad,) = launch(
        lateral_weight_back,
        "lateral_weight_back",
        (),
        [(fast_got, whole(fast_got)), (lateral_low, whole(lateral_low))],
        [((5 * c_f, c_l), BF, pl.BlockSpec((5 * c_f, c_l), lambda *_: (0, 0)))],
        [pltpu.VMEM((5 * c_f, c_l), F32)],
    )

    weight_parts = [
        part.reshape(-1, b_s)
        for part in (
            project_w_grad,
            expand_w_grad,
            spatial_w_grad,
            time_weight(own),
            time_weight(lateral_act),
        )
    ]
    sizes = [part.shape[0] for part in weight_parts]
    near = 4
    inner = [[near * k + j for j in range(near)] for k in range(wa_count // near)]
    outer = [[near * k + j for k in range(wa_count // near)] for j in range(near)]
    dp_count = lax.axis_size("dp")
    core = lax.axis_index("dp")
    swap = [(0, 1), (1, 0)]
    paired = dp_count == 2
    if paired:
        others = [lax.ppermute(part, "dp", swap) for part in weight_parts]
        rows = sum(sizes) // 2
        place_core = core.reshape(1)
        (weights,) = launch(
            weight_merge,
            "weight_merge",
            (),
            [(place_core, smem)] + [(part, whole(part)) for part in weight_parts + others],
            [((rows, b_s), BF, pl.BlockSpec((rows, b_s), lambda *_: (0, 0)))],
        )
    else:
        weights = jnp.concatenate(weight_parts, axis=0)
    first_stage = lax.psum_scatter(weights, "wa", axis_index_groups=inner, tiled=True)
    spot_in = place % near
    if paired:
        other = lax.ppermute(lateral_w_grad, "dp", swap)
        share = lateral_w_grad.shape[0] // (2 * near)
        out = ((share, c_l), BF, pl.BlockSpec((share, c_l), lambda *_: (0, 0)))
        lateral_out = launch(
            lateral_merge,
            "lateral_merge",
            (),
            [(jnp.stack([core, spot_in]), smem)]
            + [(part, whole(part)) for part in (lateral_w_grad, other)],
            [out] * near,
        )
    else:
        share = lateral_w_grad.shape[0] // near
        lateral_out = [
            lax.dynamic_slice_in_dim(lateral_w_grad, (spot_in ^ step) * share, share)
            for step in range(near)
        ]
    lateral_sum = lateral_out[0].astype(F32)
    for step in range(1, near):
        got = lax.ppermute(lateral_out[step], "wa", [(i, i ^ step) for i in range(wa_count)])
        lateral_sum = lateral_sum + got.astype(F32)
    second_stage = lax.psum(
        jnp.concatenate([first_stage, lateral_sum.astype(BF)], axis=0),
        "wa",
        axis_index_groups=outer,
    )

    cot = fast_cot.reshape(x.shape)
    fast_grad3, t3 = launch(
        fast_back_sum,
        "fast_back_sum",
        (packs,),
        [
            (fast_count, smem),
            (clip_side, smem),
            (cot, x_spec),
            (back_got, x_spec),
            (x, x_spec),
            (act2, packed_spec),
            (g3, whole(g3)),
            (fast_expand_norm, whole(fast_expand_norm)),
            (w_widen, whole(w_widen)),
        ],
        [(x.shape, F32, x_spec), stat8],
        [acc8],
    )
    h3 = gather_stats(t3)
    fast_grad2, widen_blocks, t2 = launch(
        fast_back_widen,
        "fast_back_widen",
        (packs,),
        [
            (fast_count, smem),
            (clip_side, smem),
            (fast_grad3, x_spec),
            (act2, packed_spec),
            (g3, whole(g3)),
            (h3, whole(h3)),
            (fast_expand_norm, whole(fast_expand_norm)),
            (w_widen, whole(w_widen)),
            (pre2, packed_spec),
            (g2, whole(g2)),
            (params2, whole(params2)),
            (lane_sides, sides_spec),
        ],
        [
            (packed_shape, F32, packed_spec),
            ((GROUPS, LANES, c_f), F32, pl.BlockSpec((GROUPS, LANES, c_f), lambda *_: (0, 0, 0))),
            stat8,
        ],
        [acc8],
        after=(second_stage,),
    )
    h2 = gather_stats(t2)
    pieces = [second_stage] + [
        lax.ppermute(second_stage, "wa", [(i, i ^ step) for i in range(wa_count)])
        for step in range(1, near)
    ]
    fast_grad1, plane_blocks, t1 = launch(
        fast_back_plane,
        "fast_back_plane",
        (packs,),
        [
            (fast_count, smem),
            (fast_grad2, packed_spec),
            (pre2, packed_spec),
            (g2, whole(g2)),
            (h2, whole(h2)),
            (params2, whole(params2)),
            (act1, packed_spec),
            (pre1, packed_spec),
            (g1, whole(g1)),
            (params1, whole(params1)),
            (lane_sides, sides_spec),
            (w_plane_back, whole(w_plane_back)),
        ],
        [
            (packed_shape, F32, packed_spec),
            (
                (3, 3 * LANES, LANES),
                F32,
                pl.BlockSpec((3, 3 * LANES, LANES), lambda *_: (0, 0, 0)),
            ),
            stat8,
        ],
        [acc8, fast_win, fast_low],
        after=tuple(pieces),
    )
    h1 = gather_stats(t1)
    if paired:
        pieces = pieces + [lax.ppermute(piece, "dp", swap) for piece in pieces]
    else:
        pieces = [lax.psum(piece, "dp") for piece in pieces]
    final = [
        ((c_cat, c_s), F32),
        ((b_s, c_s), F32),
        ((9 * b_s, b_s), F32),
        ((3, c_cat, b_s), F32),
        ((5 * c_f, c_l), F32),
    ]
    project_all, expand_all, spatial_all, time_all, lateral_all = launch(
        weight_split,
        "weight_split",
        (),
        [(jnp.stack([core, place % near]), smem)] + [(piece, whole(piece)) for piece in pieces],
        [
            (shape, dtype, pl.BlockSpec(shape, lambda *_, rank=len(shape): (0,) * rank))
            for shape, dtype in final
        ],
        [pltpu.VMEM((sum(sizes), b_s), BF)],
    )
    (low1,) = launch(
        fast_back_first,
        "fast_back_first",
        (packs,),
        [
            (fast_count, smem),
            (fast_grad1, packed_spec),
            (pre1, packed_spec),
            (g1, whole(g1)),
            (h1, whole(h1)),
            (params1, whole(params1)),
            (lane_sides, sides_spec),
        ],
        [((2, packs, cells, LANES), BF, pl.BlockSpec((2, 1, cells, LANES), lambda i: (0, i, 0, 0)))],
    )
    low_prev = lax.ppermute(low1[1], "wa", forward)
    low_next = lax.ppermute(low1[0], "wa", backward)
    fast_grad, first_blocks = launch(
        fast_back_out,
        "fast_back_out",
        (packs,),
        [
            (fast_grad3, x_spec),
            (low1, pl.BlockSpec((2, 1, cells, LANES), lambda i: (0, i, 0, 0))),
            (low_prev, rim_spec),
            (low_next, rim_spec),
            (x, x_spec),
            (w_first_back, whole(w_first_back)),
        ],
        [
            (x.shape, BF, x_spec),
            (
                (GROUPS, c_f, 3 * LANES),
                F32,
                pl.BlockSpec((GROUPS, c_f, 3 * LANES), lambda *_: (0, 0, 0)),
            ),
        ],
        after=(grad_got,),
    )
    expand_part = sum(widen_blocks[g, g * b_f : (g + 1) * b_f] for g in range(GROUPS))
    plane_view = plane_blocks.reshape(3, 3, GROUPS, b_f, GROUPS, b_f)
    spatial_part = sum(plane_view[:, :, g, :, g] for g in range(GROUPS))
    first_view = first_blocks.reshape(GROUPS, c_f, 3, GROUPS, b_f)
    reduce_part = sum(first_view[g, :, :, g] for g in range(GROUPS)).transpose(1, 0, 2)

    small = jnp.concatenate(
        [reduce_part.reshape(-1), spatial_part.reshape(-1), expand_part.reshape(-1)]
    )
    share = -(-small.shape[0] // (devices * LANES)) * LANES
    padded = jnp.pad(small, (0, share * devices - small.shape[0])).reshape(devices, share // LANES, LANES)
    mine = jnp.sum(gather_stats(padded), axis=0)
    copies = jnp.broadcast_to(mine[None], padded.shape)
    (small_all,) = gate([gather_stats(copies)], slow_grad)
    small_all = small_all.reshape(-1)
    first_size, plane_size = reduce_part.size, spatial_part.size
    fast_reduce_grad = small_all[:first_size].reshape(fast_reduce.shape)
    fast_spatial_grad = small_all[first_size : first_size + plane_size].reshape(fast_spatial.shape)
    fast_expand_grad = small_all[first_size + plane_size : small.shape[0]].reshape(fast_expand.shape)

    def norm_grad(sums, moments, count, folded=False):
        total, moment = jnp.sum(sums, axis=0), jnp.sum(moments, axis=0)
        if folded:
            total = total.reshape(total.shape[0], GROUPS, -1).sum(axis=1)
            moment = moment.reshape(moment.shape[0], GROUPS, -1).sum(axis=1)
        mean = moment[0] / count[0, 0]
        inv = lax.rsqrt(moment[1] / count[0, 0] - mean * mean + EPSILON)
        return jnp.stack([(total[1] - mean * total[0]) * inv, total[0]])

    h_project = jnp.concatenate([h_w[:, 0:1], h_w[:, 2:3]], axis=1)
    return (
        slow_result,
        fast_result.reshape(fast_in.shape),
        slow_grad,
        fast_grad.reshape(fast_in.shape),
        fast_reduce_grad,
        fast_spatial_grad,
        fast_expand_grad,
        lateral_all.reshape(lateral_weight.shape),
        time_all,
        spatial_all.reshape(slow_spatial.shape),
        expand_all,
        project_all,
        norm_grad(h1, g1, fast_count, True),
        norm_grad(h2, g2, fast_count, True),
        norm_grad(h3, g3, fast_count),
        norm_grad(h_l, g_l, slow_count),
        norm_grad(h_n, g_n, slow_count),
        norm_grad(h_m, g_m, slow_count),
        norm_grad(h_w[:, 0:2], g_w[:, 0:2], slow_count),
        norm_grad(h_project, g_w[:, 2:4], slow_count),
    )


def solution(mesh):
    wide = P("dp", None, None, None, "wa")
    fast = P("dp", "wa", None, None, None)
    same = P()
    return jax.shard_map(
        per_device,
        mesh=mesh,
        in_specs=(wide, fast, P("dp")) + (same,) * 16 + (wide, fast),
        out_specs=(wide, fast, wide, fast) + (same,) * 16,
        check_vma=False,
    )
```
